32 devices in a mesh: grid: 8 (over z, x), rep: 4 (over y, core).
Axes of the slice: x: 2, y: 2, z: 4, core: 2. Of those that a mesh axis runs over, the one named last changes fastest.
Arguments:
- functions: bfloat16 [2048, 32768], P(('grid', 'rep')), may hold values from -6 to 6
- filter_taps: bfloat16 [16], replicated, may hold values from -0.59765625 to 0.59765625
- potential: float32 [32768], replicated, may hold values from 0 to 1
- energies: float32 [2048], P(('grid', 'rep')), may hold values from -1.5 to -0.5
- region_start: int32 [2048], P(('grid', 'rep')), may hold values from 0 to 128
- region_length: int32 [2048], P(('grid', 'rep')), may hold values from 256 to 384
- partner_groups: int32 [32, 3], replicated, may hold values from 0 to 31, as said below
Outputs:
- corrected: bfloat16 [2048, 32768], P(('grid', 'rep'))
The draws below stay inside these ranges and needn't reach their ends.
Inputs may be any that keep to these rules, and one draw needn't show every extreme that they name: `partner_groups`: the 3 entries of a row are distinct and differ from the row's own group; each is the row's group plus an offset of magnitude 1 to 15, modulo 32.
All inputs are finite; a program needn't handle non-finite values.
Results may differ from the reference program's by a relative error of at most 0.005.
Values may be sent and summed in bfloat16 or wider, within the bound.
No kernel may reach another device: no remote copies, remote signals or barrier semaphores. Data moves between devices by JAX's collectives and lax.ppermute only.
A program may use at most 128 MiB of HBM per device.

```python
import jax
import jax.numpy as jnp
from jax import lax

SIDE = 32
NC = 32768
BLOCK = 64
NB = 512
GROUP = 64
TAPS = 16
PARTNERS = 3
LMIN = 256
LMAX = 384
NF = 2048
NG = 32


def draw_partner_groups(key, part):
    half = (NG - 1) // 2
    upward = jnp.arange(1, half + 1, dtype=jnp.int32)
    offsets = jnp.concatenate([upward, -upward])
    subkeys = jax.random.split(key, NG)
    shuffled = jax.vmap(lambda subkey: jax.random.permutation(subkey, offsets))(subkeys)[:, :PARTNERS]
    without_minus = jnp.concatenate([upward, -upward[1:]])
    without_plus = jnp.concatenate([upward[1:], -upward])
    first_key = jax.random.fold_in(key, 7001)
    last_key = jax.random.fold_in(key, 7002)
    first_row = jnp.concatenate([jnp.array([-1], jnp.int32), jax.random.permutation(first_key, without_minus)[:PARTNERS - 1]])
    last_row = jnp.concatenate([jnp.array([1], jnp.int32), jax.random.permutation(last_key, without_plus)[:PARTNERS - 1]])
    shuffled = shuffled.at[0].set(first_row).at[NG - 1].set(last_row)
    return ((jnp.arange(NG, dtype=jnp.int32)[:, None] + shuffled) % NG).astype(jnp.int32)


def set_ends(entries, rng, low, high):
    longest = entries.shape.index(max(entries.shape))
    spots = []
    for shift in (0, 1):
        where = [jax.random.randint(jax.random.fold_in(rng, axis), (), 0, length) for axis, length in enumerate(entries.shape)]
        where[longest] = (where[longest] + shift) % entries.shape[longest]
        spots.append(tuple(where))
    return entries.at[spots[0]].set(low).at[spots[1]].set(high)


def steps_of(key, extent, cuts, least, high):
    def one(position, blocks):
        steps = jax.random.uniform(jax.random.fold_in(jax.random.fold_in(key, 6), position), (blocks,), jnp.float32, least / len(cuts), high / len(cuts))
        return jnp.repeat(jnp.exp(steps), extent[position] // blocks).reshape((-1,) + (1,) * (len(extent) - position - 1))

    loudness = one(*cuts[0])
    for cut in cuts[1:]:
        loudness = loudness * one(*cut)
    return loudness


def noise(rng, extent, deviation, reach, pieces=(), kind=jnp.bfloat16):
    entries = deviation * jax.random.normal(rng, extent, jnp.float32)
    if pieces:
        entries = entries * steps_of(rng, extent, pieces, -0.22, 0.18)
    return jnp.clip(entries, -reach, reach).astype(kind)


def setup_inputs(seed: int = 0) -> dict:
    key_list = jax.random.split(jax.random.key(seed), 8)
    functions = noise(key_list[0], (NF, NC), 1.0, 6.0, ((0, 32),))
    filter_taps = noise(key_list[1], (TAPS,), 0.1, 0.59765625)
    potential = jnp.clip(jax.random.uniform(key_list[2], (NC,), jnp.float32, 0.0, 1.0), 0.0, 1.0)
    energies = jnp.clip(-1.5 + 1.0 * jax.random.uniform(key_list[3], (NF,), jnp.float32) ** steps_of(key_list[3], (NF,), ((0, 32),), -0.2, 0.2), -1.5, -0.5)
    region_start = set_ends(jax.random.randint(key_list[4], (NF,), 0, NB - LMAX + 1), jax.random.fold_in(key_list[4], 1), 0, NB - LMAX).astype(jnp.int32)
    region_length = set_ends(jax.random.randint(key_list[5], (NF,), LMIN, LMAX + 1), jax.random.fold_in(key_list[5], 1), LMIN, LMAX).astype(jnp.int32)
    partner_groups = draw_partner_groups(jax.random.fold_in(key_list[7], 71), 0)
    return {"functions": functions, "filter_taps": filter_taps, "potential": potential, "energies": energies, "region_start": region_start, "region_length": region_length, "partner_groups": partner_groups}


def filter_along(values, taps, along_axis):
    centre = TAPS // 2
    widths = [(0, 0)] * values.ndim
    widths[along_axis] = (centre, TAPS - centre)
    padded = jnp.pad(values, widths)
    running = jnp.zeros(values.shape, jnp.float32)
    for offset in range(TAPS):
        running = running + taps[offset] * lax.slice_in_dim(padded, offset, offset + SIDE, axis=along_axis)
    return running


def reference(functions, filter_taps, potential, energies, region_start, region_length, partner_groups):
    taps = filter_taps.astype(jnp.float32)
    block_index = (jnp.arange(NC) // BLOCK).astype(jnp.int32)

    def refine(packed):
        rows, energy, first, count = packed
        values = rows.astype(jnp.float32)
        cube = values.reshape(GROUP, SIDE, SIDE, SIDE)
        kinetic = filter_along(cube, taps, 1) + filter_along(cube, taps, 2) + filter_along(cube, taps, 3)
        kinetic = kinetic.reshape(GROUP, NC)
        gradient = kinetic + potential[None, :] * values - energy[:, None] * values
        updated = values - 0.3 * gradient / (1.0 - energy)[:, None]
        inside = (block_index[None, :] >= first[:, None]) & (block_index[None, :] < (first + count)[:, None])
        return jnp.where(inside, updated, 0.0).astype(jnp.bfloat16)

    refined = lax.map(refine, (functions.reshape(NG, GROUP, NC), energies.reshape(NG, GROUP),
                               region_start.reshape(NG, GROUP), region_length.reshape(NG, GROUP)))
    identity_block = jnp.concatenate([jnp.eye(GROUP, dtype=jnp.float32)[None],
                                      jnp.zeros((PARTNERS, GROUP, GROUP), jnp.float32)], axis=0)
    weight = 1.0 / (BLOCK * LMAX)

    def correct(group):
        members = jnp.concatenate([group[None].astype(jnp.int32), partner_groups[group].astype(jnp.int32)])
        own_rows = refined[group].astype(jnp.float32)
        blocks = refined[members].astype(jnp.float32)
        intersection = jnp.einsum('gc,khc->kgh', own_rows, blocks, precision=lax.Precision.HIGHEST) * weight
        coupling = (0.5 * (intersection - identity_block)).astype(jnp.bfloat16)
        shifted = jnp.einsum('kgh,khc->gc', coupling.astype(jnp.float32), blocks, precision=lax.Precision.HIGHEST)
        return (own_rows - shifted).astype(jnp.bfloat16)

    corrected = lax.map(correct, jnp.arange(NG, dtype=jnp.int32))
    return corrected.reshape(NF, NC)
```

```python
import functools

import jax
import jax.numpy as jnp
from jax import lax
from jax.experimental import pallas as pl
from jax.experimental.pallas import tpu as pltpu
from jax.sharding import PartitionSpec as P

SIDE = 32
PLANE = SIDE * SIDE
NC = SIDE * PLANE
BLOCK = 64
NB = NC // BLOCK
GROUP = 64
TAPS = 16
MEMBERS = 4
LMAX = 384
FOLD = (NB - LMAX) * BLOCK
MID = NC - 2 * FOLD
SLOTS = 32
ROWS = 16
TILE = 256
EDGE = FOLD // SLOTS // 2
INNER = MID // SLOTS // 2
EDGE_SLOTS = PLANE // 2 // EDGE
INNER_SLOTS = PLANE // 2 // INNER
STEP = 4
AXES = ("grid", "rep")
MIB = 1024 * 1024
VMEM = 24 * MIB


def to_column(row, size):
    eye = lax.broadcasted_iota(jnp.int32, (size, size), 0) == lax.broadcasted_iota(
        jnp.int32, (size, size), 1
    )
    return jnp.sum(jnp.where(eye, jnp.broadcast_to(row, (size, size)), 0), axis=1, keepdims=True)


def tap_rows(taps, outer, shift, inner_first):
    size = outer if inner_first else TILE // outer
    row = lax.broadcasted_iota(jnp.int32, (size, TILE), 0)
    col = lax.broadcasted_iota(jnp.int32, (size, TILE), 1)
    col = col // (TILE // outer) if inner_first else col % (TILE // outer)
    distance = shift + row - col + TAPS // 2
    total = jnp.zeros(distance.shape, jnp.float32)
    for t in range(TAPS):
        total = jnp.where(distance == t, taps[t], total)
    return total


def spread_outer(rows, outer):
    inner = TILE // outer
    row = lax.broadcasted_iota(jnp.int32, (inner, TILE), 0)
    same = row == lax.broadcasted_iota(jnp.int32, (inner, TILE), 1) % inner
    return jnp.concatenate(
        [jnp.where(same, jnp.broadcast_to(rows[a : a + 1], (inner, TILE)), 0.0) for a in range(outer)], axis=0
    )


def spread_inner(rows, outer):
    inner = TILE // outer
    block = lax.broadcasted_iota(jnp.int32, (inner, TILE), 1) // inner
    return jnp.concatenate([jnp.where(block == a, rows, 0.0) for a in range(outer)], axis=0)


def refine_kernel(
    half, taps_ref, functions_ref, potential_ref, energies_ref, start_ref, length_ref, out_ref,
    plane_ref, line_ref, slabs_ref, rows_ref, ends_ref,
):
    count = energies_ref.shape[1]

    @pl.when(pl.program_id(0) == 0)
    def _():
        taps = [taps_ref[0, t] for t in range(TAPS)]
        outer = TILE // SIDE
        lines = []
        for j in range(3):
            part = spread_outer(tap_rows(taps, outer, (j - 1) * outer, True), outer)
            if j == 1:
                part = part + spread_inner(tap_rows(taps, outer, 0, False), outer)
            plane_ref[j * TILE : (j + 1) * TILE, :] = part.astype(jnp.bfloat16)
            flipped = [taps[TAPS - 1 - t] for t in range(TAPS)]
            rows = tap_rows(flipped, TILE // ROWS, (1 - j) * (TILE // ROWS) - 1, True)
            lines.append(spread_outer(rows, TILE // ROWS).astype(jnp.bfloat16))
        for h in range(SIDE * ROWS // TILE):
            for i in range(SIDE * ROWS // TILE):
                line_ref[h * TILE : (h + 1) * TILE, i * TILE : (i + 1) * TILE] = lines[i - h + 1]
        wide = (count, 2 * BLOCK)
        energy = to_column(energies_ref[...], count)
        first = to_column(start_ref[...], count)
        rows_ref[0] = jnp.broadcast_to(energy, wide)
        rows_ref[1] = jnp.broadcast_to(0.3 / (1.0 - energy), wide)
        ends_ref[0] = jnp.broadcast_to(first, wide)
        ends_ref[1] = jnp.broadcast_to(first + to_column(length_ref[...], count), wide)

    for x in range(SIDE):
        slabs_ref[x * ROWS : (x + 1) * ROWS, :] = functions_ref[:, x * PLANE : (x + 1) * PLANE]
    here = pl.ds(pl.multiple_of(pl.program_id(0) * ROWS, ROWS), ROWS)

    def widen(value):
        return jnp.concatenate([value] * (TILE // (2 * BLOCK)), axis=1)

    energy, scale = widen(rows_ref[0, here, :]), widen(rows_ref[1, here, :])
    lane_block = lax.broadcasted_iota(jnp.int32, (ROWS, TILE), 1) // BLOCK
    first = widen(ends_ref[0, here, :]) - lane_block
    last = widen(ends_ref[1, here, :]) - lane_block
    blocks = PLANE // TILE
    for j in range(half * blocks // 2, (half + 1) * blocks // 2):
        cols = slice(j * TILE, (j + 1) * TILE)
        low, high = max(0, j - 1), min(blocks, j + 2)
        total = jnp.dot(
            slabs_ref[:, low * TILE : high * TILE],
            plane_ref[(low - j + 1) * TILE : (high - j + 1) * TILE, :],
            preferred_element_type=jnp.float32,
        ) + jnp.dot(line_ref[...], slabs_ref[:, cols], preferred_element_type=jnp.float32)

        def refined(x):
            rows = slice(x * ROWS, (x + 1) * ROWS)
            value = slabs_ref[rows, cols].astype(jnp.float32)
            place = potential_ref[0:1, x * PLANE + j * TILE : x * PLANE + (j + 1) * TILE]
            gradient = total[rows] + (place - energy) * value
            block = (x * PLANE + j * TILE) // BLOCK
            inside = (first <= block) & (last > block)
            return inside, value - scale * gradient

        for x in range(SIDE):
            column = x * PLANE + j * TILE
            if column < FOLD:
                inside, value = refined(x)
                inside_far, value_far = refined(x + (NC - FOLD) // PLANE)
                value = jnp.where(inside, value, jnp.where(inside_far, value_far, 0.0))
                value = value.astype(jnp.bfloat16)
                for i in range(TILE // EDGE):
                    slot = x * EDGE_SLOTS + (j * (TILE // EDGE) + i) % EDGE_SLOTS
                    out_ref[slot, :, :EDGE] = value[:, i * EDGE : (i + 1) * EDGE]
            elif column < NC - FOLD:
                inside, value = refined(x)
                value = jnp.where(inside, value, 0.0)
                slot = (x - FOLD // PLANE) * INNER_SLOTS + j % INNER_SLOTS
                out_ref[slot, :, EDGE:] = value.astype(jnp.bfloat16)


def refine(half, taps, functions, potential, energies, start, length):
    count = functions.shape[0]
    steps = count // ROWS
    row = pl.BlockSpec((1, count), lambda i: (0, 0))
    return pl.pallas_call(
        functools.partial(refine_kernel, half),
        grid=(steps,),
        in_specs=[
            pl.BlockSpec(memory_space=pltpu.SMEM),
            pl.BlockSpec((ROWS, NC), lambda i: (i, 0)),
            pl.BlockSpec((1, NC), lambda i: (0, 0)),
            row,
            row,
            row,
        ],
        out_specs=pl.BlockSpec((SLOTS, ROWS, EDGE + INNER), lambda i: (0, i, 0)),
        out_shape=jax.ShapeDtypeStruct((SLOTS, count, EDGE + INNER), jnp.bfloat16),
        scratch_shapes=[
            pltpu.VMEM((3 * TILE, TILE), jnp.bfloat16),
            pltpu.VMEM((SIDE * ROWS, SIDE * ROWS), jnp.bfloat16),
            pltpu.VMEM((SIDE * ROWS, PLANE), jnp.bfloat16),
            pltpu.VMEM((2, count, 2 * BLOCK), jnp.float32),
            pltpu.VMEM((2, count, 2 * BLOCK), jnp.int32),
        ],
        compiler_params=pltpu.CompilerParams(vmem_limit_bytes=VMEM),
        cost_estimate=pl.CostEstimate(
            flops=steps * 18 * 2 * TILE**3, bytes_accessed=count * NC * 3, transcendentals=0
        ),
        name="refine",
    )(
        taps.astype(jnp.float32).reshape(1, TAPS),
        functions,
        potential.reshape(1, NC),
        energies.reshape(1, count),
        start.reshape(1, count),
        length.reshape(1, count),
    )


class Order:
    def __init__(self):
        self.grid, self.rep = lax.axis_size("grid"), lax.axis_size("rep")
        self.devices = self.grid * self.rep
        self.far, self.near = self.grid // 2, self.rep

    def place(self, device):
        grid, rep = device // self.rep, device % self.rep
        return ((rep % 2 * (self.rep // 2) + rep // 2) * 2 + grid % 2) * self.far + grid // 2

    def device(self, place):
        high, low = place // self.far, place % self.far
        rep = high // 2 % (self.rep // 2) * 2 + high // 2 // (self.rep // 2)
        return (low * 2 + high % 2) * self.rep + rep

    def send(self, block, apart):
        pairs = [(i, self.device(self.place(i) ^ apart)) for i in range(self.devices)]
        return lax.ppermute(block, AXES, pairs)


def gram_kernel(order, edge, final, partners_ref, info_ref, start_ref, folded_ref, *refs):
    if final:
        before_ref, whole_ref, keep_ref, send_ref = refs
    else:
        whole_ref, total_ref = refs
    groups = folded_ref.shape[0]
    lane_block = (info_ref[1] + lax.broadcasted_iota(jnp.int32, (GROUP, edge), 1)) // BLOCK

    def unfold(g, carry):
        near = jnp.broadcast_to(to_column(start_ref[g], GROUP), (GROUP, edge)) <= lane_block
        both = folded_ref[g, :, :edge].astype(jnp.float32)
        whole_ref[g, :, :edge] = jnp.where(near, both, 0.0).astype(jnp.bfloat16)
        whole_ref[g, :, edge : 2 * edge] = jnp.where(near, 0.0, both).astype(jnp.bfloat16)
        whole_ref[g, :, 2 * edge :] = folded_ref[g, :, edge:]
        return carry

    lax.fori_loop(0, groups, unfold, 0, unroll=4)

    def product(i):
        g = order.device(i ^ info_ref[0])
        own = whole_ref[g]
        members = jnp.concatenate(
            [own] + [whole_ref[partners_ref[g, k]] for k in range(MEMBERS - 1)], axis=0
        )
        return lax.dot_general(
            own, members, (((1,), (1,)), ((), ())), preferred_element_type=jnp.float32
        )

    def start(i, carry):
        total_ref[i] = product(i)
        return carry

    def finish(i, carry):
        keep_ref[i] = (before_ref[i] + product(i)).astype(jnp.bfloat16)
        j = i + groups // 2
        send_ref[i] = (before_ref[j] + product(j)).astype(jnp.bfloat16)
        return carry

    if final:
        lax.fori_loop(0, groups // 2, finish, 0, unroll=2)
    else:
        lax.fori_loop(0, groups, start, 0, unroll=4)


def gram(order, partners, info, start, folded, edge, before=None):
    groups, _, width = folded.shape
    whole = width + edge
    block = (GROUP, MEMBERS * GROUP)
    shapes = [jax.ShapeDtypeStruct((groups, GROUP, whole), jnp.bfloat16)]
    if before is None:
        shapes += [jax.ShapeDtypeStruct((groups, *block), jnp.float32)]
    else:
        shapes += [jax.ShapeDtypeStruct((groups // 2, *block), jnp.bfloat16)] * 2
    arrays = [start, folded] + ([] if before is None else [before])
    return pl.pallas_call(
        functools.partial(gram_kernel, order, edge, before is not None),
        in_specs=[pl.BlockSpec(memory_space=pltpu.SMEM)] * 2
        + [pl.BlockSpec(memory_space=pltpu.VMEM)] * len(arrays),
        out_specs=[pl.BlockSpec(memory_space=pltpu.VMEM)] * len(shapes),
        out_shape=shapes,
        compiler_params=pltpu.CompilerParams(vmem_limit_bytes=VMEM),
        cost_estimate=pl.CostEstimate(
            flops=groups * 2 * GROUP * GROUP * MEMBERS * whole,
            bytes_accessed=groups * GROUP * whole * 4,
            transcendentals=0,
        ),
        name="gram",
    )(partners, info, *arrays)


def add_kernel(count, pieces, *refs):
    outs = refs[count:]
    each = refs[0].shape[0] // pieces
    for o in range(pieces):
        total = refs[0][o * each : (o + 1) * each].astype(jnp.float32)
        for i in range(1, count):
            total = total + refs[i][o * each : (o + 1) * each].astype(jnp.float32)
        outs[o][...] = total.astype(jnp.bfloat16)


def add(arrays, pieces):
    shape = arrays[0].shape
    out = jax.ShapeDtypeStruct((shape[0] // pieces, *shape[1:]), jnp.bfloat16)
    return pl.pallas_call(
        functools.partial(add_kernel, len(arrays), pieces),
        out_shape=[out] * pieces,
        compiler_params=pltpu.CompilerParams(vmem_limit_bytes=VMEM),
        name="add",
    )(*arrays)


def couple_kernel(*refs):
    out_ref = refs[-1]
    total = refs[0][0].astype(jnp.float32)
    for ref in refs[1:-1]:
        total = total + ref[0].astype(jnp.float32)
    row = lax.broadcasted_iota(jnp.int32, total.shape, 0)
    col = lax.broadcasted_iota(jnp.int32, total.shape, 1)
    unit = jnp.where(row == col, 1.0, 0.0)
    out_ref[0] = (0.5 * (total * (1.0 / (BLOCK * LMAX)) - unit)).astype(jnp.bfloat16)


def couple(parts):
    return pl.pallas_call(
        couple_kernel,
        out_shape=jax.ShapeDtypeStruct(parts[0].shape, jnp.bfloat16),
        compiler_params=pltpu.CompilerParams(vmem_limit_bytes=VMEM),
        name="couple",
    )(*parts)


def correct_kernel(order, partners_ref, info_ref, held_ref, other_ref, whole_ref, out_ref):
    half = held_ref.shape[0]
    for i in range(STEP):
        g = pl.program_id(0) * STEP + i
        own = whole_ref[g]
        members = jnp.concatenate(
            [own] + [whole_ref[partners_ref[g, k]] for k in range(MEMBERS - 1)], axis=0
        )
        apart = order.place(g) ^ info_ref[0]
        near = jnp.broadcast_to(apart, (GROUP, MEMBERS * GROUP)) < half
        coupling = jnp.where(
            near,
            held_ref[apart % half].astype(jnp.float32),
            other_ref[apart % half].astype(jnp.float32),
        ).astype(jnp.bfloat16)
        shifted = jnp.dot(coupling, members, preferred_element_type=jnp.float32)
        out_ref[i] = (own.astype(jnp.float32) - shifted).astype(jnp.bfloat16)


def correct(order, partners, info, held, other, whole):
    groups, _, width = whole.shape
    return pl.pallas_call(
        functools.partial(correct_kernel, order),
        grid=(groups // STEP,),
        in_specs=[pl.BlockSpec(memory_space=pltpu.SMEM)] * 2
        + [pl.BlockSpec(memory_space=pltpu.VMEM)] * 3,
        out_specs=pl.BlockSpec((STEP, GROUP, width), lambda g: (g, 0, 0)),
        out_shape=jax.ShapeDtypeStruct(whole.shape, jnp.bfloat16),
        compiler_params=pltpu.CompilerParams(vmem_limit_bytes=VMEM),
        cost_estimate=pl.CostEstimate(
            flops=groups * 2 * GROUP * GROUP * MEMBERS * width,
            bytes_accessed=groups * GROUP * width * 4,
            transcendentals=0,
        ),
        name="correct",
    )(partners, info, held, other, whole)


def place_kernel(*refs):
    out_ref = refs[-1]
    for half, in_ref in enumerate(refs[:-1]):
        for s in range(SLOTS):
            edge = s // EDGE_SLOTS * PLANE + half * (PLANE // 2) + s % EDGE_SLOTS * EDGE
            inner = FOLD + s // INNER_SLOTS * PLANE + half * (PLANE // 2) + s % INNER_SLOTS * INNER
            far = edge + NC - FOLD
            out_ref[:, edge : edge + EDGE] = in_ref[s, :, :EDGE]
            out_ref[:, far : far + EDGE] = in_ref[s, :, EDGE : 2 * EDGE]
            out_ref[:, inner : inner + INNER] = in_ref[s, :, 2 * EDGE :]


def place(halves):
    _, count, width = halves[0].shape
    return pl.pallas_call(
        place_kernel,
        grid=(count // ROWS,),
        in_specs=[pl.BlockSpec((SLOTS, ROWS, width), lambda i: (0, i, 0))] * len(halves),
        out_specs=pl.BlockSpec((ROWS, NC), lambda i: (i, 0)),
        out_shape=jax.ShapeDtypeStruct((count, NC), jnp.bfloat16),
        compiler_params=pltpu.CompilerParams(vmem_limit_bytes=16 * MIB),
        cost_estimate=pl.CostEstimate(flops=0, bytes_accessed=count * NC * 4, transcendentals=0),
        name="place",
    )(*halves)


def split_slots(pieces, ratio, bounds):
    if ratio == 1:
        return pieces
    slots, rows, _ = pieces.shape
    parts = []
    for low, high in zip(bounds[:-1], bounds[1:]):
        part = pieces[:, :, low:high].reshape(slots, rows, ratio, (high - low) // ratio)
        parts.append(part.transpose(0, 2, 1, 3).reshape(slots * ratio, rows, -1))
    return jnp.concatenate(parts, axis=2)


def join_slots(pieces, ratio, bounds):
    if ratio == 1:
        return pieces
    count, rows, _ = pieces.shape
    parts = []
    for low, high in zip(bounds[:-1], bounds[1:]):
        part = pieces[:, :, low // ratio : high // ratio]
        part = part.reshape(count // ratio, ratio, rows, (high - low) // ratio)
        parts.append(part.transpose(0, 2, 1, 3).reshape(count // ratio, rows, high - low))
    return jnp.concatenate(parts, axis=2)


def on_device(
    functions, filter_taps, potential, energies, region_start, region_length, partner_groups
):
    order = Order()
    ratio = order.devices // SLOTS
    edge, inner = EDGE // ratio, INNER // ratio
    me = lax.axis_index(AXES)
    slot = me // ratio
    column = slot // EDGE_SLOTS * PLANE + slot % EDGE_SLOTS * EDGE + me % ratio * edge
    infos = [jnp.stack([order.place(me), column + half * (PLANE // 2)]) for half in range(2)]
    infos = [info.astype(jnp.int32) for info in infos]

    starts = jnp.broadcast_to(region_start.reshape(1, 1, GROUP), (order.devices, 1, GROUP))
    starts = lax.all_to_all(starts, AXES, split_axis=0, concat_axis=0, tiled=True)
    folded = []
    for half in range(2):
        pieces = refine(
            half, filter_taps, functions, potential, energies, region_start, region_length
        )
        pieces = split_slots(pieces, ratio, (0, EDGE, EDGE + INNER))
        folded.append(lax.all_to_all(pieces, AXES, split_axis=0, concat_axis=0, tiled=True))

    whole = [None, None]
    whole[0], sums = gram(order, partner_groups, infos[0], starts, folded[0], edge)
    whole[1], keep, send = gram(order, partner_groups, infos[1], starts, folded[1], edge, sums)
    pieces = add([keep, order.send(send, order.devices // 2)], order.near)
    arrived = [order.send(pieces[i], i * order.far) for i in range(1, order.near)]
    pieces = add([pieces[0]] + arrived, order.far)
    arrived = [order.send(pieces[i], i) for i in range(1, order.far)]
    coupling = couple([pieces[0]] + arrived)
    held = jnp.concatenate([coupling] + [order.send(coupling, i) for i in range(1, order.far)], 0)
    held = jnp.concatenate([held] + [order.send(held, i * order.far) for i in range(1, order.near)], 0)
    other = order.send(held, order.devices // 2)

    halves = []
    for half in range(2):
        pieces = correct(order, partner_groups, infos[half], held, other, whole[half])
        pieces = lax.all_to_all(pieces, AXES, split_axis=0, concat_axis=0, tiled=True)
        halves.append(join_slots(pieces, ratio, (0, EDGE, 2 * EDGE, 2 * EDGE + INNER)))
    return place(halves)


def solution(mesh):
    return jax.shard_map(
        on_device,
        mesh=mesh,
        in_specs=(
            P(AXES, None),
            P(),
            P(),
            P(AXES),
            P(AXES),
            P(AXES),
            P(),
        ),
        out_specs=P(AXES, None),
        check_vma=False,
    )
```

```python
import functools

import jax
import jax.numpy as jnp
from jax import lax
from jax.experimental import pallas as pl
from jax.experimental.pallas import tpu as pltpu
from jax.sharding import PartitionSpec as P

SIDE = 32
PLANE = SIDE * SIDE
NC = SIDE * PLANE
BLOCK = 64
NB = NC // BLOCK
GROUP = 64
TAPS = 16
MEMBERS = 4
LMAX = 384
FOLD = (NB - LMAX) * BLOCK
MID = NC - 2 * FOLD
SLOTS = 32
ROWS = 16
TILE = 256
EDGE = FOLD // SLOTS
INNER = MID // SLOTS
EDGE_SLOTS = PLANE // EDGE
INNER_SLOTS = PLANE // INNER
STEP = 4
AXES = ("grid", "rep")
MIB = 1024 * 1024
VMEM = 24 * MIB


def to_column(row, size):
    eye = lax.broadcasted_iota(jnp.int32, (size, size), 0) == lax.broadcasted_iota(
        jnp.int32, (size, size), 1
    )
    return jnp.sum(jnp.where(eye, jnp.broadcast_to(row, (size, size)), 0), axis=1, keepdims=True)


def tap_rows(taps, outer, shift, inner_first):
    size = outer if inner_first else TILE // outer
    row = lax.broadcasted_iota(jnp.int32, (size, TILE), 0)
    col = lax.broadcasted_iota(jnp.int32, (size, TILE), 1)
    col = col // (TILE // outer) if inner_first else col % (TILE // outer)
    distance = shift + row - col + TAPS // 2
    total = jnp.zeros(distance.shape, jnp.float32)
    for t in range(TAPS):
        total = jnp.where(distance == t, taps[t], total)
    return total


def spread_outer(rows, outer):
    inner = TILE // outer
    row = lax.broadcasted_iota(jnp.int32, (inner, TILE), 0)
    same = row == lax.broadcasted_iota(jnp.int32, (inner, TILE), 1) % inner
    return jnp.concatenate(
        [jnp.where(same, jnp.broadcast_to(rows[a : a + 1], (inner, TILE)), 0.0) for a in range(outer)], axis=0
    )


def spread_inner(rows, outer):
    inner = TILE // outer
    block = lax.broadcasted_iota(jnp.int32, (inner, TILE), 1) // inner
    return jnp.concatenate([jnp.where(block == a, rows, 0.0) for a in range(outer)], axis=0)


def refine_kernel(
    taps_ref, functions_ref, potential_ref, energies_ref, start_ref, length_ref, out_ref,
    plane_ref, line_ref, slabs_ref, rows_ref, ends_ref,
):
    count = energies_ref.shape[1]

    @pl.when(pl.program_id(0) == 0)
    def _():
        taps = [taps_ref[0, t] for t in range(TAPS)]
        outer = TILE // SIDE
        lines = []
        for j in range(3):
            part = spread_outer(tap_rows(taps, outer, (j - 1) * outer, True), outer)
            if j == 1:
                part = part + spread_inner(tap_rows(taps, outer, 0, False), outer)
            plane_ref[j * TILE : (j + 1) * TILE, :] = part.astype(jnp.bfloat16)
            flipped = [taps[TAPS - 1 - t] for t in range(TAPS)]
            rows = tap_rows(flipped, TILE // ROWS, (1 - j) * (TILE // ROWS) - 1, True)
            lines.append(spread_outer(rows, TILE // ROWS).astype(jnp.bfloat16))
        for h in range(SIDE * ROWS // TILE):
            for i in range(SIDE * ROWS // TILE):
                line_ref[h * TILE : (h + 1) * TILE, i * TILE : (i + 1) * TILE] = lines[i - h + 1]
        wide = (count, 2 * BLOCK)
        energy = to_column(energies_ref[...], count)
        first = to_column(start_ref[...], count)
        rows_ref[0] = jnp.broadcast_to(energy, wide)
        rows_ref[1] = jnp.broadcast_to(0.3 / (1.0 - energy), wide)
        ends_ref[0] = jnp.broadcast_to(first, wide)
        ends_ref[1] = jnp.broadcast_to(first + to_column(length_ref[...], count), wide)

    for x in range(SIDE):
        slabs_ref[x * ROWS : (x + 1) * ROWS, :] = functions_ref[:, x * PLANE : (x + 1) * PLANE]
    here = pl.ds(pl.multiple_of(pl.program_id(0) * ROWS, ROWS), ROWS)

    def widen(value):
        return jnp.concatenate([value] * (TILE // (2 * BLOCK)), axis=1)

    energy, scale = widen(rows_ref[0, here, :]), widen(rows_ref[1, here, :])
    lane_block = lax.broadcasted_iota(jnp.int32, (ROWS, TILE), 1) // BLOCK
    first = widen(ends_ref[0, here, :]) - lane_block
    last = widen(ends_ref[1, here, :]) - lane_block
    blocks = PLANE // TILE
    near, far = FOLD // PLANE, (NC - FOLD) // PLANE
    for j in range(blocks):
        cols = slice(j * TILE, (j + 1) * TILE)
        low, high = max(0, j - 1), min(blocks, j + 2)
        total = jnp.dot(
            slabs_ref[:, low * TILE : high * TILE],
            plane_ref[(low - j + 1) * TILE : (high - j + 1) * TILE, :],
            preferred_element_type=jnp.float32,
        ) + jnp.dot(line_ref[...], slabs_ref[:, cols], preferred_element_type=jnp.float32)

        def refined(x):
            rows = slice(x * ROWS, (x + 1) * ROWS)
            value = slabs_ref[rows, cols].astype(jnp.float32)
            place = potential_ref[0:1, x * PLANE + j * TILE : x * PLANE + (j + 1) * TILE]
            gradient = total[rows] + (place - energy) * value
            block = (x * PLANE + j * TILE) // BLOCK
            inside = (first <= block) & (last > block)
            return inside, value - scale * gradient

        for x in range(far):
            inside, value = refined(x)
            if x < near:
                inside_far, value_far = refined(x + far)
                value = jnp.where(inside, value, jnp.where(inside_far, value_far, 0.0))
                column = x * PLANE + j * TILE
                slot, place = column // EDGE, column % EDGE
            else:
                value = jnp.where(inside, value, 0.0)
                column = (x - near) * PLANE + j * TILE
                slot, place = column // INNER, EDGE + column % INNER
            out_ref[slot, :, place : place + TILE] = value.astype(jnp.bfloat16)


def refine(taps, functions, potential, energies, start, length):
    count = functions.shape[0]
    steps = count // ROWS
    width = EDGE + INNER
    row = pl.BlockSpec((1, count), lambda i: (0, 0))
    return pl.pallas_call(
        refine_kernel,
        grid=(steps,),
        in_specs=[
            pl.BlockSpec(memory_space=pltpu.SMEM),
            pl.BlockSpec((ROWS, NC), lambda i: (i, 0)),
            pl.BlockSpec((1, NC), lambda i: (0, 0)),
            row,
            row,
            row,
        ],
        out_specs=pl.BlockSpec((SLOTS, ROWS, width), lambda i: (0, i, 0)),
        out_shape=jax.ShapeDtypeStruct((SLOTS, count, width), jnp.bfloat16),
        scratch_shapes=[
            pltpu.VMEM((3 * TILE, TILE), jnp.bfloat16),
            pltpu.VMEM((SIDE * ROWS, SIDE * ROWS), jnp.bfloat16),
            pltpu.VMEM((SIDE * ROWS, PLANE), jnp.bfloat16),
            pltpu.VMEM((2, count, 2 * BLOCK), jnp.float32),
            pltpu.VMEM((2, count, 2 * BLOCK), jnp.int32),
        ],
        compiler_params=pltpu.CompilerParams(vmem_limit_bytes=60 * MIB),
        cost_estimate=pl.CostEstimate(
            flops=steps * 36 * 2 * TILE**3, bytes_accessed=count * NC * 3, transcendentals=0
        ),
        name="refine",
    )(
        taps.astype(jnp.float32).reshape(1, TAPS),
        functions,
        potential.reshape(1, NC),
        energies.reshape(1, count),
        start.reshape(1, count),
        length.reshape(1, count),
    )


class Order:
    def __init__(self):
        self.grid, self.rep = lax.axis_size("grid"), lax.axis_size("rep")
        self.devices = self.grid * self.rep
        self.far, self.near = self.grid // 2, self.rep

    def place(self, device):
        grid, rep = device // self.rep, device % self.rep
        return ((rep % 2 * (self.rep // 2) + rep // 2) * 2 + grid % 2) * self.far + grid // 2

    def device(self, place):
        high, low = place // self.far, place % self.far
        rep = high // 2 % (self.rep // 2) * 2 + high // 2 // (self.rep // 2)
        return (low * 2 + high % 2) * self.rep + rep

    def send(self, block, apart):
        pairs = [(i, self.device(self.place(i) ^ apart)) for i in range(self.devices)]
        return lax.ppermute(block, AXES, pairs)

    def gather(self, blocks):
        blocks = jnp.stack([blocks, self.send(blocks, self.devices // 2)])
        sent = [self.send(blocks, i * self.far) for i in range(1, self.near)]
        blocks = jnp.stack([blocks] + sent, axis=1)
        sent = [self.send(blocks, i) for i in range(1, self.far)]
        blocks = jnp.stack([blocks] + sent, axis=2)
        return blocks.reshape(self.devices, *blocks.shape[4:])


def members_of(partners_ref, blocks_ref, g):
    return jnp.concatenate(
        [blocks_ref[g]] + [blocks_ref[partners_ref[g, k]] for k in range(MEMBERS - 1)], axis=0
    )


def gram_kernel(
    order, fold, partners_ref, info_ref, start_ref, folded_ref, whole_ref, keep_ref, send_ref
):
    groups = folded_ref.shape[0]
    lane_block = (info_ref[1] + lax.broadcasted_iota(jnp.int32, (GROUP, fold), 1)) // BLOCK

    def unfold(i, carry):
        g = order.device(i ^ info_ref[0])
        near = jnp.broadcast_to(to_column(start_ref[i], GROUP), (GROUP, fold)) <= lane_block
        both = folded_ref[g, :, :fold].astype(jnp.float32)
        whole_ref[g, :, :fold] = jnp.where(near, both, 0.0).astype(jnp.bfloat16)
        whole_ref[g, :, fold : 2 * fold] = jnp.where(near, 0.0, both).astype(jnp.bfloat16)
        whole_ref[g, :, 2 * fold :] = folded_ref[g, :, fold:]
        return carry

    lax.fori_loop(0, groups, unfold, 0, unroll=4)

    def step(i, carry):
        for part, out_ref in enumerate((keep_ref, send_ref)):
            g = order.device((i + part * (groups // 2)) ^ info_ref[0])
            out_ref[i] = lax.dot_general(
                whole_ref[g], members_of(partners_ref, whole_ref, g), (((1,), (1,)), ((), ())),
                preferred_element_type=jnp.float32,
            ).astype(jnp.bfloat16)
        return carry

    lax.fori_loop(0, groups // 2, step, 0, unroll=2)


def gram(order, partners, info, start, folded, fold):
    groups, _, width = folded.shape
    whole = width + fold
    half = jax.ShapeDtypeStruct((groups // 2, GROUP, MEMBERS * GROUP), jnp.bfloat16)
    return pl.pallas_call(
        functools.partial(gram_kernel, order, fold),
        in_specs=[pl.BlockSpec(memory_space=pltpu.SMEM)] * 2
        + [pl.BlockSpec(memory_space=pltpu.VMEM)] * 2,
        out_specs=[pl.BlockSpec(memory_space=pltpu.VMEM)] * 3,
        out_shape=[jax.ShapeDtypeStruct((groups, GROUP, whole), jnp.bfloat16), half, half],
        compiler_params=pltpu.CompilerParams(vmem_limit_bytes=VMEM),
        cost_estimate=pl.CostEstimate(
            flops=groups * 2 * GROUP * GROUP * MEMBERS * whole,
            bytes_accessed=groups * GROUP * whole * 4,
            transcendentals=0,
        ),
        name="gram",
    )(partners, info, start, folded)


def add_kernel(count, pieces, *refs):
    outs = refs[count:]
    each = refs[0].shape[0] // pieces
    for o in range(pieces):
        total = refs[0][o * each : (o + 1) * each].astype(jnp.float32)
        for i in range(1, count):
            total = total + refs[i][o * each : (o + 1) * each].astype(jnp.float32)
        outs[o][...] = total.astype(jnp.bfloat16)


def add(arrays, pieces):
    shape = arrays[0].shape
    out = jax.ShapeDtypeStruct((shape[0] // pieces, *shape[1:]), jnp.bfloat16)
    return pl.pallas_call(
        functools.partial(add_kernel, len(arrays), pieces),
        out_shape=[out] * pieces,
        compiler_params=pltpu.CompilerParams(vmem_limit_bytes=VMEM),
        name="add",
    )(*arrays)


def couple_kernel(*refs):
    out_ref = refs[-1]
    total = refs[0][0].astype(jnp.float32)
    for ref in refs[1:-1]:
        total = total + ref[0].astype(jnp.float32)
    row = lax.broadcasted_iota(jnp.int32, total.shape, 0)
    col = lax.broadcasted_iota(jnp.int32, total.shape, 1)
    unit = jnp.where(row == col, 1.0, 0.0)
    out_ref[0] = (0.5 * (total * (1.0 / (BLOCK * LMAX)) - unit)).astype(jnp.bfloat16)


def couple(parts):
    return pl.pallas_call(
        couple_kernel,
        out_shape=jax.ShapeDtypeStruct(parts[0].shape, jnp.bfloat16),
        compiler_params=pltpu.CompilerParams(vmem_limit_bytes=VMEM),
        name="couple",
    )(*parts)


def correct_kernel(
    order, partners_ref, info_ref, held_ref, other_ref, whole_ref, out_ref
):
    half = held_ref.shape[0]
    for i in range(STEP):
        g = pl.program_id(0) * STEP + i
        apart = order.place(g) ^ info_ref[0]
        near = jnp.broadcast_to(apart, (GROUP, MEMBERS * GROUP)) < half
        coupling = jnp.where(
            near,
            held_ref[apart % half].astype(jnp.float32),
            other_ref[apart % half].astype(jnp.float32),
        ).astype(jnp.bfloat16)
        shifted = jnp.dot(
            coupling, members_of(partners_ref, whole_ref, g), preferred_element_type=jnp.float32
        )
        out_ref[i] = (whole_ref[g].astype(jnp.float32) - shifted).astype(jnp.bfloat16)


def correct(order, partners, info, held, other, whole):
    groups, _, width = whole.shape
    return pl.pallas_call(
        functools.partial(correct_kernel, order),
        grid=(groups // STEP,),
        in_specs=[pl.BlockSpec(memory_space=pltpu.SMEM)] * 2
        + [pl.BlockSpec(memory_space=pltpu.VMEM)] * 3,
        out_specs=pl.BlockSpec((STEP, GROUP, width), lambda g: (g, 0, 0)),
        out_shape=jax.ShapeDtypeStruct((groups, GROUP, width), jnp.bfloat16),
        compiler_params=pltpu.CompilerParams(vmem_limit_bytes=VMEM),
        cost_estimate=pl.CostEstimate(
            flops=groups * 2 * GROUP * GROUP * MEMBERS * width,
            bytes_accessed=groups * GROUP * width * 4,
            transcendentals=0,
        ),
        name="correct",
    )(partners, info, held, other, whole)


def place_kernel(in_ref, out_ref):
    for s in range(SLOTS):
        near, inner = s * EDGE, FOLD + s * INNER
        far = near + NC - FOLD
        out_ref[:, near : near + EDGE] = in_ref[s, :, :EDGE]
        out_ref[:, far : far + EDGE] = in_ref[s, :, EDGE : 2 * EDGE]
        out_ref[:, inner : inner + INNER] = in_ref[s, :, 2 * EDGE :]


def place(pieces):
    _, count, width = pieces.shape
    return pl.pallas_call(
        place_kernel,
        grid=(count // ROWS,),
        in_specs=[pl.BlockSpec((SLOTS, ROWS, width), lambda i: (0, i, 0))],
        out_specs=pl.BlockSpec((ROWS, NC), lambda i: (i, 0)),
        out_shape=jax.ShapeDtypeStruct((count, NC), jnp.bfloat16),
        compiler_params=pltpu.CompilerParams(vmem_limit_bytes=16 * MIB),
        cost_estimate=pl.CostEstimate(flops=0, bytes_accessed=count * NC * 4, transcendentals=0),
        name="place",
    )(pieces)


def split_slots(pieces, ratio, bounds):
    if ratio == 1:
        return pieces
    slots, rows, _ = pieces.shape
    parts = []
    for low, high in zip(bounds[:-1], bounds[1:]):
        part = pieces[:, :, low:high].reshape(slots, rows, ratio, (high - low) // ratio)
        parts.append(part.transpose(0, 2, 1, 3).reshape(slots * ratio, rows, -1))
    return jnp.concatenate(parts, axis=2)


def join_slots(pieces, ratio, bounds):
    if ratio == 1:
        return pieces
    count, rows, _ = pieces.shape
    parts = []
    for low, high in zip(bounds[:-1], bounds[1:]):
        part = pieces[:, :, low // ratio : high // ratio]
        part = part.reshape(count // ratio, ratio, rows, (high - low) // ratio)
        parts.append(part.transpose(0, 2, 1, 3).reshape(count // ratio, rows, high - low))
    return jnp.concatenate(parts, axis=2)


def exchange(pieces):
    return lax.all_to_all(pieces, AXES, split_axis=0, concat_axis=0, tiled=True)


def on_device(
    functions, filter_taps, potential, energies, region_start, region_length, partner_groups
):
    order = Order()
    ratio = order.devices // SLOTS
    me = lax.axis_index(AXES)
    info = jnp.stack([order.place(me), me * (FOLD // order.devices)]).astype(jnp.int32)
    pieces = refine(
        filter_taps, functions, potential, energies, region_start, region_length
    )
    folded = exchange(split_slots(pieces, ratio, (0, EDGE, EDGE + INNER)))
    starts = order.gather(region_start.reshape(1, 1, GROUP))
    fold = FOLD // order.devices
    whole, keep, send = gram(order, partner_groups, info, starts, folded, fold)
    pieces = add([keep, order.send(send, order.devices // 2)], order.near)
    arrived = [order.send(pieces[i], i * order.far) for i in range(1, order.near)]
    pieces = add([pieces[0]] + arrived, order.far)
    arrived = [order.send(pieces[i], i) for i in range(1, order.far)]
    coupling = couple([pieces[0]] + arrived)
    held = jnp.concatenate([coupling] + [order.send(coupling, i) for i in range(1, order.far)], 0)
    held = jnp.concatenate([held] + [order.send(held, i * order.far) for i in range(1, order.near)], 0)
    other = order.send(held, order.devices // 2)

    result = exchange(correct(order, partner_groups, info, held, other, whole))
    return place(join_slots(result, ratio, (0, EDGE, 2 * EDGE, 2 * EDGE + INNER)))


def solution(mesh):
    return jax.shard_map(
        on_device,
        mesh=mesh,
        in_specs=(
            P(AXES, None),
            P(),
            P(),
            P(AXES),
            P(AXES),
            P(AXES),
            P(),
        ),
        out_specs=P(AXES, None),
        check_vma=False,
    )
```

```python
import functools

import jax
import jax.numpy as jnp
from jax import lax
from jax.experimental import pallas as pl
from jax.experimental.pallas import tpu as pltpu
from jax.sharding import PartitionSpec as P

SIDE = 32
PLANE = SIDE * SIDE
NC = SIDE * PLANE
BLOCK = 64
NB = NC // BLOCK
GROUP = 64
TAPS = 16
MEMBERS = 4
LMAX = 384
FOLD = (NB - LMAX) * BLOCK
MID = NC - 2 * FOLD
SLOTS = 32
ROWS = 16
TILE = 256
EDGE = FOLD // SLOTS
INNER = MID // SLOTS
EDGE_SLOTS = PLANE // EDGE
INNER_SLOTS = PLANE // INNER
STEP = 4
FILL = 128
CUTS = (0, 8, 19, 26, 32)
AXES = ("grid", "rep")
MIB = 1024 * 1024
VMEM = 24 * MIB


def to_column(row, size):
    eye = lax.broadcasted_iota(jnp.int32, (size, size), 0) == lax.broadcasted_iota(
        jnp.int32, (size, size), 1
    )
    return jnp.sum(jnp.where(eye, jnp.broadcast_to(row, (size, size)), 0), axis=1, keepdims=True)


def tap_rows(taps, outer, shift, inner_first):
    size = outer if inner_first else TILE // outer
    row = lax.broadcasted_iota(jnp.int32, (size, TILE), 0)
    col = lax.broadcasted_iota(jnp.int32, (size, TILE), 1)
    col = col // (TILE // outer) if inner_first else col % (TILE // outer)
    distance = shift + row - col + TAPS // 2
    total = jnp.zeros(distance.shape, jnp.float32)
    for t in range(TAPS):
        total = jnp.where(distance == t, taps[t], total)
    return total


def spread_outer(rows, outer):
    inner = TILE // outer
    row = lax.broadcasted_iota(jnp.int32, (inner, TILE), 0)
    same = row == lax.broadcasted_iota(jnp.int32, (inner, TILE), 1) % inner
    return jnp.concatenate(
        [jnp.where(same, jnp.broadcast_to(rows[a : a + 1], (inner, TILE)), 0.0) for a in range(outer)], axis=0
    )


def spread_inner(rows, outer):
    inner = TILE // outer
    block = lax.broadcasted_iota(jnp.int32, (inner, TILE), 1) // inner
    return jnp.concatenate([jnp.where(block == a, rows, 0.0) for a in range(outer)], axis=0)


def refine_kernel(
    taps_ref, functions_ref, potential_ref, energies_ref, start_ref, length_ref, out_ref,
    plane_ref, line_ref, slabs_ref, rows_ref, ends_ref,
):
    count = energies_ref.shape[1]

    @pl.when(pl.program_id(0) == 0)
    def _():
        taps = [taps_ref[0, t] for t in range(TAPS)]
        outer = TILE // SIDE
        lines = []
        for j in range(3):
            part = spread_outer(tap_rows(taps, outer, (j - 1) * outer, True), outer)
            if j == 1:
                part = part + spread_inner(tap_rows(taps, outer, 0, False), outer)
            plane_ref[j * TILE : (j + 1) * TILE, :] = part.astype(jnp.bfloat16)
            flipped = [taps[TAPS - 1 - t] for t in range(TAPS)]
            rows = tap_rows(flipped, TILE // ROWS, (1 - j) * (TILE // ROWS) - 1, True)
            lines.append(spread_outer(rows, TILE // ROWS).astype(jnp.bfloat16))
        for h in range(SIDE * ROWS // TILE):
            for i in range(SIDE * ROWS // TILE):
                line_ref[h * TILE : (h + 1) * TILE, i * TILE : (i + 1) * TILE] = lines[i - h + 1]
        wide = (count, 2 * BLOCK)
        energy = to_column(energies_ref[...], count)
        first = to_column(start_ref[...], count)
        rows_ref[0] = jnp.broadcast_to(energy, wide)
        rows_ref[1] = jnp.broadcast_to(0.3 / (1.0 - energy), wide)
        ends_ref[0] = jnp.broadcast_to(first, wide)
        ends_ref[1] = jnp.broadcast_to(first + to_column(length_ref[...], count), wide)

    for x in range(SIDE):
        slabs_ref[x * ROWS : (x + 1) * ROWS, :] = functions_ref[:, x * PLANE : (x + 1) * PLANE]
    here = pl.ds(pl.multiple_of(pl.program_id(0) * ROWS, ROWS), ROWS)

    def widen(value):
        return jnp.concatenate([value] * (TILE // (2 * BLOCK)), axis=1)

    energy, scale = widen(rows_ref[0, here, :]), widen(rows_ref[1, here, :])
    lane_block = lax.broadcasted_iota(jnp.int32, (ROWS, TILE), 1) // BLOCK
    first = widen(ends_ref[0, here, :]) - lane_block
    last = widen(ends_ref[1, here, :]) - lane_block
    blocks = PLANE // TILE
    near, far = FOLD // PLANE, (NC - FOLD) // PLANE
    for j in range(blocks):
        cols = slice(j * TILE, (j + 1) * TILE)
        low, high = max(0, j - 1), min(blocks, j + 2)
        total = jnp.dot(
            slabs_ref[:, low * TILE : high * TILE],
            plane_ref[(low - j + 1) * TILE : (high - j + 1) * TILE, :],
            preferred_element_type=jnp.float32,
        ) + jnp.dot(line_ref[...], slabs_ref[:, cols], preferred_element_type=jnp.float32)

        def refined(x):
            rows = slice(x * ROWS, (x + 1) * ROWS)
            value = slabs_ref[rows, cols].astype(jnp.float32)
            place = potential_ref[0:1, x * PLANE + j * TILE : x * PLANE + (j + 1) * TILE]
            gradient = total[rows] + (place - energy) * value
            block = (x * PLANE + j * TILE) // BLOCK
            inside = (first <= block) & (last > block)
            return inside, value - scale * gradient

        for x in range(far):
            inside, value = refined(x)
            if x < near:
                inside_far, value_far = refined(x + far)
                value = jnp.where(inside, value, jnp.where(inside_far, value_far, 0.0))
                column = x * PLANE + j * TILE
                slot, place = column // EDGE, column % EDGE
            else:
                value = jnp.where(inside, value, 0.0)
                column = (x - near) * PLANE + j * TILE
                slot, place = column // INNER, EDGE + column % INNER
            out_ref[slot, :, place : place + TILE] = value.astype(jnp.bfloat16)


def refine(taps, functions, potential, energies, start, length):
    count = functions.shape[0]
    steps = count // ROWS
    width = EDGE + INNER
    row = pl.BlockSpec((1, count), lambda i: (0, 0))
    return pl.pallas_call(
        refine_kernel,
        grid=(steps,),
        in_specs=[
            pl.BlockSpec(memory_space=pltpu.SMEM),
            pl.BlockSpec((ROWS, NC), lambda i: (i, 0)),
            pl.BlockSpec((1, NC), lambda i: (0, 0)),
            row,
            row,
            row,
        ],
        out_specs=pl.BlockSpec((SLOTS, ROWS, width), lambda i: (0, i, 0)),
        out_shape=jax.ShapeDtypeStruct((SLOTS, count, width), jnp.bfloat16),
        scratch_shapes=[
            pltpu.VMEM((3 * TILE, TILE), jnp.bfloat16),
            pltpu.VMEM((SIDE * ROWS, SIDE * ROWS), jnp.bfloat16),
            pltpu.VMEM((SIDE * ROWS, PLANE), jnp.bfloat16),
            pltpu.VMEM((2, count, 2 * BLOCK), jnp.float32),
            pltpu.VMEM((2, count, 2 * BLOCK), jnp.int32),
        ],
        compiler_params=pltpu.CompilerParams(vmem_limit_bytes=60 * MIB),
        cost_estimate=pl.CostEstimate(
            flops=steps * 36 * 2 * TILE**3, bytes_accessed=count * NC * 3, transcendentals=0
        ),
        name="refine",
    )(
        taps.astype(jnp.float32).reshape(1, TAPS),
        functions,
        potential.reshape(1, NC),
        energies.reshape(1, count),
        start.reshape(1, count),
        length.reshape(1, count),
    )


class Order:
    def __init__(self):
        self.grid, self.rep = lax.axis_size("grid"), lax.axis_size("rep")
        self.devices = self.grid * self.rep
        self.far, self.near = self.grid // 2, self.rep

    def place(self, device):
        grid, rep = device // self.rep, device % self.rep
        return ((rep % 2 * (self.rep // 2) + rep // 2) * 2 + grid % 2) * self.far + grid // 2

    def device(self, place):
        high, low = place // self.far, place % self.far
        rep = high // 2 % (self.rep // 2) * 2 + high // 2 // (self.rep // 2)
        return (low * 2 + high % 2) * self.rep + rep

    def send(self, block, apart):
        pairs = [(i, self.device(self.place(i) ^ apart)) for i in range(self.devices)]
        return lax.ppermute(block, AXES, pairs)

    def gather(self, blocks):
        blocks = jnp.stack([blocks, self.send(blocks, self.devices // 2)])
        sent = [self.send(blocks, i * self.far) for i in range(1, self.near)]
        blocks = jnp.stack([blocks] + sent, axis=1)
        sent = [self.send(blocks, i) for i in range(1, self.far)]
        blocks = jnp.stack([blocks] + sent, axis=2)
        return blocks.reshape(self.devices, *blocks.shape[4:])


def members_of(partners_ref, blocks_ref, g, low=0, high=None):
    return jnp.concatenate(
        [blocks_ref[g, :, low:high]]
        + [blocks_ref[partners_ref[g, k], :, low:high] for k in range(MEMBERS - 1)],
        axis=0,
    )


def unfold(start_ref, info_ref, which, order, fill, folded_ref, whole_ref, begin=0):
    groups = folded_ref.shape[0]
    fold = FOLD // order.devices
    parts = [(0, fill, info_ref[which])]
    if fill < fold and folded_ref.shape[2] > fill:
        parts.append((fill, fold - fill, info_ref[which + 1]))

    def step(i, carry):
        first = to_column(start_ref[order.place(i + begin) ^ info_ref[0]], GROUP)
        for low, width, column in parts:
            lane = lax.broadcasted_iota(jnp.int32, (GROUP, width), 1)
            near = jnp.broadcast_to(first, (GROUP, width)) <= (column + lane) // BLOCK
            both = folded_ref[i, :, low : low + width].astype(jnp.float32)
            at = 2 * low
            whole_ref[i + begin, :, at : at + width] = jnp.where(near, both, 0.0).astype(jnp.bfloat16)
            at += width
            whole_ref[i + begin, :, at : at + width] = jnp.where(near, 0.0, both).astype(jnp.bfloat16)
        if folded_ref.shape[2] > fold:
            whole_ref[i + begin, :, 2 * fold :] = folded_ref[i, :, fold:]
        return carry

    lax.fori_loop(0, groups, step, 0, unroll=4)


def gram_kernel(
    order, fill, partners_ref, info_ref, start_ref, folded_ref, whole_ref, keep_ref, send_ref
):
    groups = folded_ref.shape[0]
    unfold(start_ref, info_ref, 1, order, fill, folded_ref, whole_ref)

    def step(i, carry):
        for part, out_ref in enumerate((keep_ref, send_ref)):
            g = order.device((i + part * (groups // 2)) ^ info_ref[0])
            out_ref[i] = lax.dot_general(
                whole_ref[g], members_of(partners_ref, whole_ref, g), (((1,), (1,)), ((), ())),
                preferred_element_type=jnp.float32,
            ).astype(jnp.bfloat16)
        return carry

    lax.fori_loop(0, groups // 2, step, 0, unroll=2)


def gram(order, fill, partners, info, start, folded):
    groups, _, width = folded.shape
    whole = width + FOLD // order.devices
    half = jax.ShapeDtypeStruct((groups // 2, GROUP, MEMBERS * GROUP), jnp.bfloat16)
    return pl.pallas_call(
        functools.partial(gram_kernel, order, fill),
        in_specs=[pl.BlockSpec(memory_space=pltpu.SMEM)] * 2
        + [pl.BlockSpec(memory_space=pltpu.VMEM)] * 2,
        out_specs=[pl.BlockSpec(memory_space=pltpu.VMEM)] * 3,
        out_shape=[jax.ShapeDtypeStruct((groups, GROUP, whole), jnp.bfloat16), half, half],
        compiler_params=pltpu.CompilerParams(vmem_limit_bytes=VMEM),
        cost_estimate=pl.CostEstimate(
            flops=groups * 2 * GROUP * GROUP * MEMBERS * whole,
            bytes_accessed=groups * GROUP * whole * 4,
            transcendentals=0,
        ),
        name="gram",
    )(partners, info, start, folded)


def add_kernel(count, pieces, *refs):
    outs = refs[count:]
    each = refs[0].shape[0] // pieces
    for o in range(pieces):
        total = refs[0][o * each : (o + 1) * each].astype(jnp.float32)
        for i in range(1, count):
            total = total + refs[i][o * each : (o + 1) * each].astype(jnp.float32)
        outs[o][...] = total.astype(jnp.bfloat16)


def add(arrays, pieces):
    shape = arrays[0].shape
    out = jax.ShapeDtypeStruct((shape[0] // pieces, *shape[1:]), jnp.bfloat16)
    return pl.pallas_call(
        functools.partial(add_kernel, len(arrays), pieces),
        out_shape=[out] * pieces,
        compiler_params=pltpu.CompilerParams(vmem_limit_bytes=VMEM),
        name="add",
    )(*arrays)


def couple_kernel(*refs):
    out_ref = refs[-1]
    total = refs[0][0].astype(jnp.float32)
    for ref in refs[1:-1]:
        total = total + ref[0].astype(jnp.float32)
    row = lax.broadcasted_iota(jnp.int32, total.shape, 0)
    col = lax.broadcasted_iota(jnp.int32, total.shape, 1)
    unit = jnp.where(row == col, 1.0, 0.0)
    out_ref[0] = (0.5 * (total * (1.0 / (BLOCK * LMAX)) - unit)).astype(jnp.bfloat16)


def couple(parts):
    return pl.pallas_call(
        couple_kernel,
        out_shape=jax.ShapeDtypeStruct(parts[0].shape, jnp.bfloat16),
        compiler_params=pltpu.CompilerParams(vmem_limit_bytes=VMEM),
        name="couple",
    )(*parts)


def corrected(partners_ref, coupling, whole_ref, g, low=0, high=None):
    shifted = jnp.dot(
        coupling, members_of(partners_ref, whole_ref, g, low, high),
        preferred_element_type=jnp.float32,
    )
    return (whole_ref[g, :, low:high].astype(jnp.float32) - shifted).astype(jnp.bfloat16)


def correct_kernel(
    order, low, partners_ref, info_ref, held_ref, other_ref, whole_ref, out_ref
):
    half = held_ref.shape[0]
    for i in range(STEP):
        g = pl.program_id(0) * STEP + i
        apart = order.place(g) ^ info_ref[0]
        near = jnp.broadcast_to(apart, (GROUP, MEMBERS * GROUP)) < half
        coupling = jnp.where(
            near,
            held_ref[apart % half].astype(jnp.float32),
            other_ref[apart % half].astype(jnp.float32),
        ).astype(jnp.bfloat16)
        out_ref[i] = corrected(partners_ref, coupling, whole_ref, g, low)


def correct(order, low, partners, info, held, other, whole):
    groups, _, width = whole.shape
    width = width - low
    return pl.pallas_call(
        functools.partial(correct_kernel, order, low),
        grid=(groups // STEP,),
        in_specs=[pl.BlockSpec(memory_space=pltpu.SMEM)] * 2
        + [pl.BlockSpec(memory_space=pltpu.VMEM)] * 3,
        out_specs=pl.BlockSpec((STEP, GROUP, width), lambda g: (g, 0, 0)),
        out_shape=jax.ShapeDtypeStruct((groups, GROUP, width), jnp.bfloat16),
        compiler_params=pltpu.CompilerParams(vmem_limit_bytes=VMEM),
        cost_estimate=pl.CostEstimate(
            flops=groups * 2 * GROUP * GROUP * MEMBERS * width,
            bytes_accessed=groups * GROUP * width * 4,
            transcendentals=0,
        ),
        name="correct",
    )(partners, info, held, other, whole)


def correct_half_kernel(
    order, low, partners_ref, info_ref, start_ref, held_ref, other_ref, whole_ref, *refs
):
    out_ref, filled_ref = refs[-2:]
    begin = 0
    for folded_ref in refs[:-2]:
        unfold(start_ref, info_ref, 3, order, low // 2, folded_ref, filled_ref, begin)
        begin += folded_ref.shape[0]
    half = held_ref.shape[0]
    for apart in range(out_ref.shape[0]):
        g = info_ref[4] ^ apart
        at = order.place(apart)
        coupling = (held_ref if at < half else other_ref)[at % half]
        out_ref[apart, :, :low] = corrected(partners_ref, coupling, whole_ref, g, 0, low)
        out_ref[apart, :, low:] = corrected(partners_ref, coupling, filled_ref, g)


def correct_half(order, partners, info, starts, held, other, whole, filled):
    low = 2 * filled[0].shape[2]
    count = order.devices // 2
    return pl.pallas_call(
        functools.partial(correct_half_kernel, order, low),
        in_specs=[pl.BlockSpec(memory_space=pltpu.SMEM)] * 2
        + [pl.BlockSpec(memory_space=pltpu.VMEM)] * (4 + len(filled)),
        out_specs=pl.BlockSpec(memory_space=pltpu.VMEM),
        out_shape=jax.ShapeDtypeStruct((count, GROUP, 2 * low), jnp.bfloat16),
        scratch_shapes=[pltpu.VMEM((order.devices, GROUP, low), jnp.bfloat16)],
        compiler_params=pltpu.CompilerParams(vmem_limit_bytes=VMEM),
        cost_estimate=pl.CostEstimate(
            flops=count * 4 * GROUP * GROUP * MEMBERS * low,
            bytes_accessed=count * GROUP * low * 12,
            transcendentals=0,
        ),
        name="correct_half",
    )(partners, info, starts, held, other, whole, *filled)


def place_kernel(base_ref, in_ref, *refs):
    out_ref = refs[-1]
    rest = EDGE - FILL
    for s in range(SLOTS):
        near, inner = s * EDGE + FILL, FOLD + s * INNER
        far = near + NC - FOLD
        if rest:
            out_ref[:, near : near + rest] = in_ref[s, :, :rest]
            out_ref[:, far : far + rest] = in_ref[s, :, rest : 2 * rest]
        out_ref[:, inner : inner + INNER] = in_ref[s, :, 2 * rest :]
    for apart, piece_ref in enumerate(refs[:-1]):
        slot = base_ref[0] ^ apart
        for part, s in enumerate((slot, slot ^ (SLOTS // 2))):
            near = pl.multiple_of(s * EDGE, EDGE)
            far = pl.multiple_of(s * EDGE + NC - FOLD, EDGE)
            low = 2 * part * FILL
            out_ref[:, pl.ds(near, FILL)] = piece_ref[0, :, low : low + FILL]
            out_ref[:, pl.ds(far, FILL)] = piece_ref[0, :, low + FILL : low + 2 * FILL]


def place(base, pieces, half):
    _, count, width = pieces.shape
    return pl.pallas_call(
        place_kernel,
        grid=(count // ROWS,),
        in_specs=[
            pl.BlockSpec(memory_space=pltpu.SMEM),
            pl.BlockSpec((SLOTS, ROWS, width), lambda i: (0, i, 0)),
        ]
        + [pl.BlockSpec((1, ROWS, 4 * FILL), lambda i: (0, i, 0))] * len(half),
        out_specs=pl.BlockSpec((ROWS, NC), lambda i: (i, 0)),
        out_shape=jax.ShapeDtypeStruct((count, NC), jnp.bfloat16),
        compiler_params=pltpu.CompilerParams(vmem_limit_bytes=60 * MIB),
        cost_estimate=pl.CostEstimate(flops=0, bytes_accessed=count * NC * 4, transcendentals=0),
        name="place",
    )(base, pieces, *half)


def split_slots(pieces, ratio, bounds):
    if ratio == 1:
        return pieces
    slots, rows, _ = pieces.shape
    parts = []
    for low, high in zip(bounds[:-1], bounds[1:]):
        part = pieces[:, :, low:high].reshape(slots, rows, ratio, (high - low) // ratio)
        parts.append(part.transpose(0, 2, 1, 3).reshape(slots * ratio, rows, -1))
    return jnp.concatenate(parts, axis=2)


def join_slots(pieces, ratio, bounds):
    if ratio == 1:
        return pieces
    count, rows, _ = pieces.shape
    parts = []
    for low, high in zip(bounds[:-1], bounds[1:]):
        part = pieces[:, :, low // ratio : high // ratio]
        part = part.reshape(count // ratio, ratio, rows, (high - low) // ratio)
        parts.append(part.transpose(0, 2, 1, 3).reshape(count // ratio, rows, high - low))
    return jnp.concatenate(parts, axis=2)


def exchange(pieces):
    return lax.all_to_all(pieces, AXES, split_axis=0, concat_axis=0, tiled=True)


def on_device(
    functions, filter_taps, potential, energies, region_start, region_length, partner_groups
):
    order = Order()
    ratio = order.devices // SLOTS
    me = lax.axis_index(AXES)
    fill, rest = FILL // ratio, (EDGE - FILL) // ratio
    away = me ^ (order.devices // 2)
    slot, part = me // ratio, me % ratio
    info = [order.place(me), slot * EDGE + part * fill, slot * EDGE + FILL + part * rest]
    info += [away // ratio * EDGE + part * fill, me]
    info = jnp.stack(info).astype(jnp.int32)

    pieces = refine(
        filter_taps, functions, potential, energies, region_start, region_length
    )
    bounds = (0, FILL, EDGE, EDGE + INNER) if rest else (0, EDGE, EDGE + INNER)
    folded = exchange(split_slots(pieces, ratio, bounds))
    starts = order.gather(region_start.reshape(1, 1, GROUP))
    def across(block):
        return order.send(block, order.far // 2)

    barrier = lax.optimization_barrier
    cuts = [cut * ratio for cut in CUTS]
    filled = [folded[low:high, :, :fill] for low, high in zip(cuts[:-1], cuts[1:])]
    folded, *filled = barrier((folded, *filled))
    filled[0] = across(filled[0])
    whole, keep, send = gram(order, fill, partner_groups, info, starts, folded)
    keep, send, filled[0] = barrier((keep, send, filled[0]))
    filled[1] = across(filled[1])
    pieces = add([keep, order.send(send, order.devices // 2)], order.near)
    arrived = [order.send(pieces[i], i * order.far) for i in range(1, order.near)]
    pieces = add([pieces[0]] + arrived, order.far)
    *pieces, filled[1] = barrier((*pieces, filled[1]))
    arrived = [order.send(pieces[i], i) for i in range(1, order.far)]
    coupling = couple([pieces[0]] + arrived)
    held = jnp.concatenate([coupling] + [order.send(coupling, i) for i in range(1, order.far)], 0)
    held, filled[2] = barrier((held, filled[2]))
    filled[2] = across(filled[2])
    held = jnp.concatenate([held] + [order.send(held, i * order.far) for i in range(1, order.near)], 0)
    held, filled[2], filled[3] = barrier((held, filled[2], filled[3]))
    filled[3] = across(filled[3])
    other = order.send(held, order.devices // 2)

    result = correct(order, 2 * fill, partner_groups, info, held, other, whole)
    half = correct_half(order, partner_groups, info, starts, held, other, whole, filled)
    result, half = barrier((result, half))
    result = exchange(result)
    half = [half[i : i + 1] for i in range(half.shape[0])]
    half = [half[0]] + [order.send(half[i], order.place(i)) for i in range(1, len(half))]
    base = me
    if ratio > 1:
        low = me % (order.devices // 2)
        half = jnp.concatenate(half, 0)[low ^ jnp.arange(len(half))]
        half = join_slots(half, ratio, tuple(i * FILL for i in range(5)))
        half = [half[i : i + 1] for i in range(SLOTS // 2)]
        base = slot // (SLOTS // 2) * (SLOTS // 2)
    rest = EDGE - FILL
    bounds = (0, rest, 2 * rest, 2 * rest + INNER) if rest else (0, INNER)
    return place(base.astype(jnp.int32).reshape(1), join_slots(result, ratio, bounds), half)


def solution(mesh):
    return jax.shard_map(
        on_device,
        mesh=mesh,
        in_specs=(
            P(AXES, None),
            P(),
            P(),
            P(AXES),
            P(AXES),
            P(AXES),
            P(),
        ),
        out_specs=P(AXES, None),
        check_vma=False,
    )
```

```python
import functools

import jax
import jax.numpy as jnp
from jax import lax
from jax.experimental import pallas as pl
from jax.experimental.pallas import tpu as pltpu
from jax.sharding import PartitionSpec as P

SIDE = 32
PLANE = SIDE * SIDE
NC = SIDE * PLANE
BLOCK = 64
NB = NC // BLOCK
GROUP = 64
TAPS = 16
MEMBERS = 4
LMAX = 384
FOLD = (NB - LMAX) * BLOCK
MID = NC - 2 * FOLD
SLOTS = 32
ROWS = 16
TILE = 256
EDGE = FOLD // SLOTS
INNER = MID // SLOTS
EDGE_SLOTS = PLANE // EDGE
INNER_SLOTS = PLANE // INNER
STEP = 4
CUTS = (0, 4, 10, 13, 16)
AXES = ("grid", "rep")
MIB = 1024 * 1024
VMEM = 24 * MIB


def to_column(row, size):
    eye = lax.broadcasted_iota(jnp.int32, (size, size), 0) == lax.broadcasted_iota(
        jnp.int32, (size, size), 1
    )
    return jnp.sum(jnp.where(eye, jnp.broadcast_to(row, (size, size)), 0), axis=1, keepdims=True)


def tap_rows(taps, outer, shift, inner_first):
    size = outer if inner_first else TILE // outer
    row = lax.broadcasted_iota(jnp.int32, (size, TILE), 0)
    col = lax.broadcasted_iota(jnp.int32, (size, TILE), 1)
    col = col // (TILE // outer) if inner_first else col % (TILE // outer)
    distance = shift + row - col + TAPS // 2
    total = jnp.zeros(distance.shape, jnp.float32)
    for t in range(TAPS):
        total = jnp.where(distance == t, taps[t], total)
    return total


def spread_outer(rows, outer):
    inner = TILE // outer
    row = lax.broadcasted_iota(jnp.int32, (inner, TILE), 0)
    same = row == lax.broadcasted_iota(jnp.int32, (inner, TILE), 1) % inner
    return jnp.concatenate(
        [jnp.where(same, jnp.broadcast_to(rows[a : a + 1], (inner, TILE)), 0.0) for a in range(outer)], axis=0
    )


def spread_inner(rows, outer):
    inner = TILE // outer
    block = lax.broadcasted_iota(jnp.int32, (inner, TILE), 1) // inner
    return jnp.concatenate([jnp.where(block == a, rows, 0.0) for a in range(outer)], axis=0)


def refine_kernel(
    taps_ref, functions_ref, potential_ref, energies_ref, start_ref, length_ref, out_ref,
    plane_ref, line_ref, slabs_ref, rows_ref, ends_ref,
):
    count = energies_ref.shape[1]

    @pl.when(pl.program_id(0) == 0)
    def _():
        taps = [taps_ref[0, t] for t in range(TAPS)]
        outer = TILE // SIDE
        lines = []
        for j in range(3):
            part = spread_outer(tap_rows(taps, outer, (j - 1) * outer, True), outer)
            if j == 1:
                part = part + spread_inner(tap_rows(taps, outer, 0, False), outer)
            plane_ref[j * TILE : (j + 1) * TILE, :] = part.astype(jnp.bfloat16)
            flipped = [taps[TAPS - 1 - t] for t in range(TAPS)]
            rows = tap_rows(flipped, TILE // ROWS, (1 - j) * (TILE // ROWS) - 1, True)
            lines.append(spread_outer(rows, TILE // ROWS).astype(jnp.bfloat16))
        for h in range(SIDE * ROWS // TILE):
            for i in range(SIDE * ROWS // TILE):
                line_ref[h * TILE : (h + 1) * TILE, i * TILE : (i + 1) * TILE] = lines[i - h + 1]
        wide = (count, 2 * BLOCK)
        energy = to_column(energies_ref[...], count)
        first = to_column(start_ref[...], count)
        rows_ref[0] = jnp.broadcast_to(energy, wide)
        rows_ref[1] = jnp.broadcast_to(0.3 / (1.0 - energy), wide)
        ends_ref[0] = jnp.broadcast_to(first, wide)
        ends_ref[1] = jnp.broadcast_to(first + to_column(length_ref[...], count), wide)

    for x in range(SIDE):
        slabs_ref[x * ROWS : (x + 1) * ROWS, :] = functions_ref[:, x * PLANE : (x + 1) * PLANE]
    here = pl.ds(pl.multiple_of(pl.program_id(0) * ROWS, ROWS), ROWS)

    def widen(value):
        return jnp.concatenate([value] * (TILE // (2 * BLOCK)), axis=1)

    energy, scale = widen(rows_ref[0, here, :]), widen(rows_ref[1, here, :])
    lane_block = lax.broadcasted_iota(jnp.int32, (ROWS, TILE), 1) // BLOCK
    first = widen(ends_ref[0, here, :]) - lane_block
    last = widen(ends_ref[1, here, :]) - lane_block
    blocks = PLANE // TILE
    near, far = FOLD // PLANE, (NC - FOLD) // PLANE
    for j in range(blocks):
        cols = slice(j * TILE, (j + 1) * TILE)
        low, high = max(0, j - 1), min(blocks, j + 2)
        total = jnp.dot(
            slabs_ref[:, low * TILE : high * TILE],
            plane_ref[(low - j + 1) * TILE : (high - j + 1) * TILE, :],
            preferred_element_type=jnp.float32,
        ) + jnp.dot(line_ref[...], slabs_ref[:, cols], preferred_element_type=jnp.float32)

        def refined(x):
            rows = slice(x * ROWS, (x + 1) * ROWS)
            value = slabs_ref[rows, cols].astype(jnp.float32)
            place = potential_ref[0:1, x * PLANE + j * TILE : x * PLANE + (j + 1) * TILE]
            gradient = total[rows] + (place - energy) * value
            block = (x * PLANE + j * TILE) // BLOCK
            inside = (first <= block) & (last > block)
            return inside, value - scale * gradient

        for x in range(far):
            inside, value = refined(x)
            if x < near:
                inside_far, value_far = refined(x + far)
                value = jnp.where(inside, value, jnp.where(inside_far, value_far, 0.0))
                column = x * PLANE + j * TILE
                slot, place = column // EDGE, column % EDGE
            else:
                value = jnp.where(inside, value, 0.0)
                column = (x - near) * PLANE + j * TILE
                slot, place = column // INNER, EDGE + column % INNER
            out_ref[slot, :, place : place + TILE] = value.astype(jnp.bfloat16)


def refine(taps, functions, potential, energies, start, length):
    count = functions.shape[0]
    steps = count // ROWS
    width = EDGE + INNER
    row = pl.BlockSpec((1, count), lambda i: (0, 0))
    return pl.pallas_call(
        refine_kernel,
        grid=(steps,),
        in_specs=[
            pl.BlockSpec(memory_space=pltpu.SMEM),
            pl.BlockSpec((ROWS, NC), lambda i: (i, 0)),
            pl.BlockSpec((1, NC), lambda i: (0, 0)),
            row,
            row,
            row,
        ],
        out_specs=pl.BlockSpec((SLOTS, ROWS, width), lambda i: (0, i, 0)),
        out_shape=jax.ShapeDtypeStruct((SLOTS, count, width), jnp.bfloat16),
        scratch_shapes=[
            pltpu.VMEM((3 * TILE, TILE), jnp.bfloat16),
            pltpu.VMEM((SIDE * ROWS, SIDE * ROWS), jnp.bfloat16),
            pltpu.VMEM((SIDE * ROWS, PLANE), jnp.bfloat16),
            pltpu.VMEM((2, count, 2 * BLOCK), jnp.float32),
            pltpu.VMEM((2, count, 2 * BLOCK), jnp.int32),
        ],
        compiler_params=pltpu.CompilerParams(vmem_limit_bytes=60 * MIB),
        cost_estimate=pl.CostEstimate(
            flops=steps * 36 * 2 * TILE**3, bytes_accessed=count * NC * 3, transcendentals=0
        ),
        name="refine",
    )(
        taps.astype(jnp.float32).reshape(1, TAPS),
        functions,
        potential.reshape(1, NC),
        energies.reshape(1, count),
        start.reshape(1, count),
        length.reshape(1, count),
    )


class Order:
    def __init__(self):
        self.grid, self.rep = lax.axis_size("grid"), lax.axis_size("rep")
        self.devices = self.grid * self.rep
        self.far, self.near = self.grid // 2, self.rep

    def place(self, device):
        grid, rep = device // self.rep, device % self.rep
        return ((rep % 2 * (self.rep // 2) + rep // 2) * 2 + grid % 2) * self.far + grid // 2

    def device(self, place):
        high, low = place // self.far, place % self.far
        rep = high // 2 % (self.rep // 2) * 2 + high // 2 // (self.rep // 2)
        return (low * 2 + high % 2) * self.rep + rep

    def send(self, block, apart):
        pairs = [(i, self.device(self.place(i) ^ apart)) for i in range(self.devices)]
        return lax.ppermute(block, AXES, pairs)

    def send_device(self, block, apart):
        return self.send(block, self.place(apart))

    def exchange_half(self, mine, theirs):
        theirs = self.send_device(theirs, 1)
        pairs = [jnp.stack([mine[i], theirs[i]]) for i in range(mine.shape[0])]
        return pairs[:1] + [self.send_device(pairs[i], 2 * i) for i in range(1, len(pairs))]

    def gather(self, blocks):
        blocks = jnp.stack([blocks, self.send(blocks, self.devices // 2)])
        sent = [self.send(blocks, i * self.far) for i in range(1, self.near)]
        blocks = jnp.stack([blocks] + sent, axis=1)
        sent = [self.send(blocks, i) for i in range(1, self.far)]
        blocks = jnp.stack([blocks] + sent, axis=2)
        return blocks.reshape(self.devices, *blocks.shape[4:])


def members_of(partners_ref, blocks_ref, g, low=0):
    return jnp.concatenate(
        [blocks_ref[g, :, low:]]
        + [blocks_ref[partners_ref[g, k], :, low:] for k in range(MEMBERS - 1)],
        axis=0,
    )


def unfold(order, start_ref, info_ref, which, folded, g, edge_ref):
    width = folded.shape[1]
    column = info_ref[which] + lax.broadcasted_iota(jnp.int32, (GROUP, width), 1)
    first = to_column(start_ref[order.place(g) ^ info_ref[0]], GROUP)
    near = jnp.broadcast_to(first, (GROUP, width)) <= column // BLOCK
    both = folded.astype(jnp.float32)
    edge_ref[g, :, :width] = jnp.where(near, both, 0.0).astype(jnp.bfloat16)
    edge_ref[g, :, width:] = jnp.where(near, 0.0, both).astype(jnp.bfloat16)


def gram_kernel(
    order, partners_ref, info_ref, start_ref, folded_ref, edge_ref, keep_ref, send_ref
):
    groups = folded_ref.shape[0]
    fold = edge_ref.shape[2] // 2

    def open_up(g, carry):
        unfold(order, start_ref, info_ref, 1, folded_ref[g, :, :fold], g, edge_ref)
        return carry

    lax.fori_loop(0, groups, open_up, 0, unroll=4)

    def step(i, carry):
        for part, out_ref in enumerate((keep_ref, send_ref)):
            g = order.device((i + part * (groups // 2)) ^ info_ref[0])
            total = 0.0
            for ref, low in ((edge_ref, 0), (folded_ref, fold)):
                total = total + lax.dot_general(
                    ref[g, :, low:], members_of(partners_ref, ref, g, low),
                    (((1,), (1,)), ((), ())), preferred_element_type=jnp.float32,
                )
            out_ref[i] = total.astype(jnp.bfloat16)
        return carry

    lax.fori_loop(0, groups // 2, step, 0, unroll=2)


def gram(order, partners, info, start, folded):
    groups, _, width = folded.shape
    fold = FOLD // order.devices
    half = jax.ShapeDtypeStruct((groups // 2, GROUP, MEMBERS * GROUP), jnp.bfloat16)
    return pl.pallas_call(
        functools.partial(gram_kernel, order),
        in_specs=[pl.BlockSpec(memory_space=pltpu.SMEM)] * 2
        + [pl.BlockSpec(memory_space=pltpu.VMEM)] * 2,
        out_specs=[pl.BlockSpec(memory_space=pltpu.VMEM)] * 3,
        out_shape=[jax.ShapeDtypeStruct((groups, GROUP, 2 * fold), jnp.bfloat16), half, half],
        compiler_params=pltpu.CompilerParams(vmem_limit_bytes=VMEM),
        cost_estimate=pl.CostEstimate(
            flops=groups * 2 * GROUP * GROUP * MEMBERS * (width + fold),
            bytes_accessed=groups * GROUP * width * 4,
            transcendentals=0,
        ),
        name="gram",
    )(partners, info, start, folded)


def add_kernel(count, pieces, *refs):
    outs = refs[count:]
    each = refs[0].shape[0] // pieces
    for o in range(pieces):
        total = refs[0][o * each : (o + 1) * each].astype(jnp.float32)
        for i in range(1, count):
            total = total + refs[i][o * each : (o + 1) * each].astype(jnp.float32)
        outs[o][...] = total.astype(jnp.bfloat16)


def add(arrays, pieces):
    shape = arrays[0].shape
    out = jax.ShapeDtypeStruct((shape[0] // pieces, *shape[1:]), jnp.bfloat16)
    return pl.pallas_call(
        functools.partial(add_kernel, len(arrays), pieces),
        out_shape=[out] * pieces,
        compiler_params=pltpu.CompilerParams(vmem_limit_bytes=VMEM),
        name="add",
    )(*arrays)


def couple_kernel(*refs):
    out_ref = refs[-1]
    total = refs[0][0].astype(jnp.float32)
    for ref in refs[1:-1]:
        total = total + ref[0].astype(jnp.float32)
    row = lax.broadcasted_iota(jnp.int32, total.shape, 0)
    col = lax.broadcasted_iota(jnp.int32, total.shape, 1)
    unit = jnp.where(row == col, 1.0, 0.0)
    out_ref[0] = (0.5 * (total * (1.0 / (BLOCK * LMAX)) - unit)).astype(jnp.bfloat16)


def couple(parts):
    return pl.pallas_call(
        couple_kernel,
        out_shape=jax.ShapeDtypeStruct(parts[0].shape, jnp.bfloat16),
        compiler_params=pltpu.CompilerParams(vmem_limit_bytes=VMEM),
        name="couple",
    )(*parts)


def corrected(partners_ref, coupling, blocks_ref, g, low=0):
    shifted = jnp.dot(
        coupling, members_of(partners_ref, blocks_ref, g, low),
        preferred_element_type=jnp.float32,
    )
    return (blocks_ref[g, :, low:].astype(jnp.float32) - shifted).astype(jnp.bfloat16)


def correct_kernel(
    order, low, partners_ref, info_ref, held_ref, other_ref, whole_ref, out_ref
):
    half = held_ref.shape[0]
    for i in range(STEP):
        g = pl.program_id(0) * STEP + i
        apart = order.place(g) ^ info_ref[0]
        near = jnp.broadcast_to(apart, (GROUP, MEMBERS * GROUP)) < half
        coupling = jnp.where(
            near,
            held_ref[apart % half].astype(jnp.float32),
            other_ref[apart % half].astype(jnp.float32),
        ).astype(jnp.bfloat16)
        out_ref[i] = corrected(partners_ref, coupling, whole_ref, g, low)


def correct(order, low, partners, info, held, other, whole):
    groups, _, width = whole.shape
    width = width - low
    return pl.pallas_call(
        functools.partial(correct_kernel, order, low),
        grid=(groups // STEP,),
        in_specs=[pl.BlockSpec(memory_space=pltpu.SMEM)] * 2
        + [pl.BlockSpec(memory_space=pltpu.VMEM)] * 3,
        out_specs=pl.BlockSpec((STEP, GROUP, width), lambda g: (g, 0, 0)),
        out_shape=jax.ShapeDtypeStruct((groups, GROUP, width), jnp.bfloat16),
        compiler_params=pltpu.CompilerParams(vmem_limit_bytes=VMEM),
        cost_estimate=pl.CostEstimate(
            flops=groups * 2 * GROUP * GROUP * MEMBERS * width,
            bytes_accessed=groups * GROUP * width * 4,
            transcendentals=0,
        ),
        name="correct",
    )(partners, info, held, other, whole)


def correct_half_kernel(
    order, count, partners_ref, info_ref, start_ref, held_ref, other_ref, edge_ref, *refs
):
    *folded_refs, mine_ref, theirs_ref, filled_ref = refs
    me, half = info_ref[3], order.devices // 2
    apart = 0
    for ref in folded_refs[:count]:
        for i in range(ref.shape[0]):
            unfold(order, start_ref, info_ref, 2, ref[i], me ^ apart, filled_ref)
            apart += 1
    begin = (me // half ^ 1) * half
    for ref in folded_refs[count:]:
        for i in range(ref.shape[0]):
            unfold(order, start_ref, info_ref, 2, ref[i], begin + i, filled_ref)
        begin += ref.shape[0]
    low = edge_ref.shape[2]
    for apart in range(half):
        g = me ^ apart
        at = order.place(apart)
        coupling = (held_ref if at < half else other_ref)[at % half]
        out_ref = theirs_ref if apart % 2 else mine_ref
        out_ref[apart // 2, :, :low] = corrected(partners_ref, coupling, edge_ref, g)
        out_ref[apart // 2, :, low:] = corrected(partners_ref, coupling, filled_ref, g)


def correct_half(order, partners, info, starts, held, other, edge, local, across):
    low = edge.shape[2]
    count = order.devices // 2
    shape = jax.ShapeDtypeStruct((count // 2, GROUP, 2 * low), jnp.bfloat16)
    folded = [*local, *across]
    return pl.pallas_call(
        functools.partial(correct_half_kernel, order, len(local)),
        in_specs=[pl.BlockSpec(memory_space=pltpu.SMEM)] * 2
        + [pl.BlockSpec(memory_space=pltpu.VMEM)] * (4 + len(folded)),
        out_specs=[pl.BlockSpec(memory_space=pltpu.VMEM)] * 2,
        out_shape=[shape] * 2,
        scratch_shapes=[pltpu.VMEM(edge.shape, jnp.bfloat16)],
        compiler_params=pltpu.CompilerParams(vmem_limit_bytes=VMEM),
        cost_estimate=pl.CostEstimate(
            flops=count * 4 * GROUP * GROUP * MEMBERS * low,
            bytes_accessed=count * GROUP * low * 12,
            transcendentals=0,
        ),
        name="correct_half",
    )(partners, info, starts, held, other, edge, *folded)


def place_kernel(base_ref, in_ref, *refs):
    out_ref = refs[-1]
    for s in range(SLOTS):
        out_ref[:, FOLD + s * INNER : FOLD + (s + 1) * INNER] = in_ref[s]
    apart = 0
    for piece_ref in refs[:-1]:
        for i in range(piece_ref.shape[0]):
            slot = base_ref[0] ^ apart
            apart += 1
            for part, s in enumerate((slot, slot ^ (SLOTS // 2))):
                near = pl.multiple_of(s * EDGE, EDGE)
                far = pl.multiple_of(s * EDGE + NC - FOLD, EDGE)
                low = 2 * part * EDGE
                out_ref[:, pl.ds(near, EDGE)] = piece_ref[i, :, low : low + EDGE]
                out_ref[:, pl.ds(far, EDGE)] = piece_ref[i, :, low + EDGE : low + 2 * EDGE]


def place(base, pieces, half):
    _, count, width = pieces.shape
    blocks = [pieces, *half]
    return pl.pallas_call(
        place_kernel,
        grid=(count // ROWS,),
        in_specs=[pl.BlockSpec(memory_space=pltpu.SMEM)]
        + [pl.BlockSpec((b.shape[0], ROWS, b.shape[2]), lambda i: (0, i, 0)) for b in blocks],
        out_specs=pl.BlockSpec((ROWS, NC), lambda i: (i, 0)),
        out_shape=jax.ShapeDtypeStruct((count, NC), jnp.bfloat16),
        compiler_params=pltpu.CompilerParams(vmem_limit_bytes=60 * MIB),
        cost_estimate=pl.CostEstimate(flops=0, bytes_accessed=count * NC * 4, transcendentals=0),
        name="place",
    )(base, *blocks)


def split_slots(pieces, ratio, bounds):
    if ratio == 1:
        return pieces
    slots, rows, _ = pieces.shape
    parts = []
    for low, high in zip(bounds[:-1], bounds[1:]):
        part = pieces[:, :, low:high].reshape(slots, rows, ratio, (high - low) // ratio)
        parts.append(part.transpose(0, 2, 1, 3).reshape(slots * ratio, rows, -1))
    return jnp.concatenate(parts, axis=2)


def join_slots(pieces, ratio, bounds):
    if ratio == 1:
        return pieces
    count, rows, _ = pieces.shape
    parts = []
    for low, high in zip(bounds[:-1], bounds[1:]):
        part = pieces[:, :, low // ratio : high // ratio]
        part = part.reshape(count // ratio, ratio, rows, (high - low) // ratio)
        parts.append(part.transpose(0, 2, 1, 3).reshape(count // ratio, rows, high - low))
    return jnp.concatenate(parts, axis=2)


def exchange(pieces):
    return lax.all_to_all(pieces, AXES, split_axis=0, concat_axis=0, tiled=True)


def on_device(
    functions, filter_taps, potential, energies, region_start, region_length, partner_groups
):
    order = Order()
    ratio = order.devices // SLOTS
    me = lax.axis_index(AXES)
    half_count = order.devices // 2
    fold = FOLD // order.devices
    info = jnp.stack([order.place(me), me * fold, (me ^ half_count) * fold, me]).astype(jnp.int32)

    pieces = refine(
        filter_taps, functions, potential, energies, region_start, region_length
    )
    pieces = split_slots(pieces, ratio, (0, EDGE, EDGE + INNER))
    folded = exchange(pieces)
    starts = order.gather(region_start.reshape(1, 1, GROUP))
    to = me ^ half_count ^ jnp.arange(half_count)
    mine, theirs = [jnp.take(pieces[:, :, :fold], to[i::2], axis=0) for i in range(2)]
    local = order.exchange_half(mine, theirs)

    barrier = lax.optimization_barrier

    def across(block):
        return order.send_device(block, half_count)

    folded, *local = barrier((folded, *local))
    begin = me // half_count * half_count
    cuts = [cut * ratio for cut in CUTS]
    filled = [
        lax.dynamic_slice(folded, (begin + low, 0, 0), (high - low, GROUP, fold))
        for low, high in zip(cuts[:-1], cuts[1:])
    ]
    folded, *filled = barrier((folded, *filled))
    filled[0] = across(filled[0])
    edge, keep, send = gram(order, partner_groups, info, starts, folded)
    keep, send, filled[0] = barrier((keep, send, filled[0]))
    filled[1] = across(filled[1])
    pieces = add([keep, order.send(send, order.devices // 2)], order.near)
    arrived = [order.send(pieces[i], i * order.far) for i in range(1, order.near)]
    pieces = add([pieces[0]] + arrived, order.far)
    *pieces, filled[1] = barrier((*pieces, filled[1]))
    arrived = [order.send(pieces[i], i) for i in range(1, order.far)]
    coupling = couple([pieces[0]] + arrived)
    held = jnp.concatenate([coupling] + [order.send(coupling, i) for i in range(1, order.far)], 0)
    held, filled[2] = barrier((held, filled[2]))
    filled[2] = across(filled[2])
    held = jnp.concatenate([held] + [order.send(held, i * order.far) for i in range(1, order.near)], 0)
    held, filled[2], filled[3] = barrier((held, filled[2], filled[3]))
    filled[3] = across(filled[3])
    other = order.send(held, order.devices // 2)

    result = correct(order, fold, partner_groups, info, held, other, folded)
    mine, theirs = correct_half(
        order, partner_groups, info, starts, held, other, edge, local, filled
    )
    result, mine, theirs = barrier((result, mine, theirs))
    result = exchange(result)
    half = order.exchange_half(mine, theirs)
    base = me
    if ratio > 1:
        half = jnp.concatenate(half, 0)[me % half_count ^ jnp.arange(half_count)]
        half = [join_slots(half, ratio, tuple(i * EDGE for i in range(5)))]
        base = me // half_count * (SLOTS // 2)
    return place(base.astype(jnp.int32).reshape(1), join_slots(result, ratio, (0, INNER)), half)


def solution(mesh):
    return jax.shard_map(
        on_device,
        mesh=mesh,
        in_specs=(
            P(AXES, None),
            P(),
            P(),
            P(AXES),
            P(AXES),
            P(AXES),
            P(),
        ),
        out_specs=P(AXES, None),
        check_vma=False,
    )
```

```python
import functools

import jax
import jax.numpy as jnp
from jax import lax
from jax.experimental import pallas as pl
from jax.experimental.pallas import tpu as pltpu
from jax.sharding import PartitionSpec as P

SIDE = 32
PLANE = SIDE * SIDE
NC = SIDE * PLANE
BLOCK = 64
NB = NC // BLOCK
GROUP = 64
TAPS = 16
MEMBERS = 4
LMIN = 256
LMAX = 384
FOLD = (NB - LMAX) * BLOCK
MID = NC - 2 * FOLD
SLOTS = 32
ROWS = 16
TILE = 256
EDGE = FOLD // SLOTS
INNER = MID // SLOTS
EDGE_SLOTS = PLANE // EDGE
INNER_SLOTS = PLANE // INNER
STEP = 16
CUTS = (0, 5, 11, 14, 16)
AXES = ("grid", "rep")
MIB = 1024 * 1024
VMEM = 24 * MIB


def to_column(row, size):
    eye = lax.broadcasted_iota(jnp.int32, (size, size), 0) == lax.broadcasted_iota(
        jnp.int32, (size, size), 1
    )
    return jnp.sum(jnp.where(eye, jnp.broadcast_to(row, (size, size)), 0), axis=1, keepdims=True)


def tap_rows(taps, outer, shift, inner_first):
    size = outer if inner_first else TILE // outer
    row = lax.broadcasted_iota(jnp.int32, (size, TILE), 0)
    col = lax.broadcasted_iota(jnp.int32, (size, TILE), 1)
    col = col // (TILE // outer) if inner_first else col % (TILE // outer)
    distance = shift + row - col + TAPS // 2
    total = jnp.zeros(distance.shape, jnp.float32)
    for t in range(TAPS):
        total = jnp.where(distance == t, taps[t], total)
    return total


def spread_outer(rows, outer):
    inner = TILE // outer
    row = lax.broadcasted_iota(jnp.int32, (inner, TILE), 0)
    same = row == lax.broadcasted_iota(jnp.int32, (inner, TILE), 1) % inner
    return jnp.concatenate(
        [jnp.where(same, jnp.broadcast_to(rows[a : a + 1], (inner, TILE)), 0.0) for a in range(outer)], axis=0
    )


def spread_inner(rows, outer):
    inner = TILE // outer
    block = lax.broadcasted_iota(jnp.int32, (inner, TILE), 1) // inner
    return jnp.concatenate([jnp.where(block == a, rows, 0.0) for a in range(outer)], axis=0)


def refine_kernel(
    taps_ref, functions_ref, potential_ref, energies_ref, start_ref, length_ref, out_ref,
    plane_ref, line_ref, slabs_ref, rows_ref, ends_ref,
):
    count = energies_ref.shape[1]

    @pl.when(pl.program_id(0) == 0)
    def _():
        taps = taps_ref[...].astype(jnp.float32)
        taps = [taps[:, t : t + 1] for t in range(TAPS)]
        outer = TILE // SIDE
        lines = []
        for j in range(3):
            part = spread_outer(tap_rows(taps, outer, (j - 1) * outer, True), outer)
            if j == 1:
                part = part + spread_inner(tap_rows(taps, outer, 0, False), outer)
            plane_ref[j * TILE : (j + 1) * TILE, :] = part.astype(jnp.bfloat16)
            flipped = [taps[TAPS - 1 - t] for t in range(TAPS)]
            rows = tap_rows(flipped, TILE // ROWS, (1 - j) * (TILE // ROWS) - 1, True)
            lines.append(spread_outer(rows, TILE // ROWS).astype(jnp.bfloat16))
        for h in range(SIDE * ROWS // TILE):
            for i in range(SIDE * ROWS // TILE):
                line_ref[h * TILE : (h + 1) * TILE, i * TILE : (i + 1) * TILE] = lines[i - h + 1]
        wide = (count, 2 * BLOCK)
        energy = to_column(energies_ref[...], count)
        first = to_column(start_ref[...], count)
        rows_ref[0] = jnp.broadcast_to(energy, wide)
        rows_ref[1] = jnp.broadcast_to(0.3 / (1.0 - energy), wide)
        ends_ref[0] = jnp.broadcast_to(first, wide)
        ends_ref[1] = jnp.broadcast_to(first + to_column(length_ref[...], count), wide)

    for x in range(SIDE):
        slabs_ref[x * ROWS : (x + 1) * ROWS, :] = functions_ref[:, x * PLANE : (x + 1) * PLANE]
    here = pl.ds(pl.multiple_of(pl.program_id(0) * ROWS, ROWS), ROWS)

    def widen(value):
        return jnp.concatenate([value] * (TILE // (2 * BLOCK)), axis=1)

    energy, scale = widen(rows_ref[0, here, :]), widen(rows_ref[1, here, :])
    lane_block = lax.broadcasted_iota(jnp.int32, (ROWS, TILE), 1) // BLOCK
    first = widen(ends_ref[0, here, :]) - lane_block
    last = widen(ends_ref[1, here, :]) - lane_block
    blocks = PLANE // TILE
    near, far = FOLD // PLANE, (NC - FOLD) // PLANE
    for j in range(blocks):
        cols = slice(j * TILE, (j + 1) * TILE)
        low, high = max(0, j - 1), min(blocks, j + 2)
        total = jnp.dot(
            slabs_ref[:, low * TILE : high * TILE],
            plane_ref[(low - j + 1) * TILE : (high - j + 1) * TILE, :],
            preferred_element_type=jnp.float32,
        ) + jnp.dot(line_ref[...], slabs_ref[:, cols], preferred_element_type=jnp.float32)

        def gradient_parts(x):
            rows = slice(x * ROWS, (x + 1) * ROWS)
            place = potential_ref[0:1, x * PLANE + j * TILE : x * PLANE + (j + 1) * TILE]
            place = jnp.broadcast_to(place, (ROWS, TILE))
            return total[rows], place, slabs_ref[rows, cols].astype(jnp.float32)

        for x in range(far):
            block = (x * PLANE + j * TILE) // BLOCK
            parts = gradient_parts(x)
            inside = None
            if x < near:
                starts = first <= block
                inside = starts | (last > block + (NC - FOLD) // BLOCK)
                parts = [
                    jnp.where(starts, one, other)
                    for one, other in zip(parts, gradient_parts(x + far))
                ]
                column = x * PLANE + j * TILE
                slot, place = column // EDGE, column % EDGE
            else:
                if block + TILE // BLOCK > LMIN:
                    inside = last > block
                column = (x - near) * PLANE + j * TILE
                slot, place = column // INNER, EDGE + column % INNER
            kinetic, potential, value = parts
            value = value - scale * (kinetic + (potential - energy) * value)
            if inside is not None:
                value = jnp.where(inside, value, 0.0)
            out_ref[slot, :, place : place + TILE] = value.astype(jnp.bfloat16)


def refine(taps, functions, potential, energies, start, length):
    count = functions.shape[0]
    steps = count // ROWS
    width = EDGE + INNER
    row = pl.BlockSpec((1, count), lambda i: (0, 0))
    return pl.pallas_call(
        refine_kernel,
        grid=(steps,),
        in_specs=[
            pl.BlockSpec((1, TAPS), lambda i: (0, 0)),
            pl.BlockSpec((ROWS, NC), lambda i: (i, 0)),
            pl.BlockSpec((1, NC), lambda i: (0, 0)),
            row,
            row,
            row,
        ],
        out_specs=pl.BlockSpec((SLOTS, ROWS, width), lambda i: (0, i, 0)),
        out_shape=jax.ShapeDtypeStruct((SLOTS, count, width), jnp.bfloat16),
        scratch_shapes=[
            pltpu.VMEM((3 * TILE, TILE), jnp.bfloat16),
            pltpu.VMEM((SIDE * ROWS, SIDE * ROWS), jnp.bfloat16),
            pltpu.VMEM((SIDE * ROWS, PLANE), jnp.bfloat16),
            pltpu.VMEM((2, count, 2 * BLOCK), jnp.float32),
            pltpu.VMEM((2, count, 2 * BLOCK), jnp.int32),
        ],
        compiler_params=pltpu.CompilerParams(vmem_limit_bytes=60 * MIB),
        cost_estimate=pl.CostEstimate(
            flops=steps * 36 * 2 * TILE**3, bytes_accessed=count * NC * 3, transcendentals=0
        ),
        name="refine",
    )(
        taps.reshape(1, TAPS),
        functions,
        potential.reshape(1, NC),
        energies.reshape(1, count),
        start.reshape(1, count),
        length.reshape(1, count),
    )


class Order:
    def __init__(self):
        self.grid, self.rep = lax.axis_size("grid"), lax.axis_size("rep")
        self.devices = self.grid * self.rep
        self.far, self.near = self.grid // 2, self.rep

    def place(self, device):
        grid, rep = device // self.rep, device % self.rep
        return ((rep % 2 * (self.rep // 2) + rep // 2) * 2 + grid % 2) * self.far + grid // 2

    def device(self, place):
        high, low = place // self.far, place % self.far
        rep = high // 2 % (self.rep // 2) * 2 + high // 2 // (self.rep // 2)
        return (low * 2 + high % 2) * self.rep + rep

    def send(self, block, apart):
        pairs = [(i, self.device(self.place(i) ^ apart)) for i in range(self.devices)]
        return lax.ppermute(block, AXES, pairs)

    def send_device(self, block, apart):
        return self.send(block, self.place(apart))

    def exchange_half(self, mine, theirs):
        theirs = self.send_device(theirs, 1)
        pairs = [jnp.stack([mine[i], theirs[i]]) for i in range(mine.shape[0])]
        return pairs[:1] + [self.send_device(pairs[i], 2 * i) for i in range(1, len(pairs))]

    def gather(self, blocks):
        blocks = jnp.stack([blocks, self.send(blocks, self.devices // 2)])
        sent = [self.send(blocks, i * self.far) for i in range(1, self.near)]
        blocks = jnp.stack([blocks] + sent, axis=1)
        sent = [self.send(blocks, i) for i in range(1, self.far)]
        blocks = jnp.stack([blocks] + sent, axis=2)
        return blocks.reshape(self.devices, *blocks.shape[4:])


def members_of(partners_ref, blocks_ref, g, low=0):
    return jnp.concatenate(
        [blocks_ref[g, :, low:]]
        + [blocks_ref[partners_ref[g, k], :, low:] for k in range(MEMBERS - 1)],
        axis=0,
    )


def unfold(order, start_ref, info_ref, which, folded, g, edge_ref):
    width = folded.shape[1]
    column = info_ref[which] + lax.broadcasted_iota(jnp.int32, (GROUP, width), 1)
    first = to_column(start_ref[order.place(g) ^ info_ref[0]], GROUP)
    near = jnp.broadcast_to(first, (GROUP, width)) <= column // BLOCK
    both = folded.astype(jnp.float32)
    edge_ref[g, :, :width] = jnp.where(near, both, 0.0).astype(jnp.bfloat16)
    edge_ref[g, :, width:] = jnp.where(near, 0.0, both).astype(jnp.bfloat16)


def gram_kernel(
    order, partners_ref, info_ref, start_ref, folded_ref, edge_ref, keep_ref, send_ref
):
    groups = folded_ref.shape[0]
    fold = edge_ref.shape[2] // 2

    def open_up(g, carry):
        unfold(order, start_ref, info_ref, 1, folded_ref[g, :, :fold], g, edge_ref)
        return carry

    lax.fori_loop(0, groups, open_up, 0, unroll=4)

    def step(i, carry):
        for part, out_ref in enumerate((keep_ref, send_ref)):
            g = order.device((i + part * (groups // 2)) ^ info_ref[0])
            total = 0.0
            for ref, low in ((edge_ref, 0), (folded_ref, fold)):
                total = total + lax.dot_general(
                    ref[g, :, low:], members_of(partners_ref, ref, g, low),
                    (((1,), (1,)), ((), ())), preferred_element_type=jnp.float32,
                )
            out_ref[i] = total.astype(jnp.bfloat16)
        return carry

    lax.fori_loop(0, groups // 2, step, 0, unroll=4)


def gram(order, partners, info, start, folded):
    groups, _, width = folded.shape
    fold = FOLD // order.devices
    half = jax.ShapeDtypeStruct((groups // 2, GROUP, MEMBERS * GROUP), jnp.bfloat16)
    return pl.pallas_call(
        functools.partial(gram_kernel, order),
        in_specs=[pl.BlockSpec(memory_space=pltpu.SMEM)] * 2
        + [pl.BlockSpec(memory_space=pltpu.VMEM)] * 2,
        out_specs=[pl.BlockSpec(memory_space=pltpu.VMEM)] * 3,
        out_shape=[jax.ShapeDtypeStruct((groups, GROUP, 2 * fold), jnp.bfloat16), half, half],
        compiler_params=pltpu.CompilerParams(vmem_limit_bytes=VMEM),
        cost_estimate=pl.CostEstimate(
            flops=groups * 2 * GROUP * GROUP * MEMBERS * (width + fold),
            bytes_accessed=groups * GROUP * width * 4,
            transcendentals=0,
        ),
        name="gram",
    )(partners, info, start, folded)


def add_kernel(count, pieces, *refs):
    outs = refs[count:]
    each = refs[0].shape[0] // pieces
    for o in range(pieces):
        total = refs[0][o * each : (o + 1) * each].astype(jnp.float32)
        for i in range(1, count):
            total = total + refs[i][o * each : (o + 1) * each].astype(jnp.float32)
        outs[o][...] = total.astype(jnp.bfloat16)


def add(arrays, pieces):
    shape = arrays[0].shape
    out = jax.ShapeDtypeStruct((shape[0] // pieces, *shape[1:]), jnp.bfloat16)
    return pl.pallas_call(
        functools.partial(add_kernel, len(arrays), pieces),
        out_shape=[out] * pieces,
        compiler_params=pltpu.CompilerParams(vmem_limit_bytes=VMEM),
        name="add",
    )(*arrays)


def couple_kernel(*refs):
    out_ref = refs[-1]
    total = refs[0][0].astype(jnp.float32)
    for ref in refs[1:-1]:
        total = total + ref[0].astype(jnp.float32)
    row = lax.broadcasted_iota(jnp.int32, total.shape, 0)
    col = lax.broadcasted_iota(jnp.int32, total.shape, 1)
    unit = jnp.where(row == col, 1.0, 0.0)
    out_ref[0] = (0.5 * (total * (1.0 / (BLOCK * LMAX)) - unit)).astype(jnp.bfloat16)


def couple(parts):
    return pl.pallas_call(
        couple_kernel,
        out_shape=jax.ShapeDtypeStruct(parts[0].shape, jnp.bfloat16),
        compiler_params=pltpu.CompilerParams(vmem_limit_bytes=VMEM),
        name="couple",
    )(*parts)


def corrected(partners_ref, coupling, blocks_ref, g, low=0):
    shifted = jnp.dot(
        coupling, members_of(partners_ref, blocks_ref, g, low),
        preferred_element_type=jnp.float32,
    )
    return (blocks_ref[g, :, low:].astype(jnp.float32) - shifted).astype(jnp.bfloat16)


def correct_kernel(
    order, low, partners_ref, info_ref, held_ref, other_ref, whole_ref, out_ref
):
    half = held_ref.shape[0]
    for i in range(STEP):
        g = pl.program_id(0) * STEP + i
        apart = order.place(g) ^ info_ref[0]
        near = jnp.broadcast_to(apart, (GROUP, MEMBERS * GROUP)) < half
        coupling = jnp.where(
            near,
            held_ref[apart % half].astype(jnp.float32),
            other_ref[apart % half].astype(jnp.float32),
        ).astype(jnp.bfloat16)
        out_ref[i] = corrected(partners_ref, coupling, whole_ref, g, low)


def correct(order, low, partners, info, held, other, whole):
    groups, _, width = whole.shape
    width = width - low
    return pl.pallas_call(
        functools.partial(correct_kernel, order, low),
        grid=(groups // STEP,),
        in_specs=[pl.BlockSpec(memory_space=pltpu.SMEM)] * 2
        + [pl.BlockSpec(memory_space=pltpu.VMEM)] * 3,
        out_specs=pl.BlockSpec((STEP, GROUP, width), lambda g: (g, 0, 0)),
        out_shape=jax.ShapeDtypeStruct((groups, GROUP, width), jnp.bfloat16),
        compiler_params=pltpu.CompilerParams(vmem_limit_bytes=VMEM),
        cost_estimate=pl.CostEstimate(
            flops=groups * 2 * GROUP * GROUP * MEMBERS * width,
            bytes_accessed=groups * GROUP * width * 4,
            transcendentals=0,
        ),
        name="correct",
    )(partners, info, held, other, whole)


def correct_half_kernel(
    order, count, partners_ref, info_ref, start_ref, held_ref, other_ref, edge_ref, *refs
):
    *folded_refs, mine_ref, theirs_ref, filled_ref = refs
    me, half = info_ref[3], order.devices // 2
    apart = 0
    for ref in folded_refs[:count]:
        for i in range(ref.shape[0]):
            unfold(order, start_ref, info_ref, 2, ref[i], me ^ apart, filled_ref)
            apart += 1
    begin = (me // half ^ 1) * half
    for ref in folded_refs[count:]:
        for i in range(ref.shape[0]):
            unfold(order, start_ref, info_ref, 2, ref[i], begin + i, filled_ref)
        begin += ref.shape[0]
    width = edge_ref.shape[2] // 2
    for apart in range(half):
        g = me ^ apart
        at = order.place(apart)
        coupling = (held_ref if at < half else other_ref)[at % half]
        out_ref = theirs_ref if apart % 2 else mine_ref
        for part, ref in enumerate((edge_ref, filled_ref)):
            result = corrected(partners_ref, coupling, ref, g)
            for side in range(2):
                low = (2 * side + part) * width
                out_ref[apart // 2, :, low : low + width] = result[:, side * width : (side + 1) * width]


def correct_half(order, partners, info, starts, held, other, edge, local, across):
    low = edge.shape[2]
    count = order.devices // 2
    shape = jax.ShapeDtypeStruct((count // 2, GROUP, 2 * low), jnp.bfloat16)
    folded = [*local, *across]
    return pl.pallas_call(
        functools.partial(correct_half_kernel, order, len(local)),
        in_specs=[pl.BlockSpec(memory_space=pltpu.SMEM)] * 2
        + [pl.BlockSpec(memory_space=pltpu.VMEM)] * (4 + len(folded)),
        out_specs=[pl.BlockSpec(memory_space=pltpu.VMEM)] * 2,
        out_shape=[shape] * 2,
        scratch_shapes=[pltpu.VMEM(edge.shape, jnp.bfloat16)],
        compiler_params=pltpu.CompilerParams(vmem_limit_bytes=60 * MIB),
        cost_estimate=pl.CostEstimate(
            flops=count * 4 * GROUP * GROUP * MEMBERS * low,
            bytes_accessed=count * GROUP * low * 12,
            transcendentals=0,
        ),
        name="correct_half",
    )(partners, info, starts, held, other, edge, *folded)


def place_inner_kernel(in_ref, out_ref):
    for s in range(in_ref.shape[0]):
        out_ref[:, s * INNER : (s + 1) * INNER] = in_ref[s]


def place_inner(pieces):
    _, count, width = pieces.shape
    return pl.pallas_call(
        place_inner_kernel,
        grid=(count // ROWS, MID // FOLD),
        in_specs=[pl.BlockSpec((FOLD // INNER, ROWS, width), lambda i, j: (j, i, 0))],
        out_specs=pl.BlockSpec((ROWS, FOLD), lambda i, j: (i, j + 1)),
        out_shape=jax.ShapeDtypeStruct((count, NC), jnp.bfloat16),
        compiler_params=pltpu.CompilerParams(vmem_limit_bytes=VMEM),
        cost_estimate=pl.CostEstimate(flops=0, bytes_accessed=count * MID * 4, transcendentals=0),
        name="place_inner",
    )(pieces)


def place_edge_kernel(base_ref, _, *refs):
    out_ref = refs[-1]
    apart = 0
    for piece_ref in refs[:-1]:
        for i in range(piece_ref.shape[0]):
            slot = base_ref[0] ^ apart
            apart += 1
            for part, s in enumerate((slot, slot ^ (SLOTS // 2))):
                at = pl.multiple_of(s * EDGE, EDGE)
                out_ref[:, pl.ds(at, EDGE)] = piece_ref[i, :, part * EDGE : (part + 1) * EDGE]


def place_edge(base, result, half):
    count = result.shape[0]
    return pl.pallas_call(
        place_edge_kernel,
        grid=(2,),
        in_specs=[pl.BlockSpec(memory_space=pltpu.SMEM), pl.BlockSpec(memory_space=pl.ANY)]
        + [pl.BlockSpec((b.shape[0], count, 2 * EDGE), lambda i: (0, 0, i)) for b in half],
        out_specs=pl.BlockSpec((count, FOLD), lambda i: (0, i * (NC // FOLD - 1))),
        out_shape=jax.ShapeDtypeStruct(result.shape, jnp.bfloat16),
        input_output_aliases={1: 0},
        compiler_params=pltpu.CompilerParams(vmem_limit_bytes=60 * MIB),
        cost_estimate=pl.CostEstimate(flops=0, bytes_accessed=count * FOLD * 8, transcendentals=0),
        name="place_edge",
    )(base, result, *half)


def split_slots(pieces, ratio, bounds):
    if ratio == 1:
        return pieces
    slots, rows, _ = pieces.shape
    parts = []
    for low, high in zip(bounds[:-1], bounds[1:]):
        part = pieces[:, :, low:high].reshape(slots, rows, ratio, (high - low) // ratio)
        parts.append(part.transpose(0, 2, 1, 3).reshape(slots * ratio, rows, -1))
    return jnp.concatenate(parts, axis=2)


def join_slots(pieces, ratio, bounds):
    if ratio == 1:
        return pieces
    count, rows, _ = pieces.shape
    parts = []
    for low, high in zip(bounds[:-1], bounds[1:]):
        part = pieces[:, :, low // ratio : high // ratio]
        part = part.reshape(count // ratio, ratio, rows, (high - low) // ratio)
        parts.append(part.transpose(0, 2, 1, 3).reshape(count // ratio, rows, high - low))
    return jnp.concatenate(parts, axis=2)


def exchange(pieces):
    return lax.all_to_all(pieces, AXES, split_axis=0, concat_axis=0, tiled=True)


def on_device(
    functions, filter_taps, potential, energies, region_start, region_length, partner_groups
):
    order = Order()
    ratio = order.devices // SLOTS
    me = lax.axis_index(AXES)
    half_count = order.devices // 2
    fold = FOLD // order.devices
    info = jnp.stack([order.place(me), me * fold, (me ^ half_count) * fold, me]).astype(jnp.int32)

    pieces = refine(
        filter_taps, functions, potential, energies, region_start, region_length
    )
    pieces = split_slots(pieces, ratio, (0, EDGE, EDGE + INNER))
    folded = exchange(pieces)
    starts = order.gather(region_start.reshape(1, 1, GROUP))
    to = me ^ half_count ^ jnp.arange(half_count)
    mine, theirs = [jnp.take(pieces[:, :, :fold], to[i::2], axis=0) for i in range(2)]
    local = order.exchange_half(mine, theirs)

    barrier = lax.optimization_barrier

    def across(block):
        return order.send_device(block, half_count)

    folded, *local = barrier((folded, *local))
    begin = me // half_count * half_count
    cuts = [cut * ratio for cut in CUTS]
    filled = [
        lax.dynamic_slice(folded, (begin + low, 0, 0), (high - low, GROUP, fold))
        for low, high in zip(cuts[:-1], cuts[1:])
    ]
    folded, *filled = barrier((folded, *filled))
    filled[0] = across(filled[0])
    edge, keep, send = gram(order, partner_groups, info, starts, folded)
    keep, send, filled[0] = barrier((keep, send, filled[0]))
    filled[1] = across(filled[1])
    pieces = add([keep, order.send(send, order.devices // 2)], order.near)
    arrived = [order.send(pieces[i], i * order.far) for i in range(1, order.near)]
    pieces = add([pieces[0]] + arrived, order.far)
    *pieces, filled[1] = barrier((*pieces, filled[1]))
    arrived = [order.send(pieces[i], i) for i in range(1, order.far)]
    coupling = couple([pieces[0]] + arrived)
    held = jnp.concatenate([coupling] + [order.send(coupling, i) for i in range(1, order.far)], 0)
    held, filled[2] = barrier((held, filled[2]))
    filled[2] = across(filled[2])
    held = jnp.concatenate([held] + [order.send(held, i * order.far) for i in range(1, order.near)], 0)
    held, filled[2], filled[3] = barrier((held, filled[2], filled[3]))
    filled[3] = across(filled[3])
    other = order.send(held, order.devices // 2)

    result = correct(order, fold, partner_groups, info, held, other, folded)
    result, *filled = barrier((result, *filled))
    mine, theirs = correct_half(
        order, partner_groups, info, starts, held, other, edge, local, filled
    )
    result = exchange(result)
    half = order.exchange_half(mine, theirs)
    base = me
    if ratio > 1:
        half = jnp.concatenate(half, 0)[me % half_count ^ jnp.arange(half_count)]
        half = [join_slots(half, ratio, tuple(i * EDGE for i in range(5)))]
        base = me // half_count * (SLOTS // 2)
    result = place_inner(join_slots(result, ratio, (0, INNER)))
    return place_edge(base.astype(jnp.int32).reshape(1), result, half)


def solution(mesh):
    return jax.shard_map(
        on_device,
        mesh=mesh,
        in_specs=(
            P(AXES, None),
            P(),
            P(),
            P(AXES),
            P(AXES),
            P(AXES),
            P(),
        ),
        out_specs=P(AXES, None),
        check_vma=False,
    )
```

```python
import functools

import jax
import jax.numpy as jnp
from jax import lax
from jax.experimental import pallas as pl
from jax.experimental.pallas import tpu as pltpu
from jax.sharding import PartitionSpec as P

SIDE = 32
PLANE = SIDE * SIDE
NC = SIDE * PLANE
BLOCK = 64
NB = NC // BLOCK
GROUP = 64
TAPS = 16
MEMBERS = 4
LMIN = 256
LMAX = 384
FOLD = (NB - LMAX) * BLOCK
MID = NC - 2 * FOLD
SLOTS = 32
ROWS = 16
TILE = 256
EDGE = FOLD // SLOTS
INNER = MID // SLOTS
EDGE_SLOTS = PLANE // EDGE
INNER_SLOTS = PLANE // INNER
STEP = 16
CUTS = (0, 5, 11, 14, 16)
AXES = ("grid", "rep")
MIB = 1024 * 1024
VMEM = 24 * MIB


def to_column(row, size):
    eye = lax.broadcasted_iota(jnp.int32, (size, size), 0) == lax.broadcasted_iota(
        jnp.int32, (size, size), 1
    )
    return jnp.sum(jnp.where(eye, jnp.broadcast_to(row, (size, size)), 0), axis=1, keepdims=True)


def tap_rows(taps, outer, shift, inner_first):
    size = outer if inner_first else TILE // outer
    row = lax.broadcasted_iota(jnp.int32, (size, TILE), 0)
    col = lax.broadcasted_iota(jnp.int32, (size, TILE), 1)
    col = col // (TILE // outer) if inner_first else col % (TILE // outer)
    distance = shift + row - col + TAPS // 2
    total = jnp.zeros(distance.shape, jnp.float32)
    for t in range(TAPS):
        total = jnp.where(distance == t, taps[t], total)
    return total


def spread_outer(rows, outer):
    inner = TILE // outer
    row = lax.broadcasted_iota(jnp.int32, (inner, TILE), 0)
    same = row == lax.broadcasted_iota(jnp.int32, (inner, TILE), 1) % inner
    return jnp.concatenate(
        [jnp.where(same, jnp.broadcast_to(rows[a : a + 1], (inner, TILE)), 0.0) for a in range(outer)], axis=0
    )


def spread_inner(rows, outer):
    inner = TILE // outer
    block = lax.broadcasted_iota(jnp.int32, (inner, TILE), 1) // inner
    return jnp.concatenate([jnp.where(block == a, rows, 0.0) for a in range(outer)], axis=0)


def refine_kernel(
    taps_ref, functions_ref, potential_ref, energies_ref, start_ref, length_ref, out_ref,
    plane_ref, line_ref, slabs_ref, rows_ref, ends_ref,
):
    count = energies_ref.shape[1]

    @pl.when(pl.program_id(0) == 0)
    def _():
        taps = taps_ref[...].astype(jnp.float32)
        taps = [taps[:, t : t + 1] for t in range(TAPS)]
        outer = TILE // SIDE
        lines = []
        for j in range(3):
            part = spread_outer(tap_rows(taps, outer, (j - 1) * outer, True), outer)
            if j == 1:
                part = part + spread_inner(tap_rows(taps, outer, 0, False), outer)
            plane_ref[j * TILE : (j + 1) * TILE, :] = part.astype(jnp.bfloat16)
            flipped = [taps[TAPS - 1 - t] for t in range(TAPS)]
            rows = tap_rows(flipped, TILE // ROWS, (1 - j) * (TILE // ROWS) - 1, True)
            lines.append(spread_outer(rows, TILE // ROWS).astype(jnp.bfloat16))
        for h in range(SIDE * ROWS // TILE):
            for i in range(SIDE * ROWS // TILE):
                line_ref[h * TILE : (h + 1) * TILE, i * TILE : (i + 1) * TILE] = lines[i - h + 1]
        wide = (count, 2 * BLOCK)
        energy = to_column(energies_ref[...], count)
        first = to_column(start_ref[...], count)
        rows_ref[0] = jnp.broadcast_to(energy, wide)
        rows_ref[1] = jnp.broadcast_to(0.3 / (1.0 - energy), wide)
        ends_ref[0] = jnp.broadcast_to(first, wide)
        ends_ref[1] = jnp.broadcast_to(first + to_column(length_ref[...], count), wide)

    for x in range(SIDE):
        slabs_ref[x * ROWS : (x + 1) * ROWS, :] = functions_ref[:, x * PLANE : (x + 1) * PLANE]
    here = pl.ds(pl.multiple_of(pl.program_id(0) * ROWS, ROWS), ROWS)

    def widen(value):
        return jnp.concatenate([value] * (TILE // (2 * BLOCK)), axis=1)

    energy, scale = widen(rows_ref[0, here, :]), widen(rows_ref[1, here, :])
    lane_block = lax.broadcasted_iota(jnp.int32, (ROWS, TILE), 1) // BLOCK
    first = widen(ends_ref[0, here, :]) - lane_block
    last = widen(ends_ref[1, here, :]) - lane_block
    blocks = PLANE // TILE
    near, far = FOLD // PLANE, (NC - FOLD) // PLANE
    for j in range(blocks):
        cols = slice(j * TILE, (j + 1) * TILE)
        low, high = max(0, j - 1), min(blocks, j + 2)
        total = jnp.dot(
            slabs_ref[:, low * TILE : high * TILE],
            plane_ref[(low - j + 1) * TILE : (high - j + 1) * TILE, :],
            preferred_element_type=jnp.float32,
        ) + jnp.dot(line_ref[...], slabs_ref[:, cols], preferred_element_type=jnp.float32)

        def gradient_parts(x):
            rows = slice(x * ROWS, (x + 1) * ROWS)
            place = potential_ref[0:1, x * PLANE + j * TILE : x * PLANE + (j + 1) * TILE]
            place = jnp.broadcast_to(place, (ROWS, TILE))
            return total[rows], place, slabs_ref[rows, cols].astype(jnp.float32)

        for x in range(far):
            block = (x * PLANE + j * TILE) // BLOCK
            parts = gradient_parts(x)
            inside = None
            if x < near:
                starts = first <= block
                inside = starts | (last > block + (NC - FOLD) // BLOCK)
                parts = [
                    jnp.where(starts, one, other)
                    for one, other in zip(parts, gradient_parts(x + far))
                ]
                column = x * PLANE + j * TILE
                slot, place = column // EDGE, column % EDGE
            else:
                if block + TILE // BLOCK > LMIN:
                    inside = last > block
                column = (x - near) * PLANE + j * TILE
                slot, place = column // INNER, EDGE + column % INNER
            kinetic, potential, value = parts
            value = value - scale * (kinetic + (potential - energy) * value)
            if inside is not None:
                value = jnp.where(inside, value, 0.0)
            out_ref[slot, :, place : place + TILE] = value.astype(jnp.bfloat16)


def refine(taps, functions, potential, energies, start, length):
    count = functions.shape[0]
    steps = count // ROWS
    width = EDGE + INNER
    row = pl.BlockSpec((1, count), lambda i: (0, 0))
    return pl.pallas_call(
        refine_kernel,
        grid=(steps,),
        in_specs=[
            pl.BlockSpec((1, TAPS), lambda i: (0, 0)),
            pl.BlockSpec((ROWS, NC), lambda i: (i, 0)),
            pl.BlockSpec((1, NC), lambda i: (0, 0)),
            row,
            row,
            row,
        ],
        out_specs=pl.BlockSpec((SLOTS, ROWS, width), lambda i: (0, i, 0)),
        out_shape=jax.ShapeDtypeStruct((SLOTS, count, width), jnp.bfloat16),
        scratch_shapes=[
            pltpu.VMEM((3 * TILE, TILE), jnp.bfloat16),
            pltpu.VMEM((SIDE * ROWS, SIDE * ROWS), jnp.bfloat16),
            pltpu.VMEM((SIDE * ROWS, PLANE), jnp.bfloat16),
            pltpu.VMEM((2, count, 2 * BLOCK), jnp.float32),
            pltpu.VMEM((2, count, 2 * BLOCK), jnp.int32),
        ],
        compiler_params=pltpu.CompilerParams(vmem_limit_bytes=60 * MIB),
        cost_estimate=pl.CostEstimate(
            flops=steps * 36 * 2 * TILE**3, bytes_accessed=count * NC * 3, transcendentals=0
        ),
        name="refine",
    )(
        taps.reshape(1, TAPS),
        functions,
        potential.reshape(1, NC),
        energies.reshape(1, count),
        start.reshape(1, count),
        length.reshape(1, count),
    )


class Order:
    def __init__(self):
        self.grid, self.rep = lax.axis_size("grid"), lax.axis_size("rep")
        self.devices = self.grid * self.rep
        self.far, self.near = self.grid // 2, self.rep

    def place(self, device):
        grid, rep = device // self.rep, device % self.rep
        return ((rep % 2 * (self.rep // 2) + rep // 2) * 2 + grid % 2) * self.far + grid // 2

    def device(self, place):
        high, low = place // self.far, place % self.far
        rep = high // 2 % (self.rep // 2) * 2 + high // 2 // (self.rep // 2)
        return (low * 2 + high % 2) * self.rep + rep

    def send(self, block, apart):
        pairs = [(i, self.device(self.place(i) ^ apart)) for i in range(self.devices)]
        return lax.ppermute(block, AXES, pairs)

    def send_device(self, block, apart):
        return self.send(block, self.place(apart))

    def exchange_half(self, mine, theirs):
        theirs = self.send_device(theirs, 1)
        pairs = [jnp.stack([mine[i], theirs[i]]) for i in range(mine.shape[0])]
        return pairs[:1] + [self.send_device(pairs[i], 2 * i) for i in range(1, len(pairs))]

    def gather(self, blocks):
        blocks = jnp.stack([blocks, self.send(blocks, self.devices // 2)])
        sent = [self.send(blocks, i * self.far) for i in range(1, self.near)]
        blocks = jnp.stack([blocks] + sent, axis=1)
        sent = [self.send(blocks, i) for i in range(1, self.far)]
        blocks = jnp.stack([blocks] + sent, axis=2)
        return blocks.reshape(self.devices, *blocks.shape[4:])


def partners_of(partners_ref, blocks_ref, g, low=0):
    return [blocks_ref[partners_ref[g, k], :, low:] for k in range(MEMBERS - 1)]


def open_fold(folded, first, column):
    column = column + lax.broadcasted_iota(jnp.int32, folded.shape, 1)
    near = jnp.broadcast_to(first, folded.shape) <= column // BLOCK
    both = folded.astype(jnp.float32)
    return [jnp.where(near, both, 0.0).astype(jnp.bfloat16), jnp.where(near, 0.0, both).astype(jnp.bfloat16)]


def own_gram_kernel(start_ref, pieces_ref, out_ref, start_column_ref):
    start_column_ref[...] = jnp.broadcast_to(to_column(start_ref[...], GROUP), start_column_ref.shape)

    def step(s, total):
        folded = pieces_ref[s, :, :EDGE]
        near, far = open_fold(folded, start_column_ref[:, :1], s * EDGE)
        whole = jnp.concatenate([near, far, pieces_ref[s, :, EDGE:]], axis=1)
        return total + lax.dot_general(
            whole, whole, (((1,), (1,)), ((), ())), preferred_element_type=jnp.float32
        )

    zero = jnp.zeros(out_ref.shape, jnp.float32)
    out_ref[...] = lax.fori_loop(0, pieces_ref.shape[0], step, zero, unroll=4)


def own_gram(start, pieces):
    return pl.pallas_call(
        own_gram_kernel,
        out_shape=jax.ShapeDtypeStruct((GROUP, GROUP), jnp.float32),
        scratch_shapes=[pltpu.VMEM((GROUP, 2 * BLOCK), jnp.int32)],
        compiler_params=pltpu.CompilerParams(vmem_limit_bytes=16 * MIB),
        cost_estimate=pl.CostEstimate(
            flops=2 * GROUP * GROUP * NC, bytes_accessed=GROUP * NC * 2, transcendentals=0
        ),
        name="own_gram",
    )(start.reshape(1, GROUP), pieces)


def unfold(order, start_ref, info_ref, which, folded, g, edge_ref):
    width = folded.shape[1]
    first = to_column(start_ref[order.place(g) ^ info_ref[0]], GROUP)
    near, far = open_fold(folded, first, info_ref[which])
    edge_ref[g, :, :width] = near
    edge_ref[g, :, width:] = far


def gram_kernel(
    order, partners_ref, info_ref, start_ref, folded_ref, edge_ref, keep_ref, send_ref
):
    groups = folded_ref.shape[0]
    fold = edge_ref.shape[2] // 2

    def open_up(g, carry):
        unfold(order, start_ref, info_ref, 1, folded_ref[g, :, :fold], g, edge_ref)
        return carry

    lax.fori_loop(0, groups, open_up, 0, unroll=16)

    def step(i, carry):
        for part, out_ref in enumerate((keep_ref, send_ref)):
            g = order.device((i + part * (groups // 2)) ^ info_ref[0])
            total = 0.0
            for ref, low in ((edge_ref, 0), (folded_ref, fold)):
                partners = jnp.concatenate(partners_of(partners_ref, ref, g, low), axis=0)
                total = total + lax.dot_general(
                    ref[g, :, low:], partners,
                    (((1,), (1,)), ((), ())), preferred_element_type=jnp.float32,
                )
            total = total.astype(jnp.bfloat16)
            out_ref[i, :GROUP, :] = total[:, : 2 * GROUP]
            third = total[:, 2 * GROUP :]
            out_ref[i, GROUP:, :] = jnp.concatenate(
                [third[: GROUP // 2], third[GROUP // 2 :]], axis=1
            )
        return carry

    lax.fori_loop(0, groups // 2, step, 0, unroll=16)


def gram(order, partners, info, start, folded):
    groups, _, width = folded.shape
    fold = FOLD // order.devices
    half = jax.ShapeDtypeStruct((groups // 2, GROUP + GROUP // 2, 2 * GROUP), jnp.bfloat16)
    return pl.pallas_call(
        functools.partial(gram_kernel, order),
        in_specs=[pl.BlockSpec(memory_space=pltpu.SMEM)] * 2
        + [pl.BlockSpec(memory_space=pltpu.VMEM)] * 2,
        out_specs=[pl.BlockSpec(memory_space=pltpu.VMEM)] * 3,
        out_shape=[jax.ShapeDtypeStruct((groups, GROUP, 2 * fold), jnp.bfloat16), half, half],
        compiler_params=pltpu.CompilerParams(vmem_limit_bytes=VMEM),
        cost_estimate=pl.CostEstimate(
            flops=groups * 2 * GROUP * GROUP * (MEMBERS - 1) * (width + fold),
            bytes_accessed=groups * GROUP * width * 4,
            transcendentals=0,
        ),
        name="gram",
    )(partners, info, start, folded)


def add_kernel(count, pieces, *refs):
    outs = refs[count:]
    each = refs[0].shape[0] // pieces
    for o in range(pieces):
        total = refs[0][o * each : (o + 1) * each].astype(jnp.float32)
        for i in range(1, count):
            total = total + refs[i][o * each : (o + 1) * each].astype(jnp.float32)
        outs[o][...] = total.astype(jnp.bfloat16)


def add(arrays, pieces):
    shape = arrays[0].shape
    out = jax.ShapeDtypeStruct((shape[0] // pieces, *shape[1:]), jnp.bfloat16)
    return pl.pallas_call(
        functools.partial(add_kernel, len(arrays), pieces),
        out_shape=[out] * pieces,
        compiler_params=pltpu.CompilerParams(vmem_limit_bytes=VMEM),
        name="add",
    )(*arrays)


def couple_kernel(own_ref, *refs):
    out_ref = refs[-1]
    total = refs[0][0].astype(jnp.float32)
    for ref in refs[1:-1]:
        total = total + ref[0].astype(jnp.float32)
    weight = 1.0 / (BLOCK * LMAX)
    row = lax.broadcasted_iota(jnp.int32, own_ref.shape, 0)
    unit = jnp.where(row == lax.broadcasted_iota(jnp.int32, own_ref.shape, 1), 1.0, 0.0)
    own = 0.5 * (own_ref[...] * weight - unit)
    total = 0.5 * (total * weight)
    third = total[GROUP:]
    third = jnp.concatenate([third[:, :GROUP], third[:, GROUP:]], axis=0)
    out_ref[0, :, : 2 * GROUP] = total[:GROUP].astype(jnp.bfloat16)
    out_ref[0, :, 2 * GROUP :] = jnp.concatenate([third, own], axis=1).astype(jnp.bfloat16)


def couple(own, parts):
    return pl.pallas_call(
        couple_kernel,
        out_shape=jax.ShapeDtypeStruct((1, GROUP, MEMBERS * GROUP), jnp.bfloat16),
        compiler_params=pltpu.CompilerParams(vmem_limit_bytes=VMEM),
        name="couple",
    )(own, *parts)


def corrected(partners_ref, coupling, blocks_ref, g, low=0):
    own = blocks_ref[g, :, low:]
    members = jnp.concatenate([*partners_of(partners_ref, blocks_ref, g, low), own], axis=0)
    shifted = jnp.dot(coupling, members, preferred_element_type=jnp.float32)
    return (own.astype(jnp.float32) - shifted).astype(jnp.bfloat16)


def correct_kernel(
    order, low, partners_ref, info_ref, held_ref, other_ref, whole_ref, out_ref
):
    half = held_ref.shape[0]
    for i in range(STEP):
        g = pl.program_id(0) * STEP + i
        apart = order.place(g) ^ info_ref[0]
        near = jnp.broadcast_to(apart, (GROUP, MEMBERS * GROUP)) < half
        coupling = jnp.where(
            near,
            held_ref[apart % half].astype(jnp.float32),
            other_ref[apart % half].astype(jnp.float32),
        ).astype(jnp.bfloat16)
        out_ref[i] = corrected(partners_ref, coupling, whole_ref, g, low)


def correct(order, low, partners, info, held, other, whole):
    groups, _, width = whole.shape
    width = width - low
    return pl.pallas_call(
        functools.partial(correct_kernel, order, low),
        grid=(groups // STEP,),
        in_specs=[pl.BlockSpec(memory_space=pltpu.SMEM)] * 2
        + [pl.BlockSpec(memory_space=pltpu.VMEM)] * 3,
        out_specs=pl.BlockSpec((STEP, GROUP, width), lambda g: (g, 0, 0)),
        out_shape=jax.ShapeDtypeStruct((groups, GROUP, width), jnp.bfloat16),
        compiler_params=pltpu.CompilerParams(vmem_limit_bytes=VMEM),
        cost_estimate=pl.CostEstimate(
            flops=groups * 2 * GROUP * GROUP * MEMBERS * width,
            bytes_accessed=groups * GROUP * width * 4,
            transcendentals=0,
        ),
        name="correct",
    )(partners, info, held, other, whole)


def correct_half_kernel(
    order, count, partners_ref, info_ref, start_ref, held_ref, other_ref, edge_ref, *refs
):
    *folded_refs, mine_ref, theirs_ref, filled_ref = refs
    me, half = info_ref[3], order.devices // 2
    apart = 0
    for ref in folded_refs[:count]:
        for i in range(ref.shape[0]):
            unfold(order, start_ref, info_ref, 2, ref[i], me ^ apart, filled_ref)
            apart += 1
    begin = (me // half ^ 1) * half
    for ref in folded_refs[count:]:
        for i in range(ref.shape[0]):
            unfold(order, start_ref, info_ref, 2, ref[i], begin + i, filled_ref)
        begin += ref.shape[0]
    width = edge_ref.shape[2] // 2
    for apart in range(half):
        g = me ^ apart
        at = order.place(apart)
        coupling = (held_ref if at < half else other_ref)[at % half]
        out_ref = theirs_ref if apart % 2 else mine_ref
        for part, ref in enumerate((edge_ref, filled_ref)):
            result = corrected(partners_ref, coupling, ref, g)
            for side in range(2):
                low = (2 * side + part) * width
                out_ref[apart // 2, :, low : low + width] = result[:, side * width : (side + 1) * width]


def correct_half(order, partners, info, starts, held, other, edge, local, across):
    low = edge.shape[2]
    count = order.devices // 2
    shape = jax.ShapeDtypeStruct((count // 2, GROUP, 2 * low), jnp.bfloat16)
    folded = [*local, *across]
    return pl.pallas_call(
        functools.partial(correct_half_kernel, order, len(local)),
        in_specs=[pl.BlockSpec(memory_space=pltpu.SMEM)] * 2
        + [pl.BlockSpec(memory_space=pltpu.VMEM)] * (4 + len(folded)),
        out_specs=[pl.BlockSpec(memory_space=pltpu.VMEM)] * 2,
        out_shape=[shape] * 2,
        scratch_shapes=[pltpu.VMEM(edge.shape, jnp.bfloat16)],
        compiler_params=pltpu.CompilerParams(vmem_limit_bytes=60 * MIB),
        cost_estimate=pl.CostEstimate(
            flops=count * 4 * GROUP * GROUP * MEMBERS * low,
            bytes_accessed=count * GROUP * low * 12,
            transcendentals=0,
        ),
        name="correct_half",
    )(partners, info, starts, held, other, edge, *folded)


def place_inner_kernel(in_ref, out_ref):
    for s in range(in_ref.shape[0]):
        out_ref[:, s * INNER : (s + 1) * INNER] = in_ref[s]


def place_inner(pieces):
    _, count, width = pieces.shape
    return pl.pallas_call(
        place_inner_kernel,
        grid=(count // ROWS, MID // FOLD),
        in_specs=[pl.BlockSpec((FOLD // INNER, ROWS, width), lambda i, j: (j, i, 0))],
        out_specs=pl.BlockSpec((ROWS, FOLD), lambda i, j: (i, j + 1)),
        out_shape=jax.ShapeDtypeStruct((count, NC), jnp.bfloat16),
        compiler_params=pltpu.CompilerParams(vmem_limit_bytes=VMEM),
        cost_estimate=pl.CostEstimate(flops=0, bytes_accessed=count * MID * 4, transcendentals=0),
        name="place_inner",
    )(pieces)


def place_edge_kernel(base_ref, _, *refs):
    out_ref = refs[-1]
    apart = 0
    for piece_ref in refs[:-1]:
        for i in range(piece_ref.shape[0]):
            slot = base_ref[0] ^ apart
            apart += 1
            for part, s in enumerate((slot, slot ^ (SLOTS // 2))):
                at = pl.multiple_of(s * EDGE, EDGE)
                out_ref[:, pl.ds(at, EDGE)] = piece_ref[i, :, part * EDGE : (part + 1) * EDGE]


def place_edge(base, result, half):
    count = result.shape[0]
    return pl.pallas_call(
        place_edge_kernel,
        grid=(2,),
        in_specs=[pl.BlockSpec(memory_space=pltpu.SMEM), pl.BlockSpec(memory_space=pl.ANY)]
        + [pl.BlockSpec((b.shape[0], count, 2 * EDGE), lambda i: (0, 0, i)) for b in half],
        out_specs=pl.BlockSpec((count, FOLD), lambda i: (0, i * (NC // FOLD - 1))),
        out_shape=jax.ShapeDtypeStruct(result.shape, jnp.bfloat16),
        input_output_aliases={1: 0},
        compiler_params=pltpu.CompilerParams(vmem_limit_bytes=60 * MIB),
        cost_estimate=pl.CostEstimate(flops=0, bytes_accessed=count * FOLD * 8, transcendentals=0),
        name="place_edge",
    )(base, result, *half)


def split_slots(pieces, ratio, bounds):
    if ratio == 1:
        return pieces
    slots, rows, _ = pieces.shape
    parts = []
    for low, high in zip(bounds[:-1], bounds[1:]):
        part = pieces[:, :, low:high].reshape(slots, rows, ratio, (high - low) // ratio)
        parts.append(part.transpose(0, 2, 1, 3).reshape(slots * ratio, rows, -1))
    return jnp.concatenate(parts, axis=2)


def join_slots(pieces, ratio, bounds):
    if ratio == 1:
        return pieces
    count, rows, _ = pieces.shape
    parts = []
    for low, high in zip(bounds[:-1], bounds[1:]):
        part = pieces[:, :, low // ratio : high // ratio]
        part = part.reshape(count // ratio, ratio, rows, (high - low) // ratio)
        parts.append(part.transpose(0, 2, 1, 3).reshape(count // ratio, rows, high - low))
    return jnp.concatenate(parts, axis=2)


def exchange(pieces):
    return lax.all_to_all(pieces, AXES, split_axis=0, concat_axis=0, tiled=True)


def on_device(
    functions, filter_taps, potential, energies, region_start, region_length, partner_groups
):
    order = Order()
    ratio = order.devices // SLOTS
    me = lax.axis_index(AXES)
    half_count = order.devices // 2
    fold = FOLD // order.devices
    info = jnp.stack([order.place(me), me * fold, (me ^ half_count) * fold, me]).astype(jnp.int32)

    pieces = refine(
        filter_taps, functions, potential, energies, region_start, region_length
    )
    own = own_gram(region_start, pieces)
    pieces = split_slots(pieces, ratio, (0, EDGE, EDGE + INNER))
    folded = exchange(pieces)
    starts = order.gather(region_start.reshape(1, 1, GROUP))
    to = me ^ half_count ^ jnp.arange(half_count)
    mine, theirs = [jnp.take(pieces[:, :, :fold], to[i::2], axis=0) for i in range(2)]
    local = order.exchange_half(mine, theirs)

    barrier = lax.optimization_barrier

    def across(block):
        return order.send_device(block, half_count)

    folded, own, *local = barrier((folded, own, *local))
    begin = me // half_count * half_count
    cuts = [cut * ratio for cut in CUTS]
    filled = [
        lax.dynamic_slice(folded, (begin + low, 0, 0), (high - low, GROUP, fold))
        for low, high in zip(cuts[:-1], cuts[1:])
    ]
    folded, *filled = barrier((folded, *filled))
    filled[0] = across(filled[0])
    edge, keep, send = gram(order, partner_groups, info, starts, folded)
    keep, send, filled[0] = barrier((keep, send, filled[0]))
    filled[1] = across(filled[1])
    pieces = add([keep, order.send(send, order.devices // 2)], order.near)
    arrived = [order.send(pieces[i], i * order.far) for i in range(1, order.near)]
    pieces = add([pieces[0]] + arrived, order.far)
    *pieces, filled[1] = barrier((*pieces, filled[1]))
    arrived = [order.send(pieces[i], i) for i in range(1, order.far)]
    coupling = couple(own, [pieces[0]] + arrived)
    held = jnp.concatenate([coupling] + [order.send(coupling, i) for i in range(1, order.far)], 0)
    held, filled[2] = barrier((held, filled[2]))
    filled[2] = across(filled[2])
    held = jnp.concatenate([held] + [order.send(held, i * order.far) for i in range(1, order.near)], 0)
    held, filled[2], filled[3] = barrier((held, filled[2], filled[3]))
    filled[3] = across(filled[3])
    other = order.send(held, order.devices // 2)

    result = correct(order, fold, partner_groups, info, held, other, folded)
    result, *filled = barrier((result, *filled))
    mine, theirs = correct_half(
        order, partner_groups, info, starts, held, other, edge, local, filled
    )
    result = exchange(result)
    half = order.exchange_half(mine, theirs)
    base = me
    if ratio > 1:
        half = jnp.concatenate(half, 0)[me % half_count ^ jnp.arange(half_count)]
        half = [join_slots(half, ratio, tuple(i * EDGE for i in range(5)))]
        base = me // half_count * (SLOTS // 2)
    result = place_inner(join_slots(result, ratio, (0, INNER)))
    return place_edge(base.astype(jnp.int32).reshape(1), result, half)


def solution(mesh):
    return jax.shard_map(
        on_device,
        mesh=mesh,
        in_specs=(
            P(AXES, None),
            P(),
            P(),
            P(AXES),
            P(AXES),
            P(AXES),
            P(),
        ),
        out_specs=P(AXES, None),
        check_vma=False,
    )
```

```python
import functools

import jax
import jax.numpy as jnp
from jax import lax
from jax.experimental import pallas as pl
from jax.experimental.pallas import tpu as pltpu
from jax.sharding import PartitionSpec as P

SIDE = 32
PLANE = SIDE * SIDE
NC = SIDE * PLANE
BLOCK = 64
NB = NC // BLOCK
GROUP = 64
TAPS = 16
MEMBERS = 4
LMIN = 256
LMAX = 384
FOLD = (NB - LMAX) * BLOCK
MID = NC - 2 * FOLD
SLOTS = 32
ROWS = 16
TILE = 256
EDGE = FOLD // SLOTS
INNER = MID // SLOTS
EDGE_SLOTS = PLANE // EDGE
INNER_SLOTS = PLANE // INNER
STEP = 16
CUTS = (0, 5, 11, 14, 16)
AXES = ("grid", "rep")
MIB = 1024 * 1024
VMEM = 24 * MIB


def to_column(row, size):
    eye = lax.broadcasted_iota(jnp.int32, (size, size), 0) == lax.broadcasted_iota(
        jnp.int32, (size, size), 1
    )
    return jnp.sum(jnp.where(eye, jnp.broadcast_to(row, (size, size)), 0), axis=1, keepdims=True)


def tap_rows(taps, outer, shift, inner_first):
    size = outer if inner_first else TILE // outer
    row = lax.broadcasted_iota(jnp.int32, (size, TILE), 0)
    col = lax.broadcasted_iota(jnp.int32, (size, TILE), 1)
    col = col // (TILE // outer) if inner_first else col % (TILE // outer)
    distance = shift + row - col + TAPS // 2
    total = jnp.zeros(distance.shape, jnp.float32)
    for t in range(TAPS):
        total = jnp.where(distance == t, taps[t], total)
    return total


def spread_outer(rows, outer):
    inner = TILE // outer
    row = lax.broadcasted_iota(jnp.int32, (inner, TILE), 0)
    same = row == lax.broadcasted_iota(jnp.int32, (inner, TILE), 1) % inner
    return jnp.concatenate(
        [jnp.where(same, jnp.broadcast_to(rows[a : a + 1], (inner, TILE)), 0.0) for a in range(outer)], axis=0
    )


def spread_inner(rows, outer):
    inner = TILE // outer
    block = lax.broadcasted_iota(jnp.int32, (inner, TILE), 1) // inner
    return jnp.concatenate([jnp.where(block == a, rows, 0.0) for a in range(outer)], axis=0)


def refine_kernel(
    taps_ref, functions_ref, potential_ref, energies_ref, start_ref, length_ref, out_ref,
    plane_ref, line_ref, slabs_ref, rows_ref, ends_ref,
):
    count = energies_ref.shape[1]

    @pl.when(pl.program_id(0) == 0)
    def _():
        taps = taps_ref[...].astype(jnp.float32)
        taps = [taps[:, t : t + 1] for t in range(TAPS)]
        outer = TILE // SIDE
        lines = []
        for j in range(3):
            part = spread_outer(tap_rows(taps, outer, (j - 1) * outer, True), outer)
            if j == 1:
                part = part + spread_inner(tap_rows(taps, outer, 0, False), outer)
            plane_ref[j * TILE : (j + 1) * TILE, :] = part.astype(jnp.bfloat16)
            flipped = [taps[TAPS - 1 - t] for t in range(TAPS)]
            rows = tap_rows(flipped, TILE // ROWS, (1 - j) * (TILE // ROWS) - 1, True)
            lines.append(spread_outer(rows, TILE // ROWS).astype(jnp.bfloat16))
        for h in range(SIDE * ROWS // TILE):
            for i in range(SIDE * ROWS // TILE):
                line_ref[h * TILE : (h + 1) * TILE, i * TILE : (i + 1) * TILE] = lines[i - h + 1]
        wide = (count, 2 * BLOCK)
        energy = to_column(energies_ref[...], count)
        first = to_column(start_ref[...], count)
        rows_ref[0] = jnp.broadcast_to(energy, wide)
        rows_ref[1] = jnp.broadcast_to(0.3 / (1.0 - energy), wide)
        ends_ref[0] = jnp.broadcast_to(first, wide)
        ends_ref[1] = jnp.broadcast_to(first + to_column(length_ref[...], count), wide)

    for x in range(SIDE):
        slabs_ref[x * ROWS : (x + 1) * ROWS, :] = functions_ref[:, x * PLANE : (x + 1) * PLANE]
    here = pl.ds(pl.multiple_of(pl.program_id(0) * ROWS, ROWS), ROWS)

    def widen(value):
        return jnp.concatenate([value] * (TILE // (2 * BLOCK)), axis=1)

    energy, scale = widen(rows_ref[0, here, :]), widen(rows_ref[1, here, :])
    lane_block = lax.broadcasted_iota(jnp.int32, (ROWS, TILE), 1) // BLOCK
    first = widen(ends_ref[0, here, :]) - lane_block
    last = widen(ends_ref[1, here, :]) - lane_block
    blocks = PLANE // TILE
    near, far = FOLD // PLANE, (NC - FOLD) // PLANE
    for j in range(blocks):
        cols = slice(j * TILE, (j + 1) * TILE)
        low, high = max(0, j - 1), min(blocks, j + 2)
        totals = []
        for h in range(SIDE * ROWS // TILE):
            rows = slice(h * TILE, (h + 1) * TILE)
            total = jnp.dot(
                slabs_ref[rows, low * TILE : high * TILE],
                plane_ref[(low - j + 1) * TILE : (high - j + 1) * TILE, :],
                preferred_element_type=jnp.float32,
            )
            total = total + jnp.dot(
                line_ref[rows, :], slabs_ref[:, cols], preferred_element_type=jnp.float32
            )
            totals += [total[i * ROWS : (i + 1) * ROWS] for i in range(TILE // ROWS)]

        def gradient_parts(x):
            rows = slice(x * ROWS, (x + 1) * ROWS)
            place = potential_ref[0:1, x * PLANE + j * TILE : x * PLANE + (j + 1) * TILE]
            place = jnp.broadcast_to(place, (ROWS, TILE))
            return totals[x], place, slabs_ref[rows, cols].astype(jnp.float32)

        for x in range(far):
            block = (x * PLANE + j * TILE) // BLOCK
            parts = gradient_parts(x)
            inside = None
            if x < near:
                starts = first <= block
                inside = starts | (last > block + (NC - FOLD) // BLOCK)
                parts = [
                    jnp.where(starts, one, other)
                    for one, other in zip(parts, gradient_parts(x + far))
                ]
                column = x * PLANE + j * TILE
                slot, place = column // EDGE, column % EDGE
            else:
                if block + TILE // BLOCK > LMIN:
                    inside = last > block
                column = (x - near) * PLANE + j * TILE
                slot, place = column // INNER, EDGE + column % INNER
            kinetic, potential, value = parts
            value = value - scale * (kinetic + (potential - energy) * value)
            if inside is not None:
                value = jnp.where(inside, value, 0.0)
            out_ref[slot, :, place : place + TILE] = value.astype(jnp.bfloat16)


def refine(taps, functions, potential, energies, start, length):
    count = functions.shape[0]
    steps = count // ROWS
    width = EDGE + INNER
    row = pl.BlockSpec((1, count), lambda i: (0, 0))
    return pl.pallas_call(
        refine_kernel,
        grid=(steps,),
        in_specs=[
            pl.BlockSpec((1, TAPS), lambda i: (0, 0)),
            pl.BlockSpec((ROWS, NC), lambda i: (i, 0)),
            pl.BlockSpec((1, NC), lambda i: (0, 0)),
            row,
            row,
            row,
        ],
        out_specs=pl.BlockSpec((SLOTS, ROWS, width), lambda i: (0, i, 0)),
        out_shape=jax.ShapeDtypeStruct((SLOTS, count, width), jnp.bfloat16),
        scratch_shapes=[
            pltpu.VMEM((3 * TILE, TILE), jnp.bfloat16),
            pltpu.VMEM((SIDE * ROWS, SIDE * ROWS), jnp.bfloat16),
            pltpu.VMEM((SIDE * ROWS, PLANE), jnp.bfloat16),
            pltpu.VMEM((2, count, 2 * BLOCK), jnp.float32),
            pltpu.VMEM((2, count, 2 * BLOCK), jnp.int32),
        ],
        compiler_params=pltpu.CompilerParams(vmem_limit_bytes=60 * MIB),
        cost_estimate=pl.CostEstimate(
            flops=steps * 36 * 2 * TILE**3, bytes_accessed=count * NC * 3, transcendentals=0
        ),
        name="refine",
    )(
        taps.reshape(1, TAPS),
        functions,
        potential.reshape(1, NC),
        energies.reshape(1, count),
        start.reshape(1, count),
        length.reshape(1, count),
    )


class Order:
    def __init__(self):
        self.grid, self.rep = lax.axis_size("grid"), lax.axis_size("rep")
        self.devices = self.grid * self.rep
        self.far, self.near = self.grid // 2, self.rep

    def place(self, device):
        grid, rep = device // self.rep, device % self.rep
        return ((rep % 2 * (self.rep // 2) + rep // 2) * 2 + grid % 2) * self.far + grid // 2

    def device(self, place):
        high, low = place // self.far, place % self.far
        rep = high // 2 % (self.rep // 2) * 2 + high // 2 // (self.rep // 2)
        return (low * 2 + high % 2) * self.rep + rep

    def send(self, block, apart):
        pairs = [(i, self.device(self.place(i) ^ apart)) for i in range(self.devices)]
        return lax.ppermute(block, AXES, pairs)

    def send_device(self, block, apart):
        return self.send(block, self.place(apart))

    def exchange_half(self, mine, theirs):
        theirs = self.send_device(theirs, 1)
        pairs = [jnp.stack([mine[i], theirs[i]]) for i in range(mine.shape[0])]
        return pairs[:1] + [self.send_device(pairs[i], 2 * i) for i in range(1, len(pairs))]

    def gather(self, blocks):
        blocks = jnp.stack([blocks, self.send(blocks, self.devices // 2)])
        sent = [self.send(blocks, i * self.far) for i in range(1, self.near)]
        blocks = jnp.stack([blocks] + sent, axis=1)
        sent = [self.send(blocks, i) for i in range(1, self.far)]
        blocks = jnp.stack([blocks] + sent, axis=2)
        return blocks.reshape(self.devices, *blocks.shape[4:])


def partners_of(partners_ref, blocks_ref, g, low=0):
    return [blocks_ref[partners_ref[g, k], :, low:] for k in range(MEMBERS - 1)]


def open_fold(folded, first, column):
    column = column + lax.broadcasted_iota(jnp.int32, folded.shape, 1)
    near = jnp.broadcast_to(first, folded.shape) <= column // BLOCK
    both = folded.astype(jnp.float32)
    return [jnp.where(near, both, 0.0).astype(jnp.bfloat16), jnp.where(near, 0.0, both).astype(jnp.bfloat16)]


def own_gram_kernel(start_ref, pieces_ref, out_ref, start_column_ref):
    start_column_ref[...] = jnp.broadcast_to(to_column(start_ref[...], GROUP), start_column_ref.shape)

    def step(s, total):
        folded = pieces_ref[s, :, :EDGE]
        near, far = open_fold(folded, start_column_ref[:, :1], s * EDGE)
        whole = jnp.concatenate([near, far, pieces_ref[s, :, EDGE:]], axis=1)
        return total + lax.dot_general(
            whole, whole, (((1,), (1,)), ((), ())), preferred_element_type=jnp.float32
        )

    zero = jnp.zeros(out_ref.shape, jnp.float32)
    out_ref[...] = lax.fori_loop(0, pieces_ref.shape[0], step, zero, unroll=4)


def own_gram(start, pieces):
    return pl.pallas_call(
        own_gram_kernel,
        out_shape=jax.ShapeDtypeStruct((GROUP, GROUP), jnp.float32),
        scratch_shapes=[pltpu.VMEM((GROUP, 2 * BLOCK), jnp.int32)],
        compiler_params=pltpu.CompilerParams(vmem_limit_bytes=16 * MIB),
        cost_estimate=pl.CostEstimate(
            flops=2 * GROUP * GROUP * NC, bytes_accessed=GROUP * NC * 2, transcendentals=0
        ),
        name="own_gram",
    )(start.reshape(1, GROUP), pieces)


def unfold(order, start_ref, info_ref, which, folded, g, edge_ref):
    width = folded.shape[1]
    first = to_column(start_ref[order.place(g) ^ info_ref[0]], GROUP)
    near, far = open_fold(folded, first, info_ref[which])
    edge_ref[g, :, :width] = near
    edge_ref[g, :, width:] = far


def gram_kernel(
    order, partners_ref, info_ref, start_ref, folded_ref, edge_ref, keep_ref, send_ref
):
    groups = folded_ref.shape[0]
    fold = edge_ref.shape[2] // 2

    def open_up(g, carry):
        unfold(order, start_ref, info_ref, 1, folded_ref[g, :, :fold], g, edge_ref)
        return carry

    lax.fori_loop(0, groups, open_up, 0, unroll=16)

    def step(i, carry):
        for part, out_ref in enumerate((keep_ref, send_ref)):
            g = order.device((i + part * (groups // 2)) ^ info_ref[0])
            total = 0.0
            for ref, low in ((edge_ref, 0), (folded_ref, fold)):
                partners = jnp.concatenate(partners_of(partners_ref, ref, g, low), axis=0)
                total = total + lax.dot_general(
                    ref[g, :, low:], partners,
                    (((1,), (1,)), ((), ())), preferred_element_type=jnp.float32,
                )
            total = total.astype(jnp.bfloat16)
            out_ref[i, :GROUP, :] = total[:, : 2 * GROUP]
            out_ref[i, GROUP:, :] = pack(total[:, 2 * GROUP :])
        return carry

    lax.fori_loop(0, groups // 2, step, 0, unroll=16)


def gram(order, partners, info, start, folded):
    groups, _, width = folded.shape
    fold = FOLD // order.devices
    half = jax.ShapeDtypeStruct((groups // 2, GROUP + GROUP // 2, 2 * GROUP), jnp.bfloat16)
    return pl.pallas_call(
        functools.partial(gram_kernel, order),
        in_specs=[pl.BlockSpec(memory_space=pltpu.SMEM)] * 2
        + [pl.BlockSpec(memory_space=pltpu.VMEM)] * 2,
        out_specs=[pl.BlockSpec(memory_space=pltpu.VMEM)] * 3,
        out_shape=[jax.ShapeDtypeStruct((groups, GROUP, 2 * fold), jnp.bfloat16), half, half],
        compiler_params=pltpu.CompilerParams(vmem_limit_bytes=VMEM),
        cost_estimate=pl.CostEstimate(
            flops=groups * 2 * GROUP * GROUP * (MEMBERS - 1) * (width + fold),
            bytes_accessed=groups * GROUP * width * 4,
            transcendentals=0,
        ),
        name="gram",
    )(partners, info, start, folded)


def add_kernel(count, pieces, *refs):
    outs = refs[count:]
    each = refs[0].shape[0] // pieces
    for o in range(pieces):
        total = refs[0][o * each : (o + 1) * each].astype(jnp.float32)
        for i in range(1, count):
            total = total + refs[i][o * each : (o + 1) * each].astype(jnp.float32)
        outs[o][...] = total.astype(jnp.bfloat16)


def add(arrays, pieces):
    shape = arrays[0].shape
    out = jax.ShapeDtypeStruct((shape[0] // pieces, *shape[1:]), jnp.bfloat16)
    return pl.pallas_call(
        functools.partial(add_kernel, len(arrays), pieces),
        out_shape=[out] * pieces,
        compiler_params=pltpu.CompilerParams(vmem_limit_bytes=VMEM),
        name="add",
    )(*arrays)


def couple_kernel(own_ref, parts_ref, *refs):
    out_ref = refs[-1]
    weight = 1.0 / (BLOCK * LMAX)
    row = lax.broadcasted_iota(jnp.int32, own_ref.shape, 0)
    unit = jnp.where(row == lax.broadcasted_iota(jnp.int32, own_ref.shape, 1), 1.0, 0.0)
    rows = GROUP + GROUP // 2
    far = parts_ref.shape[0]
    for i in range(far):
        total = parts_ref[i].astype(jnp.float32)
        for apart in range(1, far):
            at = (i ^ apart) * rows
            total = total + refs[apart - 1][at : at + rows].astype(jnp.float32)
        own = unpack(refs[i - 1][far * rows :].astype(jnp.float32)) if i else own_ref[...]
        own = 0.5 * (own * weight - unit)
        total = 0.5 * (total * weight)
        out_ref[i, :, : 2 * GROUP] = total[:GROUP].astype(jnp.bfloat16)
        out_ref[i, :, 2 * GROUP :] = jnp.concatenate(
            [unpack(total[GROUP:]), own], axis=1
        ).astype(jnp.bfloat16)


def couple(own, parts, arrived):
    return pl.pallas_call(
        couple_kernel,
        out_shape=jax.ShapeDtypeStruct((parts.shape[0], GROUP, MEMBERS * GROUP), jnp.bfloat16),
        compiler_params=pltpu.CompilerParams(vmem_limit_bytes=VMEM),
        name="couple",
    )(own, parts, *arrived)


def pack(block):
    return jnp.concatenate([block[: GROUP // 2], block[GROUP // 2 :]], axis=1)


def unpack(block):
    return jnp.concatenate([block[:, :GROUP], block[:, GROUP:]], axis=0)


def add_far_kernel(own_ref, *refs):
    parts_ref, message_ref = refs[-2:]
    rows = parts_ref.shape[1]
    for i in range(parts_ref.shape[0]):
        total = refs[0][i].astype(jnp.float32)
        for ref in refs[1:-2]:
            total = total + ref[i].astype(jnp.float32)
        total = total.astype(jnp.bfloat16)
        parts_ref[i] = total
        message_ref[i * rows : (i + 1) * rows] = total
    message_ref[parts_ref.shape[0] * rows :] = pack(own_ref[...]).astype(jnp.bfloat16)


def add_far(own, arrays):
    far, rows, width = arrays[0].shape
    return pl.pallas_call(
        add_far_kernel,
        out_shape=[
            jax.ShapeDtypeStruct((far, rows, width), jnp.bfloat16),
            jax.ShapeDtypeStruct((far * rows + GROUP // 2, width), jnp.bfloat16),
        ],
        compiler_params=pltpu.CompilerParams(vmem_limit_bytes=VMEM),
        name="add_far",
    )(own, *arrays)


def corrected(partners_ref, coupling, blocks_ref, g, low=0):
    own = blocks_ref[g, :, low:]
    members = jnp.concatenate([*partners_of(partners_ref, blocks_ref, g, low), own], axis=0)
    shifted = jnp.dot(coupling, members, preferred_element_type=jnp.float32)
    return (own.astype(jnp.float32) - shifted).astype(jnp.bfloat16)


def correct_kernel(
    order, low, partners_ref, info_ref, held_ref, other_ref, whole_ref, out_ref
):
    half = held_ref.shape[0]
    for i in range(STEP):
        g = pl.program_id(0) * STEP + i
        apart = order.place(g) ^ info_ref[0]
        near = jnp.broadcast_to(apart, (GROUP, MEMBERS * GROUP)) < half
        coupling = jnp.where(
            near,
            held_ref[apart % half].astype(jnp.float32),
            other_ref[apart % half].astype(jnp.float32),
        ).astype(jnp.bfloat16)
        out_ref[i] = corrected(partners_ref, coupling, whole_ref, g, low)


def correct(order, low, partners, info, held, other, whole):
    groups, _, width = whole.shape
    width = width - low
    return pl.pallas_call(
        functools.partial(correct_kernel, order, low),
        grid=(groups // STEP,),
        in_specs=[pl.BlockSpec(memory_space=pltpu.SMEM)] * 2
        + [pl.BlockSpec(memory_space=pltpu.VMEM)] * 3,
        out_specs=pl.BlockSpec((STEP, GROUP, width), lambda g: (g, 0, 0)),
        out_shape=jax.ShapeDtypeStruct((groups, GROUP, width), jnp.bfloat16),
        compiler_params=pltpu.CompilerParams(vmem_limit_bytes=VMEM),
        cost_estimate=pl.CostEstimate(
            flops=groups * 2 * GROUP * GROUP * MEMBERS * width,
            bytes_accessed=groups * GROUP * width * 4,
            transcendentals=0,
        ),
        name="correct",
    )(partners, info, held, other, whole)


def correct_half_kernel(
    order, count, partners_ref, info_ref, start_ref, held_ref, other_ref, edge_ref, *refs
):
    *folded_refs, mine_ref, theirs_ref, filled_ref = refs
    me, half = info_ref[3], order.devices // 2
    apart = 0
    for ref in folded_refs[:count]:
        for i in range(ref.shape[0]):
            unfold(order, start_ref, info_ref, 2, ref[i], me ^ apart, filled_ref)
            apart += 1
    begin = (me // half ^ 1) * half
    for ref in folded_refs[count:]:
        for i in range(ref.shape[0]):
            unfold(order, start_ref, info_ref, 2, ref[i], begin + i, filled_ref)
        begin += ref.shape[0]
    width = edge_ref.shape[2] // 2
    for apart in range(half):
        g = me ^ apart
        at = order.place(apart)
        coupling = (held_ref if at < half else other_ref)[at % half]
        out_ref = theirs_ref if apart % 2 else mine_ref
        for part, ref in enumerate((edge_ref, filled_ref)):
            result = corrected(partners_ref, coupling, ref, g)
            for side in range(2):
                low = (2 * side + part) * width
                out_ref[apart // 2, :, low : low + width] = result[:, side * width : (side + 1) * width]


def correct_half(order, partners, info, starts, held, other, edge, local, across):
    low = edge.shape[2]
    count = order.devices // 2
    shape = jax.ShapeDtypeStruct((count // 2, GROUP, 2 * low), jnp.bfloat16)
    folded = [*local, *across]
    return pl.pallas_call(
        functools.partial(correct_half_kernel, order, len(local)),
        in_specs=[pl.BlockSpec(memory_space=pltpu.SMEM)] * 2
        + [pl.BlockSpec(memory_space=pltpu.VMEM)] * (4 + len(folded)),
        out_specs=[pl.BlockSpec(memory_space=pltpu.VMEM)] * 2,
        out_shape=[shape] * 2,
        scratch_shapes=[pltpu.VMEM(edge.shape, jnp.bfloat16)],
        compiler_params=pltpu.CompilerParams(vmem_limit_bytes=60 * MIB),
        cost_estimate=pl.CostEstimate(
            flops=count * 4 * GROUP * GROUP * MEMBERS * low,
            bytes_accessed=count * GROUP * low * 12,
            transcendentals=0,
        ),
        name="correct_half",
    )(partners, info, starts, held, other, edge, *folded)


def place_inner_kernel(in_ref, out_ref):
    for s in range(in_ref.shape[0]):
        out_ref[:, s * INNER : (s + 1) * INNER] = in_ref[s]


def place_inner(pieces):
    _, count, width = pieces.shape
    return pl.pallas_call(
        place_inner_kernel,
        grid=(count // ROWS, MID // FOLD),
        in_specs=[pl.BlockSpec((FOLD // INNER, ROWS, width), lambda i, j: (j, i, 0))],
        out_specs=pl.BlockSpec((ROWS, FOLD), lambda i, j: (i, j + 1)),
        out_shape=jax.ShapeDtypeStruct((count, NC), jnp.bfloat16),
        compiler_params=pltpu.CompilerParams(vmem_limit_bytes=VMEM),
        cost_estimate=pl.CostEstimate(flops=0, bytes_accessed=count * MID * 4, transcendentals=0),
        name="place_inner",
    )(pieces)


def place_edge_kernel(base_ref, _, *refs):
    out_ref = refs[-1]
    apart = 0
    for piece_ref in refs[:-1]:
        for i in range(piece_ref.shape[0]):
            slot = base_ref[0] ^ apart
            apart += 1
            for part, s in enumerate((slot, slot ^ (SLOTS // 2))):
                at = pl.multiple_of(s * EDGE, EDGE)
                out_ref[:, pl.ds(at, EDGE)] = piece_ref[i, :, part * EDGE : (part + 1) * EDGE]


def place_edge(base, result, half):
    count = result.shape[0]
    return pl.pallas_call(
        place_edge_kernel,
        grid=(2,),
        in_specs=[pl.BlockSpec(memory_space=pltpu.SMEM), pl.BlockSpec(memory_space=pl.ANY)]
        + [pl.BlockSpec((b.shape[0], count, 2 * EDGE), lambda i: (0, 0, i)) for b in half],
        out_specs=pl.BlockSpec((count, FOLD), lambda i: (0, i * (NC // FOLD - 1))),
        out_shape=jax.ShapeDtypeStruct(result.shape, jnp.bfloat16),
        input_output_aliases={1: 0},
        compiler_params=pltpu.CompilerParams(vmem_limit_bytes=60 * MIB),
        cost_estimate=pl.CostEstimate(flops=0, bytes_accessed=count * FOLD * 8, transcendentals=0),
        name="place_edge",
    )(base, result, *half)


def split_slots(pieces, ratio, bounds):
    if ratio == 1:
        return pieces
    slots, rows, _ = pieces.shape
    parts = []
    for low, high in zip(bounds[:-1], bounds[1:]):
        part = pieces[:, :, low:high].reshape(slots, rows, ratio, (high - low) // ratio)
        parts.append(part.transpose(0, 2, 1, 3).reshape(slots * ratio, rows, -1))
    return jnp.concatenate(parts, axis=2)


def join_slots(pieces, ratio, bounds):
    if ratio == 1:
        return pieces
    count, rows, _ = pieces.shape
    parts = []
    for low, high in zip(bounds[:-1], bounds[1:]):
        part = pieces[:, :, low // ratio : high // ratio]
        part = part.reshape(count // ratio, ratio, rows, (high - low) // ratio)
        parts.append(part.transpose(0, 2, 1, 3).reshape(count // ratio, rows, high - low))
    return jnp.concatenate(parts, axis=2)


def exchange(pieces):
    return lax.all_to_all(pieces, AXES, split_axis=0, concat_axis=0, tiled=True)


def on_device(
    functions, filter_taps, potential, energies, region_start, region_length, partner_groups
):
    order = Order()
    ratio = order.devices // SLOTS
    me = lax.axis_index(AXES)
    half_count = order.devices // 2
    fold = FOLD // order.devices
    info = jnp.stack([order.place(me), me * fold, (me ^ half_count) * fold, me]).astype(jnp.int32)

    pieces = refine(
        filter_taps, functions, potential, energies, region_start, region_length
    )
    own = own_gram(region_start, pieces)
    pieces = split_slots(pieces, ratio, (0, EDGE, EDGE + INNER))
    folded = exchange(pieces)
    starts = order.gather(region_start.reshape(1, 1, GROUP))
    to = me ^ half_count ^ jnp.arange(half_count)
    mine, theirs = [jnp.take(pieces[:, :, :fold], to[i::2], axis=0) for i in range(2)]
    local = order.exchange_half(mine, theirs)

    barrier = lax.optimization_barrier

    def across(block):
        return order.send_device(block, half_count)

    folded, own, *local = barrier((folded, own, *local))
    begin = me // half_count * half_count
    cuts = [cut * ratio for cut in CUTS]
    filled = [
        lax.dynamic_slice(folded, (begin + low, 0, 0), (high - low, GROUP, fold))
        for low, high in zip(cuts[:-1], cuts[1:])
    ]
    folded, *filled = barrier((folded, *filled))
    filled[0] = across(filled[0])
    edge, keep, send = gram(order, partner_groups, info, starts, folded)
    keep, send, filled[0] = barrier((keep, send, filled[0]))
    filled[1] = across(filled[1])
    pieces = add([keep, order.send(send, order.devices // 2)], order.near)
    arrived = [order.send(pieces[i], i * order.far) for i in range(1, order.near)]
    pieces, message = add_far(own, [pieces[0]] + arrived)
    pieces, message, filled[1] = barrier((pieces, message, filled[1]))
    arrived = [order.send(message, i) for i in range(1, order.far)]
    held = couple(own, pieces, arrived)
    held, filled[2] = barrier((held, filled[2]))
    filled[2] = across(filled[2])
    held = jnp.concatenate([held] + [order.send(held, i * order.far) for i in range(1, order.near)], 0)
    held, filled[2], filled[3] = barrier((held, filled[2], filled[3]))
    filled[3] = across(filled[3])
    other = order.send(held, order.devices // 2)

    result = correct(order, fold, partner_groups, info, held, other, folded)
    result, *filled = barrier((result, *filled))
    mine, theirs = correct_half(
        order, partner_groups, info, starts, held, other, edge, local, filled
    )
    result = exchange(result)
    half = order.exchange_half(mine, theirs)
    base = me
    if ratio > 1:
        half = jnp.concatenate(half, 0)[me % half_count ^ jnp.arange(half_count)]
        half = [join_slots(half, ratio, tuple(i * EDGE for i in range(5)))]
        base = me // half_count * (SLOTS // 2)
    result = place_inner(join_slots(result, ratio, (0, INNER)))
    return place_edge(base.astype(jnp.int32).reshape(1), result, half)


def solution(mesh):
    return jax.shard_map(
        on_device,
        mesh=mesh,
        in_specs=(
            P(AXES, None),
            P(),
            P(),
            P(AXES),
            P(AXES),
            P(AXES),
            P(),
        ),
        out_specs=P(AXES, None),
        check_vma=False,
    )
```

```python
import functools

import jax
import jax.numpy as jnp
from jax import lax
from jax.experimental import pallas as pl
from jax.experimental.pallas import tpu as pltpu
from jax.sharding import PartitionSpec as P

SIDE = 32
PLANE = SIDE * SIDE
NC = SIDE * PLANE
BLOCK = 64
NB = NC // BLOCK
GROUP = 64
TAPS = 16
MEMBERS = 4
LMIN = 256
LMAX = 384
FOLD = (NB - LMAX) * BLOCK
MID = NC - 2 * FOLD
SLOTS = 32
ROWS = 16
TILE = 256
EDGE = FOLD // SLOTS
INNER = MID // SLOTS
EDGE_SLOTS = PLANE // EDGE
INNER_SLOTS = PLANE // INNER
STEP = 16
CUTS = (0, 5, 11, 14, 16)
AXES = ("grid", "rep")
MIB = 1024 * 1024
VMEM = 24 * MIB


def to_column(row, size):
    eye = lax.broadcasted_iota(jnp.int32, (size, size), 0) == lax.broadcasted_iota(
        jnp.int32, (size, size), 1
    )
    return jnp.sum(jnp.where(eye, jnp.broadcast_to(row, (size, size)), 0), axis=1, keepdims=True)


def tap_rows(taps, outer, shift, inner_first):
    size = outer if inner_first else TILE // outer
    row = lax.broadcasted_iota(jnp.int32, (size, TILE), 0)
    col = lax.broadcasted_iota(jnp.int32, (size, TILE), 1)
    col = col // (TILE // outer) if inner_first else col % (TILE // outer)
    distance = shift + row - col + TAPS // 2
    total = jnp.zeros(distance.shape, jnp.float32)
    for t in range(TAPS):
        total = jnp.where(distance == t, taps[t], total)
    return total


def spread_outer(rows, outer):
    inner = TILE // outer
    row = lax.broadcasted_iota(jnp.int32, (inner, TILE), 0)
    same = row == lax.broadcasted_iota(jnp.int32, (inner, TILE), 1) % inner
    return jnp.concatenate(
        [jnp.where(same, jnp.broadcast_to(rows[a : a + 1], (inner, TILE)), 0.0) for a in range(outer)], axis=0
    )


def spread_inner(rows, outer):
    inner = TILE // outer
    block = lax.broadcasted_iota(jnp.int32, (inner, TILE), 1) // inner
    return jnp.concatenate([jnp.where(block == a, rows, 0.0) for a in range(outer)], axis=0)


def refine_kernel(
    taps_ref, functions_ref, potential_ref, energies_ref, start_ref, length_ref, out_ref,
    plane_ref, line_ref, slabs_ref, rows_ref, ends_ref,
):
    count = energies_ref.shape[1]

    @pl.when(pl.program_id(0) == 0)
    def _():
        taps = taps_ref[...].astype(jnp.float32)
        taps = [taps[:, t : t + 1] for t in range(TAPS)]
        outer = TILE // SIDE
        lines = []
        for j in range(3):
            part = spread_outer(tap_rows(taps, outer, (j - 1) * outer, True), outer)
            if j == 1:
                part = part + spread_inner(tap_rows(taps, outer, 0, False), outer)
            plane_ref[j * TILE : (j + 1) * TILE, :] = part.astype(jnp.bfloat16)
            flipped = [taps[TAPS - 1 - t] for t in range(TAPS)]
            rows = tap_rows(flipped, TILE // ROWS, (1 - j) * (TILE // ROWS) - 1, True)
            lines.append(spread_outer(rows, TILE // ROWS).astype(jnp.bfloat16))
        for h in range(SIDE * ROWS // TILE):
            for i in range(SIDE * ROWS // TILE):
                line_ref[h * TILE : (h + 1) * TILE, i * TILE : (i + 1) * TILE] = lines[i - h + 1]
        wide = (count, 2 * BLOCK)
        energy = to_column(energies_ref[...], count)
        first = to_column(start_ref[...], count)
        rows_ref[0] = jnp.broadcast_to(energy, wide)
        rows_ref[1] = jnp.broadcast_to(0.3 / (1.0 - energy), wide)
        ends_ref[0] = jnp.broadcast_to(first, wide)
        ends_ref[1] = jnp.broadcast_to(first + to_column(length_ref[...], count), wide)

    for x in range(SIDE):
        slabs_ref[x * ROWS : (x + 1) * ROWS, :] = functions_ref[:, x * PLANE : (x + 1) * PLANE]
    here = pl.ds(pl.multiple_of(pl.program_id(0) * ROWS, ROWS), ROWS)

    def widen(value):
        return jnp.concatenate([value] * (TILE // (2 * BLOCK)), axis=1)

    energy, scale = widen(rows_ref[0, here, :]), widen(rows_ref[1, here, :])
    lane_block = lax.broadcasted_iota(jnp.int32, (ROWS, TILE), 1) // BLOCK
    first = widen(ends_ref[0, here, :]) - lane_block
    last = widen(ends_ref[1, here, :]) - lane_block
    blocks = PLANE // TILE
    near, far = FOLD // PLANE, (NC - FOLD) // PLANE
    for j in range(blocks):
        cols = slice(j * TILE, (j + 1) * TILE)
        low, high = max(0, j - 1), min(blocks, j + 2)
        totals = []
        for h in range(SIDE * ROWS // TILE):
            rows = slice(h * TILE, (h + 1) * TILE)
            total = jnp.dot(
                slabs_ref[rows, low * TILE : high * TILE],
                plane_ref[(low - j + 1) * TILE : (high - j + 1) * TILE, :],
                preferred_element_type=jnp.float32,
            )
            total = total + jnp.dot(
                line_ref[rows, :], slabs_ref[:, cols], preferred_element_type=jnp.float32
            )
            totals += [total[i * ROWS : (i + 1) * ROWS] for i in range(TILE // ROWS)]

        def gradient_parts(x):
            rows = slice(x * ROWS, (x + 1) * ROWS)
            place = potential_ref[0:1, x * PLANE + j * TILE : x * PLANE + (j + 1) * TILE]
            place = jnp.broadcast_to(place, (ROWS, TILE))
            return totals[x], place, slabs_ref[rows, cols].astype(jnp.float32)

        for x in range(far):
            block = (x * PLANE + j * TILE) // BLOCK
            parts = gradient_parts(x)
            inside = None
            if x < near:
                starts = first <= block
                inside = starts | (last > block + (NC - FOLD) // BLOCK)
                parts = [
                    jnp.where(starts, one, other)
                    for one, other in zip(parts, gradient_parts(x + far))
                ]
                column = x * PLANE + j * TILE
                slot, place = column // EDGE, column % EDGE
            else:
                if block + TILE // BLOCK > LMIN:
                    inside = last > block
                column = (x - near) * PLANE + j * TILE
                slot, place = column // INNER, EDGE + column % INNER
            kinetic, potential, value = parts
            value = value - scale * (kinetic + (potential - energy) * value)
            if inside is not None:
                value = jnp.where(inside, value, 0.0)
            out_ref[slot, :, place : place + TILE] = value.astype(jnp.bfloat16)


def refine(taps, functions, potential, energies, start, length):
    count = functions.shape[0]
    steps = count // ROWS
    width = EDGE + INNER
    row = pl.BlockSpec((1, count), lambda i: (0, 0))
    return pl.pallas_call(
        refine_kernel,
        grid=(steps,),
        in_specs=[
            pl.BlockSpec((1, TAPS), lambda i: (0, 0)),
            pl.BlockSpec((ROWS, NC), lambda i: (i, 0)),
            pl.BlockSpec((1, NC), lambda i: (0, 0)),
            row,
            row,
            row,
        ],
        out_specs=pl.BlockSpec((SLOTS, ROWS, width), lambda i: (0, i, 0)),
        out_shape=jax.ShapeDtypeStruct((SLOTS, count, width), jnp.bfloat16),
        scratch_shapes=[
            pltpu.VMEM((3 * TILE, TILE), jnp.bfloat16),
            pltpu.VMEM((SIDE * ROWS, SIDE * ROWS), jnp.bfloat16),
            pltpu.VMEM((SIDE * ROWS, PLANE), jnp.bfloat16),
            pltpu.VMEM((2, count, 2 * BLOCK), jnp.float32),
            pltpu.VMEM((2, count, 2 * BLOCK), jnp.int32),
        ],
        compiler_params=pltpu.CompilerParams(vmem_limit_bytes=60 * MIB),
        cost_estimate=pl.CostEstimate(
            flops=steps * 36 * 2 * TILE**3, bytes_accessed=count * NC * 3, transcendentals=0
        ),
        name="refine",
    )(
        taps.reshape(1, TAPS),
        functions,
        potential.reshape(1, NC),
        energies.reshape(1, count),
        start.reshape(1, count),
        length.reshape(1, count),
    )


class Order:
    def __init__(self):
        self.grid, self.rep = lax.axis_size("grid"), lax.axis_size("rep")
        self.devices = self.grid * self.rep
        self.far, self.near = self.grid // 2, self.rep

    def place(self, device):
        grid, rep = device // self.rep, device % self.rep
        return ((rep % 2 * (self.rep // 2) + rep // 2) * 2 + grid % 2) * self.far + grid // 2

    def device(self, place):
        high, low = place // self.far, place % self.far
        rep = high // 2 % (self.rep // 2) * 2 + high // 2 // (self.rep // 2)
        return (low * 2 + high % 2) * self.rep + rep

    def send(self, block, apart):
        pairs = [(i, self.device(self.place(i) ^ apart)) for i in range(self.devices)]
        return lax.ppermute(block, AXES, pairs)

    def send_device(self, block, apart):
        return self.send(block, self.place(apart))

    def exchange_half(self, mine, theirs):
        theirs = self.send_device(theirs, 1)
        pairs = [jnp.stack([mine[i], theirs[i]]) for i in range(mine.shape[0])]
        return pairs[:1] + [self.send_device(pairs[i], 2 * i) for i in range(1, len(pairs))]

    def gather(self, blocks):
        blocks = jnp.stack([blocks, self.send(blocks, self.devices // 2)])
        sent = [self.send(blocks, i * self.far) for i in range(1, self.near)]
        blocks = jnp.stack([blocks] + sent, axis=1)
        sent = [self.send(blocks, i) for i in range(1, self.far)]
        blocks = jnp.stack([blocks] + sent, axis=2)
        return blocks.reshape(self.devices, *blocks.shape[4:])


def partners_of(partners_ref, blocks_ref, g, low=0):
    return [blocks_ref[partners_ref[g, k], :, low:] for k in range(MEMBERS - 1)]


def open_fold(folded, first, column):
    column = column + lax.broadcasted_iota(jnp.int32, folded.shape, 1)
    near = jnp.broadcast_to(first, folded.shape) <= column // BLOCK
    both = folded.astype(jnp.float32)
    return [jnp.where(near, both, 0.0).astype(jnp.bfloat16), jnp.where(near, 0.0, both).astype(jnp.bfloat16)]


def own_gram_kernel(start_ref, pieces_ref, out_ref, start_column_ref):
    start_column_ref[...] = jnp.broadcast_to(to_column(start_ref[...], GROUP), start_column_ref.shape)

    def step(s, total):
        folded = pieces_ref[s, :, :EDGE]
        near, far = open_fold(folded, start_column_ref[:, :1], s * EDGE)
        whole = jnp.concatenate([near, far, pieces_ref[s, :, EDGE:]], axis=1)
        return total + lax.dot_general(
            whole, whole, (((1,), (1,)), ((), ())), preferred_element_type=jnp.float32
        )

    zero = jnp.zeros(out_ref.shape, jnp.float32)
    out_ref[...] = lax.fori_loop(0, pieces_ref.shape[0], step, zero, unroll=4)


def own_gram(start, pieces):
    return pl.pallas_call(
        own_gram_kernel,
        out_shape=jax.ShapeDtypeStruct((GROUP, GROUP), jnp.float32),
        scratch_shapes=[pltpu.VMEM((GROUP, 2 * BLOCK), jnp.int32)],
        compiler_params=pltpu.CompilerParams(vmem_limit_bytes=16 * MIB),
        cost_estimate=pl.CostEstimate(
            flops=2 * GROUP * GROUP * NC, bytes_accessed=GROUP * NC * 2, transcendentals=0
        ),
        name="own_gram",
    )(start.reshape(1, GROUP), pieces)


def unfold(order, start_ref, info_ref, which, folded, g, edge_ref):
    width = folded.shape[1]
    first = to_column(start_ref[order.place(g) ^ info_ref[0]], GROUP)
    near, far = open_fold(folded, first, info_ref[which])
    edge_ref[g, :, :width] = near
    edge_ref[g, :, width:] = far


def gram_kernel(
    order, partners_ref, info_ref, start_ref, folded_ref, edge_ref, keep_ref, send_ref
):
    groups = folded_ref.shape[0]
    fold = edge_ref.shape[2] // 2

    def open_up(g, carry):
        unfold(order, start_ref, info_ref, 1, folded_ref[g, :, :fold], g, edge_ref)
        return carry

    lax.fori_loop(0, groups, open_up, 0, unroll=16)

    def step(i, carry):
        for part, out_ref in enumerate((keep_ref, send_ref)):
            g = order.device((i + part * (groups // 2)) ^ info_ref[0])
            total = 0.0
            for ref, low in ((edge_ref, 0), (folded_ref, fold)):
                partners = jnp.concatenate(partners_of(partners_ref, ref, g, low), axis=0)
                total = total + lax.dot_general(
                    ref[g, :, low:], partners,
                    (((1,), (1,)), ((), ())), preferred_element_type=jnp.float32,
                )
            total = total.astype(jnp.bfloat16)
            out_ref[i, :GROUP, :] = total[:, : 2 * GROUP]
            out_ref[i, GROUP:, :] = pack(total[:, 2 * GROUP :])
        return carry

    lax.fori_loop(0, groups // 2, step, 0, unroll=16)


def gram(order, partners, info, start, folded):
    groups, _, width = folded.shape
    fold = FOLD // order.devices
    half = jax.ShapeDtypeStruct((groups // 2, GROUP + GROUP // 2, 2 * GROUP), jnp.bfloat16)
    return pl.pallas_call(
        functools.partial(gram_kernel, order),
        in_specs=[pl.BlockSpec(memory_space=pltpu.SMEM)] * 2
        + [pl.BlockSpec(memory_space=pltpu.VMEM)] * 2,
        out_specs=[pl.BlockSpec(memory_space=pltpu.VMEM)] * 3,
        out_shape=[jax.ShapeDtypeStruct((groups, GROUP, 2 * fold), jnp.bfloat16), half, half],
        compiler_params=pltpu.CompilerParams(vmem_limit_bytes=VMEM),
        cost_estimate=pl.CostEstimate(
            flops=groups * 2 * GROUP * GROUP * (MEMBERS - 1) * (width + fold),
            bytes_accessed=groups * GROUP * width * 4,
            transcendentals=0,
        ),
        name="gram",
    )(partners, info, start, folded)


def add_kernel(count, pieces, *refs):
    outs = refs[count:]
    each = refs[0].shape[0] // pieces
    for o in range(pieces):
        total = refs[0][o * each : (o + 1) * each].astype(jnp.float32)
        for i in range(1, count):
            total = total + refs[i][o * each : (o + 1) * each].astype(jnp.float32)
        outs[o][...] = total.astype(jnp.bfloat16)


def add(arrays, pieces):
    shape = arrays[0].shape
    out = jax.ShapeDtypeStruct((shape[0] // pieces, *shape[1:]), jnp.bfloat16)
    return pl.pallas_call(
        functools.partial(add_kernel, len(arrays), pieces),
        out_shape=[out] * pieces,
        compiler_params=pltpu.CompilerParams(vmem_limit_bytes=VMEM),
        name="add",
    )(*arrays)


def couple_kernel(own_ref, parts_ref, *refs):
    out_ref = refs[-1]
    weight = 1.0 / (BLOCK * LMAX)
    row = lax.broadcasted_iota(jnp.int32, own_ref.shape, 0)
    unit = jnp.where(row == lax.broadcasted_iota(jnp.int32, own_ref.shape, 1), 1.0, 0.0)
    rows = GROUP + GROUP // 2
    far = parts_ref.shape[0]
    for i in range(far):
        total = parts_ref[i].astype(jnp.float32)
        for apart in range(1, far):
            at = (i ^ apart) * rows
            total = total + refs[apart - 1][at : at + rows].astype(jnp.float32)
        own = unpack(refs[i - 1][far * rows :].astype(jnp.float32)) if i else own_ref[...]
        own = 0.5 * (own * weight - unit)
        total = 0.5 * (total * weight)
        out_ref[i, :, : 2 * GROUP] = total[:GROUP].astype(jnp.bfloat16)
        out_ref[i, :, 2 * GROUP :] = jnp.concatenate(
            [unpack(total[GROUP:]), own], axis=1
        ).astype(jnp.bfloat16)


def couple(own, parts, arrived):
    return pl.pallas_call(
        couple_kernel,
        out_shape=jax.ShapeDtypeStruct((parts.shape[0], GROUP, MEMBERS * GROUP), jnp.bfloat16),
        compiler_params=pltpu.CompilerParams(vmem_limit_bytes=VMEM),
        name="couple",
    )(own, parts, *arrived)


def pack(block):
    return jnp.concatenate([block[: GROUP // 2], block[GROUP // 2 :]], axis=1)


def unpack(block):
    return jnp.concatenate([block[:, :GROUP], block[:, GROUP:]], axis=0)


def add_far_kernel(own_ref, *refs):
    parts_ref, message_ref = refs[-2:]
    rows = parts_ref.shape[1]
    for i in range(parts_ref.shape[0]):
        total = refs[0][i].astype(jnp.float32)
        for ref in refs[1:-2]:
            total = total + ref[i].astype(jnp.float32)
        total = total.astype(jnp.bfloat16)
        parts_ref[i] = total
        message_ref[i * rows : (i + 1) * rows] = total
    message_ref[parts_ref.shape[0] * rows :] = pack(own_ref[...]).astype(jnp.bfloat16)


def add_far(own, arrays):
    far, rows, width = arrays[0].shape
    return pl.pallas_call(
        add_far_kernel,
        out_shape=[
            jax.ShapeDtypeStruct((far, rows, width), jnp.bfloat16),
            jax.ShapeDtypeStruct((far * rows + GROUP // 2, width), jnp.bfloat16),
        ],
        compiler_params=pltpu.CompilerParams(vmem_limit_bytes=VMEM),
        name="add_far",
    )(own, *arrays)


def corrected(partners_ref, coupling, blocks_ref, g, low=0):
    own = blocks_ref[g, :, low:]
    members = jnp.concatenate([*partners_of(partners_ref, blocks_ref, g, low), own], axis=0)
    shifted = jnp.dot(coupling, members, preferred_element_type=jnp.float32)
    return (own.astype(jnp.float32) - shifted).astype(jnp.bfloat16)


def correct_kernel(
    order, low, partners_ref, info_ref, held_ref, other_ref, whole_ref, out_ref
):
    half = held_ref.shape[0]
    for i in range(STEP):
        g = pl.program_id(0) * STEP + i
        apart = order.place(g) ^ info_ref[0]
        near = jnp.broadcast_to(apart, (GROUP, MEMBERS * GROUP)) < half
        coupling = jnp.where(
            near,
            held_ref[apart % half].astype(jnp.float32),
            other_ref[apart % half].astype(jnp.float32),
        ).astype(jnp.bfloat16)
        out_ref[i] = corrected(partners_ref, coupling, whole_ref, g, low)


def correct(order, low, partners, info, held, other, whole):
    groups, _, width = whole.shape
    width = width - low
    return pl.pallas_call(
        functools.partial(correct_kernel, order, low),
        grid=(groups // STEP,),
        in_specs=[pl.BlockSpec(memory_space=pltpu.SMEM)] * 2
        + [pl.BlockSpec(memory_space=pltpu.VMEM)] * 3,
        out_specs=pl.BlockSpec((STEP, GROUP, width), lambda g: (g, 0, 0)),
        out_shape=jax.ShapeDtypeStruct((groups, GROUP, width), jnp.bfloat16),
        compiler_params=pltpu.CompilerParams(vmem_limit_bytes=VMEM),
        cost_estimate=pl.CostEstimate(
            flops=groups * 2 * GROUP * GROUP * MEMBERS * width,
            bytes_accessed=groups * GROUP * width * 4,
            transcendentals=0,
        ),
        name="correct",
    )(partners, info, held, other, whole)


def correct_half_kernel(
    order, count, partners_ref, info_ref, start_ref, held_ref, other_ref, edge_ref, *refs
):
    *folded_refs, mine_ref, theirs_ref, filled_ref = refs
    me, half = info_ref[3], order.devices // 2
    apart = 0
    for ref in folded_refs[:count]:
        for i in range(ref.shape[0]):
            unfold(order, start_ref, info_ref, 2, ref[i], me ^ apart, filled_ref)
            apart += 1
    begin = (me // half ^ 1) * half
    for ref in folded_refs[count:]:
        for i in range(ref.shape[0]):
            unfold(order, start_ref, info_ref, 2, ref[i], begin + i, filled_ref)
        begin += ref.shape[0]
    width = edge_ref.shape[2] // 2
    for apart in range(half):
        g = me ^ apart
        at = order.place(apart)
        coupling = (held_ref if at < half else other_ref)[at % half]
        out_ref = theirs_ref if apart % 2 else mine_ref
        for part, ref in enumerate((edge_ref, filled_ref)):
            result = corrected(partners_ref, coupling, ref, g)
            for side in range(2):
                low = (2 * side + part) * width
                out_ref[apart // 2, :, low : low + width] = result[:, side * width : (side + 1) * width]


def correct_half(order, partners, info, starts, held, other, edge, local, across):
    low = edge.shape[2]
    count = order.devices // 2
    shape = jax.ShapeDtypeStruct((count // 2, GROUP, 2 * low), jnp.bfloat16)
    folded = [*local, *across]
    return pl.pallas_call(
        functools.partial(correct_half_kernel, order, len(local)),
        in_specs=[pl.BlockSpec(memory_space=pltpu.SMEM)] * 2
        + [pl.BlockSpec(memory_space=pltpu.VMEM)] * (4 + len(folded)),
        out_specs=[pl.BlockSpec(memory_space=pltpu.VMEM)] * 2,
        out_shape=[shape] * 2,
        scratch_shapes=[pltpu.VMEM(edge.shape, jnp.bfloat16)],
        compiler_params=pltpu.CompilerParams(vmem_limit_bytes=60 * MIB),
        cost_estimate=pl.CostEstimate(
            flops=count * 4 * GROUP * GROUP * MEMBERS * low,
            bytes_accessed=count * GROUP * low * 12,
            transcendentals=0,
        ),
        name="correct_half",
    )(partners, info, starts, held, other, edge, *folded)


def place_inner_kernel(in_ref, out_ref):
    for s in range(in_ref.shape[0]):
        out_ref[:, s * INNER : (s + 1) * INNER] = in_ref[s]


def place_inner(pieces):
    _, count, width = pieces.shape
    return pl.pallas_call(
        place_inner_kernel,
        grid=(count // ROWS, MID // FOLD),
        in_specs=[pl.BlockSpec((FOLD // INNER, ROWS, width), lambda i, j: (j, i, 0))],
        out_specs=pl.BlockSpec((ROWS, FOLD), lambda i, j: (i, j + 1)),
        out_shape=jax.ShapeDtypeStruct((count, NC), jnp.bfloat16),
        compiler_params=pltpu.CompilerParams(vmem_limit_bytes=VMEM),
        cost_estimate=pl.CostEstimate(flops=0, bytes_accessed=count * MID * 4, transcendentals=0),
        name="place_inner",
    )(pieces)


def place_edge_kernel(base_ref, _, *refs):
    out_ref = refs[-1]
    apart = 0
    for piece_ref in refs[:-1]:
        for i in range(piece_ref.shape[0]):
            slot = base_ref[0] ^ apart
            apart += 1
            for part, s in enumerate((slot, slot ^ (SLOTS // 2))):
                at = pl.multiple_of(s * EDGE, EDGE)
                out_ref[:, pl.ds(at, EDGE)] = piece_ref[i, :, part * EDGE : (part + 1) * EDGE]


def place_edge(base, result, half):
    count = result.shape[0]
    return pl.pallas_call(
        place_edge_kernel,
        grid=(2,),
        in_specs=[pl.BlockSpec(memory_space=pltpu.SMEM), pl.BlockSpec(memory_space=pl.ANY)]
        + [pl.BlockSpec((b.shape[0], count, 2 * EDGE), lambda i: (0, 0, i)) for b in half],
        out_specs=pl.BlockSpec((count, FOLD), lambda i: (0, i * (NC // FOLD - 1))),
        out_shape=jax.ShapeDtypeStruct(result.shape, jnp.bfloat16),
        input_output_aliases={1: 0},
        compiler_params=pltpu.CompilerParams(vmem_limit_bytes=16 * MIB),
        cost_estimate=pl.CostEstimate(flops=0, bytes_accessed=count * FOLD * 8, transcendentals=0),
        name="place_edge",
    )(base, result, *half)


def split_slots(pieces, ratio, bounds):
    if ratio == 1:
        return pieces
    slots, rows, _ = pieces.shape
    parts = []
    for low, high in zip(bounds[:-1], bounds[1:]):
        part = pieces[:, :, low:high].reshape(slots, rows, ratio, (high - low) // ratio)
        parts.append(part.transpose(0, 2, 1, 3).reshape(slots * ratio, rows, -1))
    return jnp.concatenate(parts, axis=2)


def join_slots(pieces, ratio, bounds):
    if ratio == 1:
        return pieces
    count, rows, _ = pieces.shape
    parts = []
    for low, high in zip(bounds[:-1], bounds[1:]):
        part = pieces[:, :, low // ratio : high // ratio]
        part = part.reshape(count // ratio, ratio, rows, (high - low) // ratio)
        parts.append(part.transpose(0, 2, 1, 3).reshape(count // ratio, rows, high - low))
    return jnp.concatenate(parts, axis=2)


def exchange(pieces):
    return lax.all_to_all(pieces, AXES, split_axis=0, concat_axis=0, tiled=True)


def on_device(
    functions, filter_taps, potential, energies, region_start, region_length, partner_groups
):
    order = Order()
    ratio = order.devices // SLOTS
    me = lax.axis_index(AXES)
    half_count = order.devices // 2
    fold = FOLD // order.devices
    info = jnp.stack([order.place(me), me * fold, (me ^ half_count) * fold, me]).astype(jnp.int32)

    pieces = refine(
        filter_taps, functions, potential, energies, region_start, region_length
    )
    own = own_gram(region_start, pieces)
    pieces = split_slots(pieces, ratio, (0, EDGE, EDGE + INNER))
    folded = exchange(pieces)
    starts = order.gather(region_start.reshape(1, 1, GROUP))
    to = me ^ half_count ^ jnp.arange(half_count)
    mine, theirs = [jnp.take(pieces[:, :, :fold], to[i::2], axis=0) for i in range(2)]
    local = order.exchange_half(mine, theirs)

    barrier = lax.optimization_barrier

    def across(block):
        return order.send_device(block, half_count)

    folded, own, *local = barrier((folded, own, *local))
    begin = me // half_count * half_count
    cuts = [cut * ratio for cut in CUTS]
    filled = [
        lax.dynamic_slice(folded, (begin + low, 0, 0), (high - low, GROUP, fold))
        for low, high in zip(cuts[:-1], cuts[1:])
    ]
    folded, *filled = barrier((folded, *filled))
    filled[0] = across(filled[0])
    edge, keep, send = gram(order, partner_groups, info, starts, folded)
    keep, send, filled[0] = barrier((keep, send, filled[0]))
    filled[1] = across(filled[1])
    pieces = add([keep, order.send(send, order.devices // 2)], order.near)
    arrived = [order.send(pieces[i], i * order.far) for i in range(1, order.near)]
    pieces, message = add_far(own, [pieces[0]] + arrived)
    pieces, message, filled[1] = barrier((pieces, message, filled[1]))
    arrived = [order.send(message, i) for i in range(1, order.far)]
    held = couple(own, pieces, arrived)
    held, filled[2] = barrier((held, filled[2]))
    filled[2] = across(filled[2])
    held = jnp.concatenate([held] + [order.send(held, i * order.far) for i in range(1, order.near)], 0)
    held, filled[2], filled[3] = barrier((held, filled[2], filled[3]))
    filled[3] = across(filled[3])
    other = order.send(held, order.devices // 2)

    result = correct(order, fold, partner_groups, info, held, other, folded)
    result, *filled = barrier((result, *filled))
    mine, theirs = correct_half(
        order, partner_groups, info, starts, held, other, edge, local, filled
    )
    result = exchange(result)
    half = order.exchange_half(mine, theirs)
    base = me
    if ratio > 1:
        half = jnp.concatenate(half, 0)[me % half_count ^ jnp.arange(half_count)]
        half = [join_slots(half, ratio, tuple(i * EDGE for i in range(5)))]
        base = me // half_count * (SLOTS // 2)
    result = place_inner(join_slots(result, ratio, (0, INNER)))
    return place_edge(base.astype(jnp.int32).reshape(1), result, half)


def solution(mesh):
    return jax.shard_map(
        on_device,
        mesh=mesh,
        in_specs=(
            P(AXES, None),
            P(),
            P(),
            P(AXES),
            P(AXES),
            P(AXES),
            P(),
        ),
        out_specs=P(AXES, None),
        check_vma=False,
    )
```
